128 devices in a mesh: row: 8 (over x, core), col: 8 (over z_lo, y), batch: 2 (over z_hi).
Axes of the slice: x: 4, y: 4, z: 4 (z_hi: 2, z_lo: 2; z = z_hi * 2 + z_lo), core: 2. Of those that a mesh axis runs over, the one named last changes fastest.
Arguments:
- syndromes: int32 [512, 1024], P(('batch', 'row'), 'col'), parts along dimension 0, may hold values from 0 to 65535
- embedding: bfloat16 [64, 16], replicated, may hold values from -1.5 to 1.5
- kernel_first: bfloat16 [3, 3, 64, 64], replicated, may hold values from -0.25 to 0.25
- kernel_second: bfloat16 [3, 3, 128, 64], replicated, may hold values from -0.25 to 0.25
- kernel_bottom: bfloat16 [3, 3, 256, 128], replicated, may hold values from -0.1875 to 0.1875
- kernel_return: bfloat16 [3, 3, 128, 256], replicated, may hold values from -0.125 to 0.125
- kernel_final: bfloat16 [3, 3, 64, 128], replicated, may hold values from -0.1875 to 0.1875
- readout: bfloat16 [2, 64], replicated, may hold values from -0.75 to 0.75
- cotangent: bfloat16 [2, 512, 1024], P(None, ('batch', 'row'), 'col'), parts along dimension 1, may hold values from -6 to 6
Outputs:
- logits: float32 [2, 512, 1024], P(None, ('batch', 'row'), 'col'), parts along dimension 1
- feature_grad: bfloat16 [64, 512, 1024], P(None, ('batch', 'row'), 'col'), parts along dimension 1
- embedding_grad: float32 [128, 16], P('batch'), parts along dimension 0
- first_grad: float32 [6, 3, 64, 64], P('batch'), parts along dimension 0
- second_grad: float32 [6, 3, 128, 64], P('batch'), parts along dimension 0
- bottom_grad: float32 [6, 3, 256, 128], P('batch'), parts along dimension 0
- return_grad: float32 [6, 3, 128, 256], P('batch'), parts along dimension 0
- final_grad: float32 [6, 3, 64, 128], P('batch'), parts along dimension 0
- readout_grad: float32 [4, 64], P('batch'), parts along dimension 0
The draws below stay inside these ranges and needn't reach their ends.
There are 2 independent parts, one for each index of `batch`. The reference program is written for one: setup_inputs(seed, part) draws one part's arguments, and reference() takes and returns one part's arrays. A program takes and returns all parts, laid end to end along the dimension named above; an argument that names none is the same for every part. Nothing has to cross between parts.
All inputs are finite; a program needn't handle non-finite values.
Results may differ from the reference program's by a relative error of at most 0.038.
Values may be sent and summed in bfloat16 or wider, within the bound.
A program may use at most 64 MiB of HBM per device.

```python
import jax
import jax.numpy as jnp
from jax import lax

BITS = 16
WIDTH_FINE = 64
WIDTH_MID = 128
WIDTH_BOTTOM = 256
OUTPUTS = 2
HEIGHT = 256
BREADTH = 1024


def set_ends(entries, key, smallest, largest):
    longest = entries.shape.index(max(entries.shape))
    spots = []
    for shift in (0, 1):
        where = [jax.random.randint(jax.random.fold_in(key, axis), (), 0, length) for axis, length in enumerate(entries.shape)]
        where[longest] = (where[longest] + shift) % entries.shape[longest]
        spots.append(tuple(where))
    return entries.at[spots[0]].set(smallest).at[spots[1]].set(largest)


def levels(rng, dims, shards, least, top_value):
    def one(position, blocks):
        draws = jax.random.uniform(jax.random.fold_in(jax.random.fold_in(rng, 6), position), (blocks,), jnp.float32, least / len(shards), top_value / len(shards))
        return jnp.repeat(jnp.exp(draws), dims[position] // blocks).reshape((-1,) + (1,) * (len(dims) - position - 1))

    level = one(*shards[0])
    for cut in shards[1:]:
        level = level * one(*cut)
    return level


def normal_values(own_key, extent, spread, limit, shards=(), kind=jnp.bfloat16):
    result = spread * jax.random.normal(own_key, extent, jnp.float32)
    if shards:
        result = result * levels(own_key, extent, shards, -0.22, 0.18)
    return jnp.clip(result, -limit, limit).astype(kind)


def setup_inputs(seed: int = 0, part: int = 0) -> dict:
    key_of = jax.random.split(jax.random.key(seed), 10)
    part_keys = jax.random.split(jax.random.fold_in(key_of[9], part), 10)
    syndromes = set_ends(jax.random.randint(part_keys[0], (HEIGHT, BREADTH), 0, 65536), jax.random.fold_in(part_keys[0], 1), 0, 65535).astype(jnp.int32)
    embedding = normal_values(key_of[1], (WIDTH_FINE, BITS), BITS ** -0.5, 1.5)
    kernel_first = normal_values(key_of[2], (3, 3, WIDTH_FINE, WIDTH_FINE), (9 * WIDTH_FINE) ** -0.5, 0.25)
    kernel_second = normal_values(key_of[3], (3, 3, WIDTH_MID, WIDTH_FINE), (9 * WIDTH_FINE) ** -0.5, 0.25)
    kernel_bottom = normal_values(key_of[4], (3, 3, WIDTH_BOTTOM, WIDTH_MID), (9 * WIDTH_MID) ** -0.5, 0.1875)
    kernel_return = normal_values(key_of[5], (3, 3, WIDTH_MID, WIDTH_BOTTOM), (9 * WIDTH_BOTTOM) ** -0.5, 0.125)
    kernel_final = normal_values(key_of[6], (3, 3, WIDTH_FINE, WIDTH_MID), (9 * WIDTH_MID) ** -0.5, 0.1875)
    readout = normal_values(key_of[7], (OUTPUTS, WIDTH_FINE), WIDTH_FINE ** -0.5, 0.75)
    cotangent = normal_values(part_keys[8], (OUTPUTS, HEIGHT, BREADTH), 1.0, 6.0, ((1, 8), (2, 8)))
    return {"syndromes": syndromes, "embedding": embedding, "kernel_first": kernel_first, "kernel_second": kernel_second, "kernel_bottom": kernel_bottom, "kernel_return": kernel_return, "kernel_final": kernel_final, "readout": readout, "cotangent": cotangent}


def unpack(syndromes, count):
    shifts = jnp.arange(count, dtype=jnp.int32)
    return (syndromes[None, :, :] >> shifts[:, None, None] & 1).astype(jnp.bfloat16)

def flatten(values):
    return values.reshape(values.shape[0], values.shape[1] * values.shape[2])

def pointwise(weight, values):
    product = jnp.dot(weight, flatten(values), preferred_element_type=jnp.float32)
    return product.reshape(weight.shape[0], values.shape[1], values.shape[2])

def convolve(padded, kernel):
    height, breadth = (padded.shape[1] - 2, padded.shape[2] - 2)
    summed = jnp.zeros((kernel.shape[2], height * breadth), jnp.float32)
    for row_tap in range(3):
        for col_tap in range(3):
            window = flatten(padded[:, row_tap:row_tap + height, col_tap:col_tap + breadth])
            summed = summed + jnp.dot(kernel[row_tap, col_tap], window, preferred_element_type=jnp.float32)
    return summed.reshape(kernel.shape[2], height, breadth)

def convolve_back(padded, kernel):
    height, breadth = (padded.shape[1] - 2, padded.shape[2] - 2)
    summed = jnp.zeros((kernel.shape[3], height * breadth), jnp.float32)
    for row_tap in range(3):
        for col_tap in range(3):
            window = flatten(padded[:, 2 - row_tap:2 - row_tap + height, 2 - col_tap:2 - col_tap + breadth])
            summed = summed + jnp.dot(kernel[row_tap, col_tap].T, window, preferred_element_type=jnp.float32)
    return summed.reshape(kernel.shape[3], height, breadth)

def kernel_grad(padded, cotan):
    height, breadth = (cotan.shape[1], cotan.shape[2])
    flattened = flatten(cotan)
    grid = []
    for row_tap in range(3):
        line = []
        for col_tap in range(3):
            window = flatten(padded[:, row_tap:row_tap + height, col_tap:col_tap + breadth])
            line.append(lax.dot_general(flattened, window, (((1,), (1,)), ((), ())), preferred_element_type=jnp.float32))
        grid.append(jnp.stack(line))
    return jnp.stack(grid)

def activate(preact):
    stored = lax.optimization_barrier(preact.astype(jnp.bfloat16))
    widened = stored.astype(jnp.float32)
    return (stored, (widened * jax.nn.sigmoid(widened)).astype(jnp.bfloat16))

def descend(incoming, stored):
    widened = stored.astype(jnp.float32)
    logistic = jax.nn.sigmoid(widened)
    return (incoming * logistic * (1.0 + widened * (1.0 - logistic))).astype(jnp.bfloat16)

def pool(values):
    channels, height, breadth = values.shape
    blocks = values.astype(jnp.float32).reshape(channels, height // 2, 2, breadth // 2, 2)
    return (blocks.sum(axis=(2, 4)) * 0.25).astype(jnp.bfloat16)

def enlarge(values):
    return jnp.repeat(jnp.repeat(values, 2, axis=1), 2, axis=2)

def block_sum(values):
    channels, height, breadth = values.shape
    return values.reshape(channels, height // 2, 2, breadth // 2, 2).sum(axis=(2, 4))

def pad_edges(values):
    return jnp.pad(values, ((0, 0), (1, 1), (1, 1)))

def reference(syndromes, embedding, kernel_first, kernel_second, kernel_bottom, kernel_return, kernel_final, readout, cotangent):
    bits = unpack(syndromes, embedding.shape[1])
    pre_embed, embedded = activate(pointwise(embedding, bits))
    embed_pad = pad_edges(embedded)
    pre_first, first_act = activate(convolve(embed_pad, kernel_first))
    pooled_one = pad_edges(pool(first_act))
    pre_second, second_act = activate(convolve(pooled_one, kernel_second))
    pooled_two = pad_edges(pool(second_act))
    pre_bottom, bottom_act = activate(convolve(pooled_two, kernel_bottom))
    rise_mid = pad_edges(enlarge(bottom_act))
    pre_return, return_act = activate(convolve(rise_mid, kernel_return) + second_act.astype(jnp.float32))
    rise_fine = pad_edges(enlarge(return_act))
    pre_final, final_act = activate(convolve(rise_fine, kernel_final) + first_act.astype(jnp.float32))
    logits = pointwise(readout, final_act)
    flat_cot = flatten(cotangent)
    readout_grad = lax.dot_general(flat_cot, flatten(final_act), (((1,), (1,)), ((), ())), preferred_element_type=jnp.float32)
    back_final = jnp.dot(readout.T, flat_cot, preferred_element_type=jnp.float32).reshape(final_act.shape)
    cot_final = descend(back_final, pre_final)
    final_grad = kernel_grad(rise_fine, cot_final)
    cot_return = descend(block_sum(convolve_back(pad_edges(cot_final), kernel_final)), pre_return)
    return_grad = kernel_grad(rise_mid, cot_return)
    cot_bottom = descend(block_sum(convolve_back(pad_edges(cot_return), kernel_return)), pre_bottom)
    bottom_grad = kernel_grad(pooled_two, cot_bottom)
    through_bottom = convolve_back(pad_edges(cot_bottom), kernel_bottom)
    cot_second = descend(cot_return.astype(jnp.float32) + 0.25 * enlarge(through_bottom), pre_second)
    second_grad = kernel_grad(pooled_one, cot_second)
    through_second = convolve_back(pad_edges(cot_second), kernel_second)
    cot_first = descend(cot_final.astype(jnp.float32) + 0.25 * enlarge(through_second), pre_first)
    first_grad = kernel_grad(embed_pad, cot_first)
    feature_grad = descend(convolve_back(pad_edges(cot_first), kernel_first), pre_embed)
    embedding_grad = lax.dot_general(flatten(feature_grad), flatten(bits), (((1,), (1,)), ((), ())), preferred_element_type=jnp.float32)
    return (logits, feature_grad, embedding_grad, first_grad, second_grad, bottom_grad, return_grad, final_grad, readout_grad)
```

```python
import jax
import jax.numpy as jnp
import numpy as np
from jax import lax
from jax.experimental import pallas as pl
from jax.experimental.pallas import tpu as pltpu
from jax.sharding import PartitionSpec as P

ROWS = 6144
HALF = ROWS // 2
PART = HALF // 2
CHUNK = PART // 4
SUB = CHUNK // 4
LEAF = SUB // 2


def places():
    row, col = lax.axis_index("row"), lax.axis_index("col")
    return row // 2, row % 2, col % 4, col // 4


def remote(src, dst, send, recv, target):
    return pltpu.make_async_remote_copy(
        src_ref=src, dst_ref=dst, send_sem=send, recv_sem=recv, device_id=target, device_id_type=pl.DeviceIdType.MESH
    )


def peer(axis, d):
    x, core, y, z = places()
    if axis == "core":
        return {"row": x * 2 + 1 - core}
    if axis == "z":
        return {"col": (1 - z) * 4 + y}
    if axis == "x":
        return {"row": (x + d) % 4 * 2 + core}
    return {"col": z * 4 + (y + d) % 4}


def sum_kernel(x_ref, o_ref, s1, r1, h1, s2, r2, h2, s3, r3, h3, s4, r4, g, ss1, rs1, ss2, rs2, ss3, rs3, ss4, rs4):
    x, core, y, z = places()
    barrier = pltpu.get_barrier_semaphore()
    hops = [("core", 1), ("z", 1)] + [(axis, d) for axis in "xy" for d in (1, 2, 3)]
    for axis, d in hops:
        pl.semaphore_signal(barrier, inc=1, device_id=peer(axis, d), device_id_type=pl.DeviceIdType.MESH)
    pl.semaphore_wait(barrier, len(hops))

    def span(start, size, unit=16):
        return pl.ds(pl.multiple_of(start, unit), size)

    bf, f32 = jnp.bfloat16, jnp.float32
    s1[...] = x_ref[span((1 - core) * HALF, HALF), :].astype(bf)
    first = remote(s1, r1, ss1.at[0], rs1.at[0], peer("core", 1))
    first.start()
    first.wait()
    h1[...] = x_ref[span(core * HALF, HALF), :] + r1[...].astype(f32)

    s2[...] = h1[...].astype(bf)
    copies = []
    for part, axis, me in ((0, "x", x), (1, "y", y)):
        for d in (1, 2, 3):
            copies.append(remote(s2.at[span(part * PART + (me + d) % 4 * CHUNK, CHUNK), :], r2.at[part, d - 1], ss2.at[part, d - 1], rs2.at[part, d - 1], peer(axis, d)))
    for copy in copies:
        copy.start()
    for copy in copies:
        copy.wait()
    for part, me in ((0, x), (1, y)):
        total = h1[span(part * PART + me * CHUNK, CHUNK), :]
        for d in range(3):
            total = total + r2[part, d].astype(f32)
        h2[part] = total

    s3[...] = h2[...].astype(bf)
    copies = []
    for part, axis, me in ((0, "y", y), (1, "x", x)):
        for d in (1, 2, 3):
            copies.append(remote(s3.at[part, span((me + d) % 4 * SUB, SUB), :], r3.at[part, d - 1], ss3.at[part, d - 1], rs3.at[part, d - 1], peer(axis, d)))
    for copy in copies:
        copy.start()
    for copy in copies:
        copy.wait()
    for part, me in ((0, y), (1, x)):
        total = h2[part, span(me * SUB, SUB), :]
        for d in range(3):
            total = total + r3[part, d].astype(f32)
        h3[part] = total

    s4[...] = h3[:, span((1 - z) * LEAF, LEAF), :].astype(bf)
    fourth = remote(s4, r4, ss4.at[0], rs4.at[0], peer("z", 1))
    fourth.start()
    fourth.wait()

    base = [core * HALF + x * CHUNK + y * SUB, core * HALF + PART + y * CHUNK + x * SUB]
    for part in (0, 1):
        g[span(base[part] + z * LEAF, LEAF), :] = (h3[part, span(z * LEAF, LEAF), :] + r4[part].astype(f32)).astype(bf)

    def spread(jobs, send, recv):
        copies = []
        for k, (start, size, axis, d) in enumerate(jobs):
            here = g.at[span(start, size), :]
            copies.append(remote(here, here, send.at[k], recv.at[k], peer(axis, d)))
        for copy in copies:
            copy.start()
        for copy in copies:
            copy.wait()

    spread([(base[part] + z * LEAF, LEAF, "z", 1) for part in (0, 1)], ss4.at[pl.ds(1, 2)], rs4.at[pl.ds(1, 2)])
    spread([(base[part], SUB, axis, d) for part, axis in ((0, "y"), (1, "x")) for d in (1, 2, 3)], ss3.at[2], rs3.at[2])
    wide = [core * HALF + x * CHUNK, core * HALF + PART + y * CHUNK]
    spread([(wide[part], CHUNK, axis, d) for part, axis in ((0, "x"), (1, "y")) for d in (1, 2, 3)], ss2.at[2], rs2.at[2])
    spread([(core * HALF, HALF, "core", 1)], ss1.at[pl.ds(1, 1)], rs1.at[pl.ds(1, 1)])
    o_ref[...] = g[...].astype(f32)


def all_sum(values):
    bf, f32 = jnp.bfloat16, jnp.float32
    return pl.pallas_call(
        sum_kernel,
        out_shape=jax.ShapeDtypeStruct((ROWS, 128), f32),
        in_specs=[pl.BlockSpec(memory_space=pltpu.VMEM)],
        out_specs=pl.BlockSpec(memory_space=pltpu.VMEM),
        scratch_shapes=[
            pltpu.VMEM((HALF, 128), bf),
            pltpu.VMEM((HALF, 128), bf),
            pltpu.VMEM((HALF, 128), f32),
            pltpu.VMEM((HALF, 128), bf),
            pltpu.VMEM((2, 3, CHUNK, 128), bf),
            pltpu.VMEM((2, CHUNK, 128), f32),
            pltpu.VMEM((2, CHUNK, 128), bf),
            pltpu.VMEM((2, 3, SUB, 128), bf),
            pltpu.VMEM((2, SUB, 128), f32),
            pltpu.VMEM((2, LEAF, 128), bf),
            pltpu.VMEM((2, LEAF, 128), bf),
            pltpu.VMEM((ROWS, 128), bf),
        ]
        + [pltpu.SemaphoreType.DMA(n) for n in ((2,), (2,), (3, 6), (3, 6), (3, 6), (3, 6), (3,), (3,))],
        compiler_params=pltpu.CompilerParams(collective_id=0, has_side_effects=True, vmem_limit_bytes=48 * 2**20),
    )(values)


def extended(cells, sides, width):
    for axis, dim in sides:
        count = lax.axis_size(axis)
        ends = count - 1
        head = lax.slice_in_dim(cells, 0, width, axis=dim)
        tail = lax.slice_in_dim(cells, cells.shape[dim] - width, cells.shape[dim], axis=dim)
        cells = jnp.concatenate(
            [
                lax.ppermute(tail, axis, [(i, (i + 1) % count) for i in range(ends)]),
                cells,
                lax.ppermute(head, axis, [((i + 1) % count, i) for i in range(ends)]),
            ],
            axis=dim,
        )
    return cells


def unpack(syndromes, count):
    shifts = jnp.arange(count, dtype=jnp.int32)
    return (syndromes[None, :, :] >> shifts[:, None, None] & 1).astype(jnp.bfloat16)


def flatten(values):
    return values.reshape(values.shape[0], values.shape[1] * values.shape[2])


def pointwise(weight, values):
    product = jnp.dot(weight, flatten(values), preferred_element_type=jnp.float32)
    return product.reshape(weight.shape[0], values.shape[1], values.shape[2])


def convolve(padded, kernel):
    height, breadth = (padded.shape[1] - 2, padded.shape[2] - 2)
    summed = jnp.zeros((kernel.shape[2], height * breadth), jnp.float32)
    for row_tap in range(3):
        for col_tap in range(3):
            window = flatten(padded[:, row_tap : row_tap + height, col_tap : col_tap + breadth])
            summed = summed + jnp.dot(
                kernel[row_tap, col_tap], window, preferred_element_type=jnp.float32
            )
    return summed.reshape(kernel.shape[2], height, breadth)


def convolve_back(padded, kernel):
    height, breadth = (padded.shape[1] - 2, padded.shape[2] - 2)
    summed = jnp.zeros((kernel.shape[3], height * breadth), jnp.float32)
    for row_tap in range(3):
        for col_tap in range(3):
            window = flatten(
                padded[:, 2 - row_tap : 2 - row_tap + height, 2 - col_tap : 2 - col_tap + breadth]
            )
            summed = summed + jnp.dot(
                kernel[row_tap, col_tap].T, window, preferred_element_type=jnp.float32
            )
    return summed.reshape(kernel.shape[3], height, breadth)


def kernel_grad(padded, cotan):
    height, breadth = (cotan.shape[1], cotan.shape[2])
    flattened = flatten(cotan)
    grid = []
    for row_tap in range(3):
        line = []
        for col_tap in range(3):
            window = flatten(padded[:, row_tap : row_tap + height, col_tap : col_tap + breadth])
            line.append(
                lax.dot_general(
                    flattened, window, (((1,), (1,)), ((), ())), preferred_element_type=jnp.float32
                )
            )
        grid.append(jnp.stack(line))
    return jnp.stack(grid)


def activate(preact):
    stored = lax.optimization_barrier(preact.astype(jnp.bfloat16))
    widened = stored.astype(jnp.float32)
    return (stored, (widened * jax.nn.sigmoid(widened)).astype(jnp.bfloat16))


def descend(incoming, stored):
    widened = stored.astype(jnp.float32)
    logistic = jax.nn.sigmoid(widened)
    return (incoming * logistic * (1.0 + widened * (1.0 - logistic))).astype(jnp.bfloat16)


def pool(values):
    channels, height, breadth = values.shape
    blocks = values.astype(jnp.float32).reshape(channels, height // 2, 2, breadth // 2, 2)
    return (blocks.sum(axis=(2, 4)) * 0.25).astype(jnp.bfloat16)


def enlarge(values):
    return jnp.repeat(jnp.repeat(values, 2, axis=1), 2, axis=2)


def block_sum(values):
    channels, height, breadth = values.shape
    return values.reshape(channels, height // 2, 2, breadth // 2, 2).sum(axis=(2, 4))


def rimmed(values):
    return extended(values, (("row", 1), ("col", 2)), 1)


def on_device(
    syndromes,
    embedding,
    kernel_first,
    kernel_second,
    kernel_bottom,
    kernel_return,
    kernel_final,
    readout,
    cotangent,
):
    bits = unpack(syndromes, embedding.shape[1])
    pre_embed, embedded = activate(pointwise(embedding, bits))
    embed_pad = rimmed(embedded)
    pre_first, first_act = activate(convolve(embed_pad, kernel_first))
    pooled_one = rimmed(pool(first_act))
    pre_second, second_act = activate(convolve(pooled_one, kernel_second))
    pooled_small = pool(second_act)
    pooled_two = rimmed(pooled_small)
    pre_bottom, bottom_act = activate(convolve(pooled_two, kernel_bottom))
    rise_mid = enlarge(rimmed(bottom_act))[:, 1:-1, 1:-1]
    pre_return, return_act = activate(
        convolve(rise_mid, kernel_return) + second_act.astype(jnp.float32)
    )
    rise_fine = enlarge(rimmed(return_act))[:, 1:-1, 1:-1]
    pre_final, final_act = activate(
        convolve(rise_fine, kernel_final) + first_act.astype(jnp.float32)
    )
    logits = pointwise(readout, final_act)
    flat_cot = flatten(cotangent)
    readout_grad = lax.dot_general(
        flat_cot, flatten(final_act), (((1,), (1,)), ((), ())), preferred_element_type=jnp.float32
    )
    back_final = jnp.dot(readout.T, flat_cot, preferred_element_type=jnp.float32).reshape(
        final_act.shape
    )
    cot_final = descend(back_final, pre_final)
    final_grad = kernel_grad(rise_fine, cot_final)
    readout_grad, final_grad = (readout_grad, final_grad)
    cot_return = descend(block_sum(convolve_back(rimmed(cot_final), kernel_final)), pre_return)
    return_grad = kernel_grad(rise_mid, cot_return)
    cot_bottom = descend(block_sum(convolve_back(rimmed(cot_return), kernel_return)), pre_bottom)
    bottom_grad = kernel_grad(pooled_two, cot_bottom)
    through_bottom = convolve_back(rimmed(cot_bottom), kernel_bottom)
    cot_second = descend(
        cot_return.astype(jnp.float32) + 0.25 * enlarge(through_bottom), pre_second
    )
    second_grad = kernel_grad(pooled_one, cot_second)
    through_second = convolve_back(rimmed(cot_second), kernel_second)
    cot_first = descend(cot_final.astype(jnp.float32) + 0.25 * enlarge(through_second), pre_first)
    first_grad = kernel_grad(embed_pad, cot_first)
    feature_grad = descend(convolve_back(rimmed(cot_first), kernel_first), pre_embed)
    embedding_grad = lax.dot_general(
        flatten(feature_grad),
        flatten(bits),
        (((1,), (1,)), ((), ())),
        preferred_element_type=jnp.float32,
    )
    grads = (embedding_grad, first_grad, second_grad, bottom_grad, return_grad, final_grad, readout_grad)
    flat = jnp.concatenate([g.reshape(-1) for g in grads])
    flat = jnp.pad(flat, (0, ROWS * 128 - flat.shape[0])).reshape(ROWS, 128)
    flat = all_sum(flat).reshape(-1)
    summed, start = [], 0
    for g in grads:
        summed.append(flat[start : start + g.size].reshape(g.shape))
        start += g.size
    return (
        logits,
        feature_grad,
        summed[0],
        summed[1],
        summed[2],
        summed[3],
        summed[4],
        summed[5],
        summed[6],
    )


def solution(mesh):
    in_specs = (
        P(("batch", "row"), "col"),
        P(),
        P(),
        P(),
        P(),
        P(),
        P(),
        P(),
        P(None, ("batch", "row"), "col"),
    )
    out_specs = (
        P(None, ("batch", "row"), "col"),
        P(None, ("batch", "row"), "col"),
        P("batch", None),
        P("batch", None, None, None),
        P("batch", None, None, None),
        P("batch", None, None, None),
        P("batch", None, None, None),
        P("batch", None, None, None),
        P("batch", None),
    )
    return jax.shard_map(
        on_device, mesh=mesh, in_specs=in_specs, out_specs=out_specs, check_vma=False
    )
```

```python
import functools

import jax
import jax.numpy as jnp
import numpy as np
from jax import lax
from jax.experimental import pallas as pl
from jax.experimental.pallas import tpu as pltpu
from jax.sharding import PartitionSpec as P

BF, F32 = jnp.bfloat16, jnp.float32
MESH = pl.DeviceIdType.MESH

DEEP, WIDE = 8, 32
CELLS = DEEP * WIDE

ROWS = 6144
HALF = ROWS // 2
PART = HALF // 2
CHUNK = PART // 4
SUB = CHUNK // 4
LEAF = SUB // 2

AT_RETURN, AT_BOTTOM, AT_FINAL, AT_SECOND, AT_FIRST, AT_READ = 0, 2304, 4608, 5184, 5824, 6080


def ranged(values, start, size, unit=16):
    return values.at[pl.ds(pl.multiple_of(start, unit), size), :]


def shift_table():
    table = {}
    for dr in (-1, 0, 1):
        for dc in (-1, 0, 1):
            m = np.zeros((CELLS, CELLS), np.float32)
            for r in range(DEEP):
                for q in range(WIDE):
                    if 0 <= r + dr < DEEP and 0 <= q + dc < WIDE:
                        m[(r + dr) * WIDE + q + dc, r * WIDE + q] = 1
            table[dr, dc] = m
    return table


def gather_tables():
    blocks, where = [], {}

    def put(name, m):
        where[name] = len(blocks)
        blocks.append(m)

    for b in range(4):
        for name, r in (("up", 0), ("down", DEEP - 1)):
            m = np.zeros((CELLS, 128), np.float32)
            for q in range(WIDE):
                m[r * WIDE + q, b * WIDE + q] = 1
            put((name, b), m)
    for p in (4, 2, 1):
        for a in range(p):
            for name, q, base, corners in (("left", 0, 0, (64, 66)), ("right", WIDE - 1, 32, (65, 67))):
                m = np.zeros((CELLS, 128), np.float32)
                for r in range(DEEP):
                    m[r * WIDE + q, base + a * DEEP + r] = 1
                if a == 0:
                    m[q, corners[0]] = 1
                if a == p - 1:
                    m[(DEEP - 1) * WIDE + q, corners[1]] = 1
                put((name, p, a), m)
    return np.concatenate(blocks), where


def halo_tables():
    blocks, where = [], {}
    for p in (4, 2, 1):
        for ea in range(p + 2):
            for eb in range(p + 2):
                dr, dc = (ea > p) - (ea < 1), (eb > p) - (eb < 1)
                if (dr, dc) == (0, 0):
                    continue
                sa, sb = (ea - 1) % p, (eb - 1) % p
                m = np.zeros((3, 128, CELLS), np.float32)
                for r in range(DEEP):
                    for q in range(WIDE):
                        rr, qq = r + dr, q + dc
                        row_in, col_in = 0 <= rr < DEEP, 0 <= qq < WIDE
                        if row_in and col_in:
                            continue
                        if col_in:
                            tile, lane = (0 if rr < 0 else 1), sb * WIDE + qq
                        elif row_in:
                            tile, lane = 2, (32 if qq < 0 else 0) + sa * DEEP + rr
                        else:
                            tile, lane = 2, {(-1, -1): 67, (-1, 1): 66, (1, -1): 65, (1, 1): 64}[dr, dc]
                        m[tile, lane, r * WIDE + q] = 1
                used = []
                for tile in range(3):
                    if m[tile].any():
                        used.append((tile, len(blocks)))
                        blocks.append(m[tile])
                where[p, ea, eb] = used
    return np.concatenate(blocks), where


def spread_table():
    m = np.zeros((512, 512), np.float32)
    for r in range(4):
        for w in range(128):
            m[r * 128 + w, (w % 4) * 128 + r * WIDE + w // 4] = 1
    return m


SHIFTS = shift_table()
SHIFT_AT = {key: n for n, key in enumerate(SHIFTS)}
SHIFT_ALL = np.concatenate(list(SHIFTS.values()))
GATHER_ALL, GATHER_AT = gather_tables()
HALO_ALL, HALO_AT = halo_tables()
SPREAD = spread_table()

UNDER = (((0,), (1, 2)), ((0, 1), (2,)))
OVER = ((2,), (1, 2), (0, 1), (0,))
BASE = (0, 1, 1, 2)


def mm(a, b):
    return jnp.dot(a, b, preferred_element_type=F32)


def nt(a, b):
    return lax.dot_general(a, b, (((1,), (1,)), ((), ())), preferred_element_type=F32)


def logistic(z):
    return 0.5 + 0.5 * jnp.tanh(0.5 * z)


def activated(v):
    stored = v.astype(BF)
    z = stored.astype(F32)
    return stored, (z * logistic(z)).astype(BF)


def sloped(incoming, stored):
    z = stored.astype(F32)
    s = logistic(z)
    return (incoming * (s * (1.0 + z * (1.0 - s)))).astype(BF)


def remote(src, dst, send, recv, target):
    return pltpu.make_async_remote_copy(
        src_ref=src, dst_ref=dst, send_sem=send, recv_sem=recv, device_id=target, device_id_type=MESH
    )


SIDES = ((-1, 0), (1, 0), (0, -1), (0, 1), (-1, -1), (-1, 1), (1, -1), (1, 1))
SLOT = {(-1, 0): 0, (1, 0): 1, (0, -1): 2, (0, 1): 3, (-1, -1): 4, (-1, 1): 5, (1, -1): 6, (1, 1): 7}


def net_kernel(counts, *refs):
    it = iter(refs)

    def take(n):
        return [next(it) for _ in range(n)]

    syn, emb, k1, k2, k3, k4, k5, rdo, cot, cS, cG, cT, cU, cV = take(14)
    logits_ref, fg_ref, g_ref = take(3)
    xb, e0, z0, z1, f1, e1, z2, f2, e2, z3, e3, z4, e4, z5, f5, t5, t4, t3, t2, t1, fg, cp = take(22)
    w0, w1, w1b, w2, w2b, w3, w3b, w4, w4b, w5, w5b, r4, r4t = take(13)
    halos = [take(2) for _ in range(10)]
    sends, recvs = take(2)

    n_row, n_col = counts
    row, col = lax.axis_index("row"), lax.axis_index("col")
    there = {
        (-1, 0): row > 0,
        (1, 0): row < n_row - 1,
        (0, -1): col > 0,
        (0, 1): col < n_col - 1,
    }
    for dr in (-1, 1):
        for dc in (-1, 1):
            there[dr, dc] = jnp.logical_and(there[dr, 0], there[0, dc])

    def place(dr, dc):
        return {"row": (row + dr + n_row) % n_row, "col": (col + dc + n_col) % n_col}

    barrier = pltpu.get_barrier_semaphore()
    for side in SIDES:
        pl.semaphore_signal(barrier, inc=1, device_id=place(*side), device_id_type=MESH)
    pl.semaphore_wait(barrier, len(SIDES))

    def shift(dr, dc):
        n = SHIFT_AT[dr, dc]
        return cS[n * CELLS : (n + 1) * CELLS, :]

    def gather(*name):
        n = GATHER_AT[name]
        return cG[n * CELLS : (n + 1) * CELLS, :]

    lane = lax.broadcasted_iota(jnp.int32, (1, 128), 1)

    def begin(n, p, width, ref):
        out, into = halos[n]

        def phase(a, b):
            start = ((a + 1) * (p + 2) + b + 1) * width
            return ref[start : start + width, :]

        out[0] = sum(mm(phase(0, b), gather("up", b)) for b in range(p)).astype(BF)
        out[1] = sum(mm(phase(p - 1, b), gather("down", b)) for b in range(p)).astype(BF)
        out[2] = sum(
            mm(phase(a, 0), gather("left", p, a)) + mm(phase(a, p - 1), gather("right", p, a)) for a in range(p)
        ).astype(BF)
        copies = []
        for k, (dr, dc) in enumerate(SIDES):
            src = out.at[(0 if dr < 0 else 1) if dc == 0 else 2]
            slot = SLOT[-dr, -dc]
            copies.append(remote(src, into.at[slot], sends.at[n, slot], recvs.at[n, slot], place(dr, dc)))
        for copy in copies:
            copy.start()
        return copies

    def end(n, p, width, ref, copies):
        into = halos[n][1]
        for copy in copies:
            copy.wait()

        def got(side, low=0, high=128):
            keep = jnp.logical_and(jnp.logical_and(lane >= low, lane < high), there[side])
            return jnp.where(keep, into[SLOT[side]].astype(F32), 0.0)

        third = got((0, 1), 0, 32) + got((0, -1), 32, 64)
        for k, side in enumerate(((1, 1), (1, -1), (-1, 1), (-1, -1))):
            third = third + got(side, 64 + k, 65 + k)
        tiles = [got((-1, 0)).astype(BF), got((1, 0)).astype(BF), third.astype(BF)]
        for ea in range(p + 2):
            for eb in range(p + 2):
                dr, dc = (ea > p) - (ea < 1), (eb > p) - (eb < 1)
                if (dr, dc) == (0, 0):
                    continue
                start = (((ea - 1) % p + 1) * (p + 2) + (eb - 1) % p + 1) * width
                moved = mm(ref[start : start + width, :], shift(dr, dc))
                for tile, block in HALO_AT[p, ea, eb]:
                    moved = moved + mm(tiles[tile], cT[block * 128 : (block + 1) * 128, :])
                start = (ea * (p + 2) + eb) * width
                ref[start : start + width, :] = moved.astype(BF)

    bit = lax.broadcasted_iota(jnp.int32, (16, 1), 0)
    groups = []
    for a in range(4):
        for t in range(2):
            line = [(syn[16 * t + 4 * r + a : 16 * t + 4 * r + a + 1, :] >> bit) & 1 for r in range(4)]
            groups.append(jnp.concatenate(line, axis=1))
    bits = jnp.concatenate(groups, axis=0).astype(F32).astype(BF)
    phased = mm(bits, cU[...]).astype(BF)
    for a in range(4):
        for t in range(2):
            for b in range(4):
                start = ((a + 1) * 6 + b + 1) * 16
                xb[start : start + 16, t * 128 : (t + 1) * 128] = phased[(a * 2 + t) * 16 : (a * 2 + t + 1) * 16, b * 128 : (b + 1) * 128]
    copies = begin(0, 4, 16, xb)

    eye = shift(0, 0)
    repeat = (lax.broadcasted_iota(jnp.int32, (16, 96), 1) % 16 == lax.broadcasted_iota(jnp.int32, (16, 96), 0)).astype(F32).astype(BF)
    tiled = mm(emb[...], repeat)
    own = lax.broadcasted_iota(jnp.int32, (64, 96), 1) // 16
    for j in range(6):
        w0[j * 64 : (j + 1) * 64, :] = jnp.where(own == j, tiled, 0.0).astype(BF)
    for ta in range(3):
        for i in range(2):
            w1[i * 64 : (i + 1) * 64, ta * 256 : (ta + 1) * 256] = sum(
                mm(k1[ta, tb], eye[(tb + i) * 64 : (tb + i + 1) * 64, :]) for tb in range(3)
            ).astype(BF)
            w2[i * 128 : (i + 1) * 128, ta * 256 : (ta + 1) * 256] = sum(
                mm(k2[ta, tb], eye[(tb + i) * 64 : (tb + i + 1) * 64, :]) for tb in range(3)
            ).astype(BF)
            blank = [jnp.zeros((64, 64), BF)]
            line = [k1[2 - ta, 2 - tb] for tb in range(3)]
            line = line + blank if i == 0 else blank + line
            w1b[i * 64 : (i + 1) * 64, ta * 256 : (ta + 1) * 256] = nt(eye[:64, :64], jnp.concatenate(line, axis=0)).astype(BF)
            blank = [jnp.zeros((128, 64), BF)]
            line = [k2[2 - ta, 2 - tb] for tb in range(3)]
            line = line + blank if i == 0 else blank + line
            w2b[i * 64 : (i + 1) * 64, ta * 512 : (ta + 1) * 512] = nt(eye[:64, :64], jnp.concatenate(line, axis=0)).astype(BF)
    for t in range(9):
        w3[:, t * 128 : (t + 1) * 128] = k3[t // 3, t % 3]
        w3b[:, t * 256 : (t + 1) * 256] = nt(eye[:128, :128], k3[2 - t // 3, 2 - t % 3]).astype(BF)

    def added(k, rows, cols):
        return sum(k[ta, tb].astype(F32) for ta in rows for tb in cols).astype(BF)

    for pa in range(2):
        for pb in range(2):
            for s in range(2):
                for u in range(2):
                    block = added(k4, UNDER[pa][s], UNDER[pb][u])
                    w4[(pa * 2 + pb) * 128 : (pa * 2 + pb + 1) * 128, (s * 2 + u) * 256 : (s * 2 + u + 1) * 256] = block
                    at = OVER.index(UNDER[pa][s]) * 4 + OVER.index(UNDER[pb][u])
                    w4b[:, at * 128 : (at + 1) * 128] = nt(eye, block).astype(BF)
                    start = pa * 128 + (1 - pb) * 64
                    w5[start : start + 64, (s * 2 + u) * 128 : (s * 2 + u + 1) * 128] = added(k5, UNDER[pa][s], UNDER[pb][u])
    for ea in range(4):
        for pair in range(2):
            stack = jnp.concatenate([added(k5, OVER[ea], OVER[2 * pair + i]) for i in range(2)], axis=0)
            at = ea * 2 + pair
            w5b[:, at * 128 : (at + 1) * 128] = nt(eye[:128, :128], stack).astype(BF)

    repeat = (lax.broadcasted_iota(jnp.int32, (64, 256), 1) % 64 == lax.broadcasted_iota(jnp.int32, (64, 256), 0)).astype(F32).astype(BF)
    tiled = mm(rdo[...], repeat)
    tiled = jnp.concatenate([tiled, jnp.zeros((2, 256), F32)] * 4, axis=0)
    own = lax.broadcasted_iota(jnp.int32, (16, 256), 1) // 64 == lax.broadcasted_iota(jnp.int32, (16, 256), 0) // 4
    r4[...] = jnp.where(own, tiled, 0.0).astype(BF)
    r4t[...] = nt(eye, r4[...]).astype(BF)

    wide = cot[...].astype(F32)
    groups = []
    for a in range(4):
        for t in range(2):
            line = jnp.concatenate([wide[:, 16 * t + 4 * r + a, :] for r in range(4)], axis=1)
            groups.append(jnp.concatenate([line, jnp.zeros((6, 512), F32)], axis=0))
    phased = mm(jnp.concatenate(groups, axis=0).astype(BF), cU[...])
    for a in range(4):
        for t in range(2):
            start = (a * 2 + t) * 8
            pieces = [phased[start : start + 4, b * 128 : (b + 1) * 128] for b in range(4)]
            cp[a * 16 : (a + 1) * 16, t * 128 : (t + 1) * 128] = jnp.concatenate(pieces, axis=0).astype(BF)

    end(0, 4, 16, xb, copies)

    for ea in range(6):
        stored, active = activated(mm(w0[...], xb[ea * 96 : (ea + 1) * 96, :]))
        e0[ea * 384 : (ea + 1) * 384, :] = active
        if 1 <= ea <= 4:
            z0[(ea - 1) * 256 : ea * 256, :] = stored[64:320, :]

    for a in range(4):
        for pair in range(2):
            v = sum(
                mm(w1[:, ta * 256 : (ta + 1) * 256], e0[((a + ta) * 6 + 2 * pair) * 64 : ((a + ta) * 6 + 2 * pair + 4) * 64, :])
                for ta in range(3)
            )
            start = (a * 4 + 2 * pair) * 64
            z1[start : start + 128, :], f1[start : start + 128, :] = activated(v)

    def pooled(ref, side, width, a, b):
        spots = [((2 * a + i) * side + 2 * b + j) * width for i in range(2) for j in range(2)]
        return (sum(ref[s : s + width, :].astype(F32) for s in spots) * 0.25).astype(BF)

    for a in range(2):
        for b in range(2):
            start = ((a + 1) * 4 + b + 1) * 64
            e1[start : start + 64, :] = pooled(f1, 4, 64, a, b)
    end(1, 2, 64, e1, begin(1, 2, 64, e1))

    for a in range(2):
        v = sum(mm(w2[:, ta * 256 : (ta + 1) * 256], e1[(a + ta) * 256 : (a + ta + 1) * 256, :]) for ta in range(3))
        z2[a * 256 : (a + 1) * 256, :], f2[a * 256 : (a + 1) * 256, :] = activated(v)
    e2[4 * 128 : 5 * 128, :] = pooled(f2, 2, 128, 0, 0)
    end(2, 1, 128, e2, begin(2, 1, 128, e2))

    z3[...], e3[4 * 256 : 5 * 256, :] = activated(mm(w3[...], e2[...]))
    end(3, 1, 256, e3, begin(3, 1, 256, e3))

    for a in range(2):
        for b in range(2):
            n = a * 2 + b
            v = sum(
                mm(w4[n * 128 : (n + 1) * 128, s * 512 : (s + 1) * 512], e3[((a + s) * 3 + b) * 256 : ((a + s) * 3 + b + 2) * 256, :])
                for s in range(2)
            )
            v = v + f2[n * 128 : (n + 1) * 128, :].astype(F32)
            start = ((a + 1) * 4 + b + 1) * 128
            z4[n * 128 : (n + 1) * 128, :], e4[start : start + 128, :] = activated(v)
    end(4, 2, 128, e4, begin(4, 2, 128, e4))

    RUNS = ((0, 1, 64, 64), (1, 2, 0, 128), (3, 1, 0, 64))
    for a in range(4):
        for b, many, first, size in RUNS:
            base = (a % 2) * 128 + first
            v = sum(
                mm(w5[base : base + size, s * 256 : (s + 1) * 256], e4[((BASE[a] + s) * 4 + BASE[b]) * 128 : ((BASE[a] + s) * 4 + BASE[b] + 2) * 128, :])
                for s in range(2)
            )
            start = (a * 4 + b) * 64
            v = v + f1[start : start + size, :].astype(F32)
            z5[start : start + size, :], f5[start : start + size, :] = activated(v)

    for a in range(4):
        back = mm(r4t[...], cp[a * 16 : (a + 1) * 16, :])
        start = ((a + 1) * 6 + 1) * 64
        t5[start : start + 256, :] = sloped(back, z5[a * 256 : (a + 1) * 256, :])
    copies = begin(5, 4, 64, t5)

    groups = []
    total = jnp.zeros((16, 256), F32)
    for a in range(4):
        here = f5[a * 256 : (a + 1) * 256, :]
        value = mm(r4[...], here)
        total = total + nt(cp[a * 16 : (a + 1) * 16, :], here)
        for t in range(2):
            groups.append(jnp.concatenate([value[b * 4 : (b + 1) * 4, t * 128 : (t + 1) * 128] for b in range(4)], axis=1))
    value = jnp.concatenate(groups, axis=0)
    laid = 0.0
    for _ in range(3):
        piece = value.astype(BF)
        laid = laid + mm(piece, cV[...])
        value = value - piece.astype(F32)
    for a in range(4):
        for t in range(2):
            for r in range(4):
                h = 16 * t + 4 * r + a
                logits_ref[:, h * 128 : (h + 1) * 128] = laid[(a * 2 + t) * 4 : (a * 2 + t + 1) * 4, r * 128 : (r + 1) * 128]
    total = sum(total[b * 4 : (b + 1) * 4, b * 64 : (b + 1) * 64] for b in range(4))
    g_ref[AT_READ : AT_READ + 64, :] = jnp.zeros((64, 128), F32)
    g_ref[AT_READ : AT_READ + 4, 0:64] = total

    sums = {}
    for a in range(4):
        for s in range(2):
            for b, many, first, size in RUNS:
                start = ((BASE[a] + s) * 4 + BASE[b]) * 128
                t_start = ((a + 1) * 6 + b + 1) * 64
                product = nt(t5[t_start : t_start + size, :], e4[start : start + 256, :])
                for m in range(many):
                    key = (a % 2, s, (b + m) % 2)
                    block = product[m * 64 : (m + 1) * 64, :]
                    sums[key] = sums[key] + block if key in sums else block

    def reads(parity, tap):
        return 0 if tap in UNDER[parity][0] else 1

    for ta in range(3):
        rowed = [sums[0, reads(0, ta), pb] + sums[1, reads(1, ta), pb] for pb in range(2)]
        for tb in range(3):
            value = sum(rowed[pb][:, reads(pb, tb) * 128 : (reads(pb, tb) + 1) * 128] for pb in range(2))
            start = AT_FINAL + (ta * 3 + tb) * 64
            g_ref[start : start + 64, :] = value

    end(5, 4, 64, t5, copies)
    for a in range(2):
        for b in range(2):
            v = sum(
                mm(w5b[:, m * 256 : (m + 1) * 256], t5[((2 * a + m) * 6 + 2 * b) * 64 : ((2 * a + m) * 6 + 2 * b + 4) * 64, :])
                for m in range(4)
            )
            start = ((a + 1) * 4 + b + 1) * 128
            n = a * 2 + b
            t4[start : start + 128, :] = sloped(v, z4[n * 128 : (n + 1) * 128, :])
    copies = begin(6, 2, 128, t4)

    for b in range(2):
        for u in range(2):
            parts = {}
            for a in range(2):
                for s in range(2):
                    start = ((a + 1) * 4 + b + 1) * 128
                    from_ = ((a + s) * 3 + b + u) * 256
                    parts[a, s] = nt(t4[start : start + 128, :], e3[from_ : from_ + 256, :])
            for ta in range(3):
                value = parts[0, reads(0, ta)] + parts[1, reads(1, ta)]
                for tb in UNDER[b][u]:
                    for half in range(2):
                        start = AT_RETURN + ((ta * 3 + tb) * 2 + half) * 128
                        piece = value[:, half * 128 : (half + 1) * 128]
                        g_ref[start : start + 128, :] = piece if b == 0 else g_ref[start : start + 128, :] + piece

    end(6, 2, 128, t4, copies)
    v = sum(mm(w4b[:, m * 512 : (m + 1) * 512], t4[m * 512 : (m + 1) * 512, :]) for m in range(4))
    t3[4 * 256 : 5 * 256, :] = sloped(v, z3[...])
    copies = begin(7, 1, 256, t3)
    for t in range(9):
        g_ref[AT_BOTTOM + t * 256 : AT_BOTTOM + (t + 1) * 256, :] = nt(t3[4 * 256 : 5 * 256, :], e2[t * 128 : (t + 1) * 128, :])
    end(7, 1, 256, t3, copies)

    through = mm(w3b[...], t3[...]) * 0.25
    for a in range(2):
        for b in range(2):
            n = a * 2 + b
            start = ((a + 1) * 4 + b + 1) * 128
            t2[start : start + 128, :] = sloped(t4[start : start + 128, :].astype(F32) + through, z2[n * 128 : (n + 1) * 128, :])
    copies = begin(8, 2, 128, t2)
    ends = []
    for ta in range(3):
        product = 0.0
        for a in range(2):
            start = ((a + 1) * 4 + 1) * 128
            product = product + nt(t2[start : start + 256, :], e1[(a + ta) * 256 : (a + ta + 1) * 256, :])
        value = product[0:128, 0:192] + product[128:256, 64:256]
        g_ref[AT_SECOND + ta * 128 : AT_SECOND + (ta + 1) * 128, :] = value[:, 0:128]
        ends.append(value[:, 128:192])
    g_ref[AT_SECOND + 384 : AT_SECOND + 512, :] = jnp.concatenate(ends[:2], axis=1)
    g_ref[AT_SECOND + 512 : AT_SECOND + 640, 0:64] = ends[2]
    end(8, 2, 128, t2, copies)

    for a in range(2):
        v = sum(mm(w2b[:, ta * 512 : (ta + 1) * 512], t2[(a + ta) * 512 : (a + ta + 1) * 512, :]) for ta in range(3)) * 0.25
        for b in range(2):
            for i in range(2):
                for j in range(2):
                    fa, fb = 2 * a + i, 2 * b + j
                    start = ((fa + 1) * 6 + fb + 1) * 64
                    n = (fa * 4 + fb) * 64
                    t1[start : start + 64, :] = sloped(t5[start : start + 64, :].astype(F32) + v[b * 64 : (b + 1) * 64, :], z1[n : n + 64, :])
    copies = begin(9, 4, 64, t1)
    for ta in range(3):
        product = 0.0
        for a in range(4):
            for pair in range(2):
                start = ((a + 1) * 6 + 2 * pair + 1) * 64
                from_ = ((a + ta) * 6 + 2 * pair) * 64
                product = product + nt(t1[start : start + 128, :], e0[from_ : from_ + 256, :])
        value = product[0:64, 0:192] + product[64:128, 64:256]
        g_ref[AT_FIRST + ta * 64 : AT_FIRST + (ta + 1) * 64, :] = value[:, 0:128]
        if ta < 2:
            g_ref[AT_SECOND + 512 + ta * 64 : AT_SECOND + 512 + (ta + 1) * 64, 64:128] = value[:, 128:192]
        else:
            g_ref[AT_FIRST + 192 : AT_FIRST + 256, 64:128] = value[:, 128:192]
    end(9, 4, 64, t1, copies)

    total = jnp.zeros((256, 64), F32)
    for a in range(4):
        for pair in range(2):
            v = sum(
                mm(w1b[:, ta * 256 : (ta + 1) * 256], t1[((a + ta) * 6 + 2 * pair) * 64 : ((a + ta) * 6 + 2 * pair + 4) * 64, :])
                for ta in range(3)
            )
            start = (a * 4 + 2 * pair) * 64
            fg[start : start + 128, :] = sloped(v, z0[start : start + 128, :])
        start = ((a + 1) * 6 + 1) * 16
        total = total + nt(fg[a * 256 : (a + 1) * 256, :], xb[start : start + 64, :])
    total = sum(total[b * 64 : (b + 1) * 64, b * 16 : (b + 1) * 16] for b in range(4))
    g_ref[AT_FIRST + 192 : AT_FIRST + 256, 0:16] = total
    g_ref[AT_FIRST + 192 : AT_FIRST + 256, 16:64] = jnp.zeros((64, 48), F32)

    for a in range(4):
        for t in range(2):
            line = jnp.concatenate([fg[(a * 4 + b) * 64 : (a * 4 + b + 1) * 64, t * 128 : (t + 1) * 128] for b in range(4)], axis=1)
            laid = mm(line, cV[...]).astype(BF)
            for r in range(4):
                h = 16 * t + 4 * r + a
                fg_ref[:, h * 128 : (h + 1) * 128] = laid[:, r * 128 : (r + 1) * 128]


LEVELS = ((4, 16), (2, 64), (1, 128), (1, 256), (2, 128), (4, 64), (2, 128), (1, 256), (2, 128), (4, 64))


def run_net(counts, *args):
    tables = [jnp.asarray(t, BF) for t in (SHIFT_ALL, GATHER_ALL, HALO_ALL, SPREAD, SPREAD.T)]
    blocks = [16 * 36, 64 * 36, 1024, 1024, 1024, 64 * 16, 512, 512, 128 * 9, 256, 256 * 9, 512, 128 * 16, 1024, 1024]
    blocks += [64 * 36, 128 * 16, 256 * 9, 128 * 16, 64 * 36, 1024, 64]
    weights = [(384, 96), (128, 768), (128, 768), (256, 768), (128, 1536), (256, 1152), (128, 2304), (512, 1024), (256, 2048), (256, 512), (128, 1024), (16, 256), (256, 16)]
    scratch = [pltpu.VMEM((n, CELLS), BF) for n in blocks] + [pltpu.VMEM(s, BF) for s in weights]
    for _, width in LEVELS:
        scratch += [pltpu.VMEM((3, width, 128), BF), pltpu.VMEM((8, width, 128), BF)]
    scratch += [pltpu.SemaphoreType.DMA((10, 8)), pltpu.SemaphoreType.DMA((10, 8))]
    vmem = pl.BlockSpec(memory_space=pltpu.VMEM)
    return pl.pallas_call(
        functools.partial(net_kernel, counts),
        out_shape=(
            jax.ShapeDtypeStruct((4, 4096), F32),
            jax.ShapeDtypeStruct((64, 4096), BF),
            jax.ShapeDtypeStruct((ROWS, 128), F32),
        ),
        in_specs=[vmem] * 14,
        out_specs=(vmem, vmem, vmem),
        scratch_shapes=scratch,
        compiler_params=pltpu.CompilerParams(collective_id=1, has_side_effects=True, vmem_limit_bytes=56 * 2**20),
    )(*args, *tables)


def unlaid(g):
    by_return = g[AT_RETURN : AT_RETURN + 2304].reshape(3, 3, 2, 128, 128).transpose(0, 1, 3, 2, 4).reshape(3, 3, 128, 256)
    by_bottom = g[AT_BOTTOM : AT_BOTTOM + 2304].reshape(3, 3, 256, 128)
    by_final = g[AT_FINAL : AT_FINAL + 576].reshape(3, 3, 64, 128)
    wide = g[AT_SECOND : AT_SECOND + 384].reshape(3, 128, 2, 64).transpose(0, 2, 1, 3)
    two = g[AT_SECOND + 384 : AT_SECOND + 512].reshape(128, 2, 64).transpose(1, 0, 2)
    one = g[AT_SECOND + 512 : AT_SECOND + 640]
    last = jnp.concatenate([two, one[None, :, :64]], axis=0)
    by_second = jnp.concatenate([wide, last[:, None]], axis=1)
    wide = g[AT_FIRST : AT_FIRST + 192].reshape(3, 64, 2, 64).transpose(0, 2, 1, 3)
    tail = g[AT_FIRST + 192 : AT_FIRST + 256]
    last = jnp.concatenate([one[:, 64:].reshape(2, 64, 64), tail[None, :, 64:]], axis=0)
    by_first = jnp.concatenate([wide, last[:, None]], axis=1)
    return tail[:, :16], by_first, by_second, by_bottom, by_return, by_final, g[AT_READ : AT_READ + 2, :64]


def places():
    row, col = lax.axis_index("row"), lax.axis_index("col")
    return row // 2, row % 2, col % 4, col // 4


def peer(axis, d):
    x, core, y, z = places()
    if axis == "core":
        return {"row": x * 2 + 1 - core}
    if axis == "z":
        return {"col": (1 - z) * 4 + y}
    if axis == "x":
        return {"row": (x + d) % 4 * 2 + core}
    return {"col": z * 4 + (y + d) % 4}


def sum_kernel(x_ref, o_ref, s1, r1, h1, s2, r2, h2, s3, r3, h3, s4, r4, g, ss1, rs1, ss2, rs2, ss3, rs3, ss4, rs4):
    x, core, y, z = places()
    barrier = pltpu.get_barrier_semaphore()
    hops = [("core", 1), ("z", 1)] + [(axis, d) for axis in "xy" for d in (1, 2, 3)]
    for axis, d in hops:
        pl.semaphore_signal(barrier, inc=1, device_id=peer(axis, d), device_id_type=pl.DeviceIdType.MESH)
    pl.semaphore_wait(barrier, len(hops))

    def span(start, size, unit=16):
        return pl.ds(pl.multiple_of(start, unit), size)

    bf, f32 = jnp.bfloat16, jnp.float32
    s1[...] = x_ref[span((1 - core) * HALF, HALF), :].astype(bf)
    first = remote(s1, r1, ss1.at[0], rs1.at[0], peer("core", 1))
    first.start()
    first.wait()
    h1[...] = x_ref[span(core * HALF, HALF), :] + r1[...].astype(f32)

    s2[...] = h1[...].astype(bf)
    copies = []
    for part, axis, me in ((0, "x", x), (1, "y", y)):
        for d in (1, 2, 3):
            copies.append(remote(s2.at[span(part * PART + (me + d) % 4 * CHUNK, CHUNK), :], r2.at[part, d - 1], ss2.at[part, d - 1], rs2.at[part, d - 1], peer(axis, d)))
    for copy in copies:
        copy.start()
    for copy in copies:
        copy.wait()
    for part, me in ((0, x), (1, y)):
        total = h1[span(part * PART + me * CHUNK, CHUNK), :]
        for d in range(3):
            total = total + r2[part, d].astype(f32)
        h2[part] = total

    s3[...] = h2[...].astype(bf)
    copies = []
    for part, axis, me in ((0, "y", y), (1, "x", x)):
        for d in (1, 2, 3):
            copies.append(remote(s3.at[part, span((me + d) % 4 * SUB, SUB), :], r3.at[part, d - 1], ss3.at[part, d - 1], rs3.at[part, d - 1], peer(axis, d)))
    for copy in copies:
        copy.start()
    for copy in copies:
        copy.wait()
    for part, me in ((0, y), (1, x)):
        total = h2[part, span(me * SUB, SUB), :]
        for d in range(3):
            total = total + r3[part, d].astype(f32)
        h3[part] = total

    s4[...] = h3[:, span((1 - z) * LEAF, LEAF), :].astype(bf)
    fourth = remote(s4, r4, ss4.at[0], rs4.at[0], peer("z", 1))
    fourth.start()
    fourth.wait()

    base = [core * HALF + x * CHUNK + y * SUB, core * HALF + PART + y * CHUNK + x * SUB]
    for part in (0, 1):
        g[span(base[part] + z * LEAF, LEAF), :] = (h3[part, span(z * LEAF, LEAF), :] + r4[part].astype(f32)).astype(bf)

    def spread(jobs, send, recv):
        copies = []
        for k, (start, size, axis, d) in enumerate(jobs):
            here = g.at[span(start, size), :]
            copies.append(remote(here, here, send.at[k], recv.at[k], peer(axis, d)))
        for copy in copies:
            copy.start()
        for copy in copies:
            copy.wait()

    spread([(base[part] + z * LEAF, LEAF, "z", 1) for part in (0, 1)], ss4.at[pl.ds(1, 2)], rs4.at[pl.ds(1, 2)])
    spread([(base[part], SUB, axis, d) for part, axis in ((0, "y"), (1, "x")) for d in (1, 2, 3)], ss3.at[2], rs3.at[2])
    wide = [core * HALF + x * CHUNK, core * HALF + PART + y * CHUNK]
    spread([(wide[part], CHUNK, axis, d) for part, axis in ((0, "x"), (1, "y")) for d in (1, 2, 3)], ss2.at[2], rs2.at[2])
    spread([(core * HALF, HALF, "core", 1)], ss1.at[pl.ds(1, 1)], rs1.at[pl.ds(1, 1)])
    o_ref[...] = g[...].astype(f32)


def all_sum(values):
    bf, f32 = jnp.bfloat16, jnp.float32
    return pl.pallas_call(
        sum_kernel,
        out_shape=jax.ShapeDtypeStruct((ROWS, 128), f32),
        in_specs=[pl.BlockSpec(memory_space=pltpu.VMEM)],
        out_specs=pl.BlockSpec(memory_space=pltpu.VMEM),
        scratch_shapes=[
            pltpu.VMEM((HALF, 128), bf),
            pltpu.VMEM((HALF, 128), bf),
            pltpu.VMEM((HALF, 128), f32),
            pltpu.VMEM((HALF, 128), bf),
            pltpu.VMEM((2, 3, CHUNK, 128), bf),
            pltpu.VMEM((2, CHUNK, 128), f32),
            pltpu.VMEM((2, CHUNK, 128), bf),
            pltpu.VMEM((2, 3, SUB, 128), bf),
            pltpu.VMEM((2, SUB, 128), f32),
            pltpu.VMEM((2, LEAF, 128), bf),
            pltpu.VMEM((2, LEAF, 128), bf),
            pltpu.VMEM((ROWS, 128), bf),
        ]
        + [pltpu.SemaphoreType.DMA(n) for n in ((2,), (2,), (3, 6), (3, 6), (3, 6), (3, 6), (3,), (3,))],
        compiler_params=pltpu.CompilerParams(collective_id=0, has_side_effects=True, vmem_limit_bytes=48 * 2**20),
    )(values)


def on_device(counts, *args):
    logits, features, grads = run_net(counts, *args)
    grads = unlaid(all_sum(grads))
    return (logits[:2].reshape(2, 32, 128), features.reshape(64, 32, 128)) + grads


def solution(mesh):
    counts = (mesh.shape["row"], mesh.shape["col"])
    cells = P(None, ("batch", "row"), "col")
    in_specs = (P(("batch", "row"), "col"),) + (P(),) * 7 + (cells,)
    out_specs = (cells, cells, P("batch", None)) + (P("batch", None, None, None),) * 5 + (P("batch", None),)
    return jax.shard_map(
        functools.partial(on_device, counts), mesh=mesh, in_specs=in_specs, out_specs=out_specs, check_vma=False
    )
```

```python
import functools

import jax
import jax.numpy as jnp
import numpy as np
from jax import lax
from jax.experimental import pallas as pl
from jax.experimental.pallas import tpu as pltpu
from jax.sharding import PartitionSpec as P

BF, F32 = jnp.bfloat16, jnp.float32
MESH = pl.DeviceIdType.MESH

DEEP, WIDE = 8, 32
CELLS = DEEP * WIDE

ROWS = 6144
PARTS = ((0, 2048, "row"), (2048, 3072, "col"), (5120, 1024, "row"))
AT_RETURN, AT_FINAL, AT_BOTTOM, AT_SECOND, AT_FIRST, AT_READ = 0, 2304, 2880, 5184, 5760, 6080


def ranged(values, start, size):
    return values.at[pl.ds(pl.multiple_of(start, 16), size), :]


def bounds(p):
    side = max(DEEP * p, 16)
    left = 2 * WIDE * p
    return WIDE * p, left, left + side, left + 2 * side


def shift_table():
    table = {}
    for dr in (-1, 0, 1):
        for dc in (-1, 0, 1):
            m = np.zeros((CELLS, CELLS), np.float32)
            for r in range(DEEP):
                for q in range(WIDE):
                    if 0 <= r + dr < DEEP and 0 <= q + dc < WIDE:
                        m[(r + dr) * WIDE + q + dc, r * WIDE + q] = 1
            table[dr, dc] = m
    return table


def pick_table():
    m = np.zeros((112, CELLS), np.float32)
    for q in range(WIDE):
        m[q, q] = 1
        m[32 + q, (DEEP - 1) * WIDE + q] = 1
    for r in range(DEEP):
        m[64 + r, r * WIDE] = 1
        m[80 + r, r * WIDE + WIDE - 1] = 1
    for k, cell in enumerate((0, WIDE - 1, CELLS - WIDE, CELLS - 1)):
        m[96 + k, cell] = 1
    return m


CORNERS = {(-1, -1): 3, (-1, 1): 2, (1, -1): 1, (1, 1): 0}


def halo_tables():
    blocks, where = [], {}
    for p in (4, 2, 1):
        for ea in range(p + 2):
            for eb in range(p + 2):
                dr, dc = (ea > p) - (ea < 1), (eb > p) - (eb < 1)
                if (dr, dc) == (0, 0):
                    continue
                sa, sb = (ea - 1) % p, (eb - 1) % p
                down, left, right, corner = bounds(p)
                m = np.zeros((384, CELLS), np.float32)
                for r in range(DEEP):
                    for q in range(WIDE):
                        rr, qq = r + dr, q + dc
                        row_in, col_in = 0 <= rr < DEEP, 0 <= qq < WIDE
                        if row_in and col_in:
                            continue
                        if col_in:
                            spot = (0 if rr < 0 else down) + sb * WIDE + qq
                        elif row_in:
                            spot = (left if qq < 0 else right) + sa * DEEP + rr
                        else:
                            spot = corner + CORNERS[dr, dc]
                        m[spot, r * WIDE + q] = 1
                used = []
                for tile in range(3):
                    block = m[tile * 128 : (tile + 1) * 128]
                    if block.any():
                        used.append((tile, len(blocks)))
                        blocks.append(block)
                where[p, ea, eb] = used
    return np.concatenate(blocks), where


def spread_table():
    m = np.zeros((512, 512), np.float32)
    for r in range(4):
        for w in range(128):
            m[r * 128 + w, (w % 4) * 128 + r * WIDE + w // 4] = 1
    return m


SHIFTS = shift_table()
SHIFT_AT = {key: n for n, key in enumerate(SHIFTS)}
SHIFT_ALL = np.concatenate(list(SHIFTS.values()))
PICK = pick_table()
HALO_ALL, HALO_AT = halo_tables()
SPREAD = spread_table()

EYE = SHIFT_AT[0, 0] * CELLS

UNDER = (((0,), (1, 2)), ((0, 1), (2,)))
OVER = ((2,), (1, 2), (0, 1), (0,))
BASE = (0, 1, 1, 2)


def mm(a, b):
    return jnp.dot(a, b, preferred_element_type=F32)


def nt(a, b):
    return lax.dot_general(a, b, (((1,), (1,)), ((), ())), preferred_element_type=F32)


def logistic(z):
    return 0.5 + 0.5 * jnp.tanh(0.5 * z)


def activated(v):
    stored = v.astype(BF)
    z = stored.astype(F32)
    return stored, (z * logistic(z)).astype(BF)


def sloped(incoming, stored):
    z = stored.astype(F32)
    s = logistic(z)
    return (incoming * (s * (1.0 + z * (1.0 - s)))).astype(BF)


def remote(src, dst, send, recv, target):
    return pltpu.make_async_remote_copy(
        src_ref=src, dst_ref=dst, send_sem=send, recv_sem=recv, device_id=target, device_id_type=MESH
    )


SIDES = ((-1, 0), (1, 0), (0, -1), (0, 1), (-1, -1), (-1, 1), (1, -1), (1, 1))


def net_kernel(counts, *refs):
    it = iter(refs)

    def take(n):
        return [next(it) for _ in range(n)]

    syn, embt, k1, k2t, k3, k4, k5, rdo, cot, cS, cQ, cT, cU = take(13)
    logits_ref, features_ref, grads_ref = take(3)
    xb, e0, z0, z1, f1, e1, z2, f2, e2, z3, e3, z4, e4, z5, f5, t5, t4, t3, t2, t1, fg, cp = take(22)
    w0, w1, w1b, w2, w2b, w3, w3b, w4, w4b, w5, w5b, r4, r4t = take(13)
    halos = [take(2) for _ in range(10)]
    sends, recvs = take(2)
    g_ref, whole, tall = take(3)
    stages = [take(5) for _ in PARTS]
    sum_sends, sum_recvs = take(2)

    n_row, n_col = counts
    row, col = lax.axis_index("row"), lax.axis_index("col")
    there = {
        (-1, 0): row > 0,
        (1, 0): row < n_row - 1,
        (0, -1): col > 0,
        (0, 1): col < n_col - 1,
    }
    for dr in (-1, 1):
        for dc in (-1, 1):
            there[dr, dc] = jnp.logical_and(there[dr, 0], there[0, dc])

    def place(dr, dc):
        return {"row": (row + dr + n_row) % n_row, "col": (col + dc + n_col) % n_col}

    partners = [(d, 0) for d in range(1, n_row)] + [(0, d) for d in range(1, n_col)] + list(SIDES[4:])
    barrier = pltpu.get_barrier_semaphore()
    for partner in partners:
        pl.semaphore_signal(barrier, inc=1, device_id=place(*partner), device_id_type=MESH)

    def shift(dr, dc):
        n = SHIFT_AT[dr, dc]
        return cS[n * CELLS : (n + 1) * CELLS, :]

    lane = lax.broadcasted_iota(jnp.int32, (1, 128), 1)
    sixteen = lax.broadcasted_iota(jnp.int32, (16, 1), 0)

    def begin(n, p, width, ref, ahead=None):
        out, into = halos[n]
        down, left, right, corner = bounds(p)
        picked = {}
        for a in range(p):
            for b in range(p):
                if a in (0, p - 1) or b in (0, p - 1):
                    start = ((a + 1) * (p + 2) + b + 1) * width
                    picked[a, b] = nt(cQ[...], ref[start : start + width, :])
        for b in range(p):
            out[b * WIDE : (b + 1) * WIDE, 0:width] = picked[0, b][0:32].astype(BF)
            out[down + b * WIDE : down + (b + 1) * WIDE, 0:width] = picked[p - 1, b][32:64].astype(BF)
        for base, at, b in ((left, 64, 0), (right, 80, p - 1)):
            if p == 1:
                out[base : base + 16, 0:width] = picked[0, 0][at : at + 16].astype(BF)
            else:
                side = jnp.concatenate([picked[a, b][at : at + 8] for a in range(p)], axis=0)
                out[base : base + DEEP * p, 0:width] = side.astype(BF)
        ends = 0.0
        for k, spot in enumerate(((0, 0), (0, p - 1), (p - 1, 0), (p - 1, p - 1))):
            ends = ends + jnp.where(sixteen == k, picked[spot][96:112], 0.0)
        out[corner : corner + 16, 0:width] = ends.astype(BF)

        size = {(-1, 0): (0, down, down), (1, 0): (down, left, 0), (0, -1): (left, right, right), (0, 1): (right, corner, left)}
        copies = []
        for k, (dr, dc) in enumerate(SIDES):
            if (dr, dc) in size:
                start, stop, target = size[dr, dc]
            else:
                start, stop = corner, corner + 16
                target = corner + 16 * (1 + CORNERS[-dr, -dc])
            copies.append(
                remote(out.at[start:stop], into.at[target : target + stop - start], sends.at[n, k], recvs.at[n, k], place(dr, dc))
            )
        if ahead is not None:
            ahead()
        for copy in copies:
            copy.start()
        return copies

    def end(n, p, width, ref, copies):
        into = halos[n][1]
        down, left, right, corner = bounds(p)
        for copy in copies:
            copy.wait()
        ends = 0.0
        for side, k in CORNERS.items():
            tile = into[corner + 16 * (k + 1) : corner + 16 * (k + 2), 0:width].astype(F32)
            ends = ends + jnp.where(jnp.logical_and(sixteen == k, there[side]), tile, 0.0)
        into[corner : corner + 16, 0:width] = ends.astype(BF)
        tiles = []
        for tile in range(-(-(corner + 16) // 128)):
            at = lane + tile * 128
            keep = jnp.logical_and(at >= corner, at < corner + 16)
            for low, high, side in ((0, down, (-1, 0)), (down, left, (1, 0)), (left, right, (0, -1)), (right, corner, (0, 1))):
                keep = jnp.logical_or(keep, jnp.logical_and(jnp.logical_and(at >= low, at < high), there[side]))
            turned = nt(cS[EYE : EYE + width, 0:width], into[tile * 128 : (tile + 1) * 128, 0:width])
            tiles.append(jnp.where(keep, turned, 0.0).astype(BF))
        for ea in range(p + 2):
            for eb in range(p + 2):
                dr, dc = (ea > p) - (ea < 1), (eb > p) - (eb < 1)
                if (dr, dc) == (0, 0):
                    continue
                start = (((ea - 1) % p + 1) * (p + 2) + (eb - 1) % p + 1) * width
                moved = mm(ref[start : start + width, :], shift(dr, dc))
                for tile, block in HALO_AT[p, ea, eb]:
                    moved = moved + mm(tiles[tile], cT[block * 128 : (block + 1) * 128, :])
                start = (ea * (p + 2) + eb) * width
                ref[start : start + width, :] = moved.astype(BF)

    ways = {"row": (row, n_row, lambda d: place(d, 0)), "col": (col, n_col, lambda d: place(0, d))}
    flying = {}

    def sum_step(part, step):
        start, size, first = PARTS[part]
        s1, r1, h1, s2, r2 = stages[part]
        me1, n1, to1 = ways[first]
        me2, n2, to2 = ways["col" if first == "row" else "row"]
        c1, c2 = size // n1, size // n1 // n2
        for copy in flying.pop(part, ()):
            copy.wait()
        if step == 4:
            return
        if step == 0:
            s1[...] = g_ref[start : start + size, :].astype(BF)
        elif step == 1:
            total = g_ref[pl.ds(pl.multiple_of(start + me1 * c1, 16), c1), :]
            for d in range(n1 - 1):
                total = total + r1[d].astype(F32)
            h1[...] = total
            s2[...] = total.astype(BF)
        elif step == 2:
            total = h1[pl.ds(pl.multiple_of(me2 * c2, 16), c2), :]
            for d in range(n2 - 1):
                total = total + r2[d].astype(F32)
            whole[pl.ds(pl.multiple_of(start + me1 * c1 + me2 * c2, 16), c2), :] = total.astype(BF)
        copies = []
        for d in range(1, n1 if step in (0, 3) else n2):
            if step == 0:
                src, dst, to = ranged(s1, (me1 + d) % n1 * c1, c1), r1.at[d - 1], to1
            elif step == 1:
                src, dst, to = ranged(s2, (me2 + d) % n2 * c2, c2), r2.at[d - 1], to2
            elif step == 2:
                src = dst = ranged(whole, start + me1 * c1 + me2 * c2, c2)
                to = to2
            else:
                src = dst = ranged(whole, start + me1 * c1, c1)
                to = to1
            copies.append(remote(src, dst, sum_sends.at[part, step, d], sum_recvs.at[part, step, d], to(d)))
        for copy in copies:
            copy.start()
        flying[part] = copies

    bit = lax.broadcasted_iota(jnp.int32, (16, 1), 0)
    groups = []
    for a in range(4):
        for t in range(2):
            line = [(syn[16 * t + 4 * r + a : 16 * t + 4 * r + a + 1, :] >> bit) & 1 for r in range(4)]
            groups.append(jnp.concatenate(line, axis=1))
    bits = jnp.concatenate(groups, axis=0).astype(F32).astype(BF)
    phased = mm(bits, cU[...]).astype(BF)
    for a in range(4):
        for t in range(2):
            for b in range(4):
                start = ((a + 1) * 6 + b + 1) * 16
                xb[start : start + 16, t * 128 : (t + 1) * 128] = phased[(a * 2 + t) * 16 : (a * 2 + t + 1) * 16, b * 128 : (b + 1) * 128]
    copies = begin(0, 4, 16, xb, lambda: pl.semaphore_wait(barrier, len(partners)))

    eye = shift(0, 0)

    def beside(blocks, i, blank):
        return jnp.concatenate(blocks + [blank] if i == 0 else [blank] + blocks, axis=0)

    def added(k, rows, cols):
        return sum(k[ta, tb].astype(F32) for ta in rows for tb in cols).astype(BF)

    def arrange_first():
        repeat = (lax.broadcasted_iota(jnp.int32, (16, 96), 1) % 16 == lax.broadcasted_iota(jnp.int32, (16, 96), 0)).astype(F32).astype(BF)
        tiled = mm(nt(eye[:64, :64], embt[...]).astype(BF), repeat)
        own = lax.broadcasted_iota(jnp.int32, (64, 96), 1) // 16
        for j in range(6):
            w0[j * 64 : (j + 1) * 64, :] = jnp.where(own == j, tiled, 0.0).astype(BF)
        for ta in range(3):
            for i in range(2):
                w1[i * 64 : (i + 1) * 64, ta * 256 : (ta + 1) * 256] = sum(
                    mm(k1[ta, tb], eye[(tb + i) * 64 : (tb + i + 1) * 64, :]) for tb in range(3)
                ).astype(BF)

    def arrange_second():
        blank, empty = jnp.zeros((64, 128), BF), jnp.zeros((64, 64), BF)
        for ta in range(3):
            for i in range(2):
                line = beside([k2t[ta, tb] for tb in range(3)], i, blank)
                w2[i * 128 : (i + 1) * 128, ta * 256 : (ta + 1) * 256] = nt(eye[:128, :128], line).astype(BF)
                for tb in range(3):
                    w2b[i * 64 : (i + 1) * 64, ta * 512 + (tb + i) * 128 : ta * 512 + (tb + i + 1) * 128] = k2t[2 - ta, 2 - tb]
                hole = ta * 512 + (384 if i == 0 else 0)
                w2b[i * 64 : (i + 1) * 64, hole : hole + 128] = blank
                line = beside([k1[2 - ta, 2 - tb] for tb in range(3)], i, empty)
                w1b[i * 64 : (i + 1) * 64, ta * 256 : (ta + 1) * 256] = nt(eye[:64, :64], line).astype(BF)

    def arrange_bottom():
        for t in range(9):
            w3[:, t * 128 : (t + 1) * 128] = k3[t // 3, t % 3]
            w3b[:, t * 256 : (t + 1) * 256] = nt(eye[:128, :128], k3[2 - t // 3, 2 - t % 3]).astype(BF)

    def arrange_return():
        for pa in range(2):
            for pb in range(2):
                for s in range(2):
                    for u in range(2):
                        block = added(k4, UNDER[pa][s], UNDER[pb][u])
                        w4[(pa * 2 + pb) * 128 : (pa * 2 + pb + 1) * 128, (s * 2 + u) * 256 : (s * 2 + u + 1) * 256] = block
                        at = OVER.index(UNDER[pa][s]) * 4 + OVER.index(UNDER[pb][u])
                        w4b[:, at * 128 : (at + 1) * 128] = nt(eye, block).astype(BF)

    def arrange_final():
        for pa in range(2):
            for pb in range(2):
                for s in range(2):
                    for u in range(2):
                        start = pa * 128 + (1 - pb) * 64
                        w5[start : start + 64, (s * 2 + u) * 128 : (s * 2 + u + 1) * 128] = added(k5, UNDER[pa][s], UNDER[pb][u])
        for ea in range(4):
            for pair in range(2):
                stack = jnp.concatenate([added(k5, OVER[ea], OVER[2 * pair + i]) for i in range(2)], axis=0)
                at = ea * 2 + pair
                w5b[:, at * 128 : (at + 1) * 128] = nt(eye[:128, :128], stack).astype(BF)

    def arrange_readout():
        repeat = (lax.broadcasted_iota(jnp.int32, (64, 256), 1) % 64 == lax.broadcasted_iota(jnp.int32, (64, 256), 0)).astype(F32).astype(BF)
        tiled = mm(rdo[...], repeat)
        tiled = jnp.concatenate([tiled, jnp.zeros((2, 256), F32)] * 4, axis=0)
        own = lax.broadcasted_iota(jnp.int32, (16, 256), 1) // 64 == lax.broadcasted_iota(jnp.int32, (16, 256), 0) // 4
        r4[...] = jnp.where(own, tiled, 0.0).astype(BF)
        r4t[...] = nt(eye, r4[...]).astype(BF)

        wide = cot[...].astype(F32)
        groups = []
        for a in range(4):
            for t in range(2):
                line = jnp.concatenate([wide[:, 16 * t + 4 * r + a, :] for r in range(4)], axis=1)
                groups.append(jnp.concatenate([line, jnp.zeros((6, 512), F32)], axis=0))
        phased = mm(jnp.concatenate(groups, axis=0).astype(BF), cU[...])
        for a in range(4):
            for t in range(2):
                start = (a * 2 + t) * 8
                pieces = [phased[start : start + 4, b * 128 : (b + 1) * 128] for b in range(4)]
                cp[a * 16 : (a + 1) * 16, t * 128 : (t + 1) * 128] = jnp.concatenate(pieces, axis=0).astype(BF)

    arrange_first()
    arrange_readout()
    end(0, 4, 16, xb, copies)

    for ea in range(6):
        stored, active = activated(mm(w0[...], xb[ea * 96 : (ea + 1) * 96, :]))
        e0[ea * 384 : (ea + 1) * 384, :] = active
        if 1 <= ea <= 4:
            z0[(ea - 1) * 256 : ea * 256, :] = stored[64:320, :]

    for a in range(4):
        for pair in range(2):
            v = sum(
                mm(w1[:, ta * 256 : (ta + 1) * 256], e0[((a + ta) * 6 + 2 * pair) * 64 : ((a + ta) * 6 + 2 * pair + 4) * 64, :])
                for ta in range(3)
            )
            start = (a * 4 + 2 * pair) * 64
            z1[start : start + 128, :], f1[start : start + 128, :] = activated(v)

    def pooled(ref, side, width, a, b):
        spots = [((2 * a + i) * side + 2 * b + j) * width for i in range(2) for j in range(2)]
        return (sum(ref[s : s + width, :].astype(F32) for s in spots) * 0.25).astype(BF)

    for a in range(2):
        for b in range(2):
            start = ((a + 1) * 4 + b + 1) * 64
            e1[start : start + 64, :] = pooled(f1, 4, 64, a, b)
    copies = begin(1, 2, 64, e1)
    arrange_second()
    end(1, 2, 64, e1, copies)

    for a in range(2):
        v = sum(mm(w2[:, ta * 256 : (ta + 1) * 256], e1[(a + ta) * 256 : (a + ta + 1) * 256, :]) for ta in range(3))
        z2[a * 256 : (a + 1) * 256, :], f2[a * 256 : (a + 1) * 256, :] = activated(v)
    e2[4 * 128 : 5 * 128, :] = pooled(f2, 2, 128, 0, 0)
    copies = begin(2, 1, 128, e2)
    arrange_bottom()
    end(2, 1, 128, e2, copies)

    z3[...], e3[4 * 256 : 5 * 256, :] = activated(mm(w3[...], e2[...]))
    copies = begin(3, 1, 256, e3)
    arrange_return()
    end(3, 1, 256, e3, copies)

    for a in range(2):
        for b in range(2):
            n = a * 2 + b
            v = sum(
                mm(w4[n * 128 : (n + 1) * 128, s * 512 : (s + 1) * 512], e3[((a + s) * 3 + b) * 256 : ((a + s) * 3 + b + 2) * 256, :])
                for s in range(2)
            )
            v = v + f2[n * 128 : (n + 1) * 128, :].astype(F32)
            start = ((a + 1) * 4 + b + 1) * 128
            z4[n * 128 : (n + 1) * 128, :], e4[start : start + 128, :] = activated(v)
    copies = begin(4, 2, 128, e4)
    arrange_final()
    end(4, 2, 128, e4, copies)

    RUNS = ((0, 1, 64, 64), (1, 2, 0, 128), (3, 1, 0, 64))
    for a in range(4):
        for b, many, first, size in RUNS:
            base = (a % 2) * 128 + first
            v = sum(
                mm(w5[base : base + size, s * 256 : (s + 1) * 256], e4[((BASE[a] + s) * 4 + BASE[b]) * 128 : ((BASE[a] + s) * 4 + BASE[b] + 2) * 128, :])
                for s in range(2)
            )
            start = (a * 4 + b) * 64
            v = v + f1[start : start + size, :].astype(F32)
            z5[start : start + size, :], f5[start : start + size, :] = activated(v)

    for a in range(4):
        back = mm(r4t[...], cp[a * 16 : (a + 1) * 16, :])
        start = ((a + 1) * 6 + 1) * 64
        t5[start : start + 256, :] = sloped(back, z5[a * 256 : (a + 1) * 256, :])
    copies = begin(5, 4, 64, t5)

    groups = []
    total = jnp.zeros((16, 256), F32)
    for a in range(4):
        here = f5[a * 256 : (a + 1) * 256, :]
        value = mm(r4[...], here)
        total = total + nt(cp[a * 16 : (a + 1) * 16, :], here)
        for t in range(2):
            groups.append(jnp.concatenate([value[b * 4 : (b + 1) * 4, t * 128 : (t + 1) * 128] for b in range(4)], axis=1))
    value = jnp.concatenate(groups, axis=0)
    laid = 0.0
    for _ in range(3):
        piece = value.astype(BF)
        laid = laid + nt(piece, cU[...])
        value = value - piece.astype(F32)
    for a in range(4):
        for t in range(2):
            for r in range(4):
                h = 16 * t + 4 * r + a
                logits_ref[:, h : h + 1, :] = laid[(a * 2 + t) * 4 : (a * 2 + t) * 4 + 2, r * 128 : (r + 1) * 128].reshape(2, 1, 128)
    total = sum(total[b * 4 : (b + 1) * 4, b * 64 : (b + 1) * 64] for b in range(4))
    g_ref[AT_READ:ROWS, :] = jnp.zeros((ROWS - AT_READ, 128), F32)
    g_ref[AT_READ : AT_READ + 4, 0:64] = total

    sums = {}
    for a in range(4):
        for s in range(2):
            for b, many, first, size in RUNS:
                start = ((BASE[a] + s) * 4 + BASE[b]) * 128
                t_start = ((a + 1) * 6 + b + 1) * 64
                product = nt(t5[t_start : t_start + size, :], e4[start : start + 256, :])
                for m in range(many):
                    key = (a % 2, s, (b + m) % 2)
                    block = product[m * 64 : (m + 1) * 64, :]
                    sums[key] = sums[key] + block if key in sums else block

    def reads(parity, tap):
        return 0 if tap in UNDER[parity][0] else 1

    for ta in range(3):
        rowed = [sums[0, reads(0, ta), pb] + sums[1, reads(1, ta), pb] for pb in range(2)]
        for tb in range(3):
            value = sum(rowed[pb][:, reads(pb, tb) * 128 : (reads(pb, tb) + 1) * 128] for pb in range(2))
            start = AT_FINAL + (ta * 3 + tb) * 64
            g_ref[start : start + 64, :] = value

    end(5, 4, 64, t5, copies)
    for a in range(2):
        for b in range(2):
            v = sum(
                mm(w5b[:, m * 256 : (m + 1) * 256], t5[((2 * a + m) * 6 + 2 * b) * 64 : ((2 * a + m) * 6 + 2 * b + 4) * 64, :])
                for m in range(4)
            )
            start = ((a + 1) * 4 + b + 1) * 128
            n = a * 2 + b
            t4[start : start + 128, :] = sloped(v, z4[n * 128 : (n + 1) * 128, :])
    copies = begin(6, 2, 128, t4)

    for b in range(2):
        for u in range(2):
            parts = {}
            for a in range(2):
                for s in range(2):
                    start = ((a + 1) * 4 + b + 1) * 128
                    from_ = ((a + s) * 3 + b + u) * 256
                    parts[a, s] = nt(t4[start : start + 128, :], e3[from_ : from_ + 256, :])
            for ta in range(3):
                value = parts[0, reads(0, ta)] + parts[1, reads(1, ta)]
                for tb in UNDER[b][u]:
                    for half in range(2):
                        start = AT_RETURN + ((ta * 3 + tb) * 2 + half) * 128
                        piece = value[:, half * 128 : (half + 1) * 128]
                        g_ref[start : start + 128, :] = piece if b == 0 else g_ref[start : start + 128, :] + piece

    sum_step(0, 0)
    end(6, 2, 128, t4, copies)
    v = sum(mm(w4b[:, m * 512 : (m + 1) * 512], t4[m * 512 : (m + 1) * 512, :]) for m in range(4))
    t3[4 * 256 : 5 * 256, :] = sloped(v, z3[...])
    copies = begin(7, 1, 256, t3)
    for t in range(9):
        g_ref[AT_BOTTOM + t * 256 : AT_BOTTOM + (t + 1) * 256, :] = nt(t3[4 * 256 : 5 * 256, :], e2[t * 128 : (t + 1) * 128, :])
    sum_step(1, 0)
    end(7, 1, 256, t3, copies)

    through = mm(w3b[...], t3[...]) * 0.25
    for a in range(2):
        for b in range(2):
            n = a * 2 + b
            start = ((a + 1) * 4 + b + 1) * 128
            t2[start : start + 128, :] = sloped(t4[start : start + 128, :].astype(F32) + through, z2[n * 128 : (n + 1) * 128, :])
    copies = begin(8, 2, 128, t2)
    for ta in range(3):
        product = 0.0
        for a in range(2):
            start = ((a + 1) * 4 + 1) * 128
            product = product + nt(e1[(a + ta) * 256 : (a + ta + 1) * 256, :], t2[start : start + 256, :])
        g_ref[AT_SECOND + ta * 192 : AT_SECOND + (ta + 1) * 192, :] = product[0:192, 0:128] + product[64:256, 128:256]
    sum_step(0, 1)
    end(8, 2, 128, t2, copies)

    for a in range(2):
        v = sum(mm(w2b[:, ta * 512 : (ta + 1) * 512], t2[(a + ta) * 512 : (a + ta + 1) * 512, :]) for ta in range(3)) * 0.25
        for b in range(2):
            for i in range(2):
                for j in range(2):
                    fa, fb = 2 * a + i, 2 * b + j
                    start = ((fa + 1) * 6 + fb + 1) * 64
                    n = (fa * 4 + fb) * 64
                    t1[start : start + 64, :] = sloped(t5[start : start + 64, :].astype(F32) + v[b * 64 : (b + 1) * 64, :], z1[n : n + 64, :])
    copies = begin(9, 4, 64, t1)
    for ta in range(3):
        product = 0.0
        for a in range(4):
            for pair in range(2):
                start = ((a + 1) * 6 + 2 * pair + 1) * 64
                from_ = ((a + ta) * 6 + 2 * pair) * 64
                product = product + nt(t1[start : start + 128, :], e0[from_ : from_ + 256, :])
        value = product[0:64, 0:192] + product[64:128, 64:256]
        g_ref[AT_FIRST + ta * 64 : AT_FIRST + (ta + 1) * 64, :] = value[:, 0:128]
        start = AT_FIRST + (192 if ta < 2 else 256)
        g_ref[start : start + 64, ta % 2 * 64 : ta % 2 * 64 + 64] = value[:, 128:192]
    sum_step(1, 1)
    sum_step(0, 2)
    end(9, 4, 64, t1, copies)

    total = jnp.zeros((64, 256), F32)
    for a in range(4):
        for pair in range(2):
            v = sum(
                mm(w1b[:, ta * 256 : (ta + 1) * 256], t1[((a + ta) * 6 + 2 * pair) * 64 : ((a + ta) * 6 + 2 * pair + 4) * 64, :])
                for ta in range(3)
            )
            start = (a * 4 + 2 * pair) * 64
            fg[start : start + 128, :] = sloped(v, z0[start : start + 128, :])
        start = ((a + 1) * 6 + 1) * 16
        total = total + nt(xb[start : start + 64, :], fg[a * 256 : (a + 1) * 256, :])
    total = sum(total[b * 16 : (b + 1) * 16, b * 64 : (b + 1) * 64] for b in range(4))
    g_ref[AT_FIRST + 256 : AT_FIRST + 272, 64:128] = total
    g_ref[AT_FIRST + 272 : AT_FIRST + 320, 64:128] = jnp.zeros((48, 64), F32)

    def lay(a):
        for t in range(2):
            line = jnp.concatenate([fg[(a * 4 + b) * 64 : (a * 4 + b + 1) * 64, t * 128 : (t + 1) * 128] for b in range(4)], axis=1)
            laid = nt(line, cU[...])
            for r in range(4):
                tall[:, 16 * t + 4 * r + a, :] = laid[:, r * 128 : (r + 1) * 128]

    sum_step(2, 0)
    sum_step(0, 3)
    sum_step(1, 2)
    lay(0)
    lay(1)
    sum_step(2, 1)
    sum_step(1, 3)
    lay(2)
    lay(3)
    sum_step(2, 2)
    features_ref[...] = tall[...].astype(BF)
    sum_step(2, 3)
    for part in range(3):
        sum_step(part, 4)
    grads_ref[...] = whole[...]


LEVELS = ((4, 16), (2, 64), (1, 128), (1, 256), (2, 128), (4, 64), (2, 128), (1, 256), (2, 128), (4, 64))


def run_net(counts, *args):
    syn, emb, k1, k2, *rest = args
    args = (syn, emb.T, k1, k2.transpose(0, 1, 3, 2), *rest)
    tables = [jnp.asarray(t, BF) for t in (SHIFT_ALL, PICK, HALO_ALL, SPREAD)]
    blocks = [16 * 36, 64 * 36, 1024, 1024, 1024, 64 * 16, 512, 512, 128 * 9, 256, 256 * 9, 512, 128 * 16, 1024, 1024]
    blocks += [64 * 36, 128 * 16, 256 * 9, 128 * 16, 64 * 36, 1024, 64]
    weights = [(384, 96), (128, 768), (128, 768), (256, 768), (128, 1536), (256, 1152), (128, 2304), (512, 1024), (256, 2048), (256, 512), (128, 1024), (16, 256), (256, 16)]
    scratch = [pltpu.VMEM((n, CELLS), BF) for n in blocks] + [pltpu.VMEM(s, BF) for s in weights]
    for p, width in LEVELS:
        out = bounds(p)[3] + 16
        into = max(out + 64, -(-out // 128) * 128)
        scratch += [pltpu.VMEM((rows, max(width, 128)), BF) for rows in (out, into)]
    scratch += [pltpu.SemaphoreType.DMA((10, 8)), pltpu.SemaphoreType.DMA((10, 8))]
    scratch += [pltpu.VMEM((ROWS, 128), F32), pltpu.VMEM((ROWS, 128), BF), pltpu.VMEM((64, 32, 128), F32)]
    n_row, n_col = counts
    most = max(n_row, n_col)
    for _, size, first in PARTS:
        n1, n2 = (n_row, n_col) if first == "row" else (n_col, n_row)
        c1, c2 = size // n1, size // n1 // n2
        scratch += [
            pltpu.VMEM((size, 128), BF),
            pltpu.VMEM((n1 - 1, c1, 128), BF),
            pltpu.VMEM((c1, 128), F32),
            pltpu.VMEM((c1, 128), BF),
            pltpu.VMEM((n2 - 1, c2, 128), BF),
        ]
    scratch += [pltpu.SemaphoreType.DMA((len(PARTS), 4, most)), pltpu.SemaphoreType.DMA((len(PARTS), 4, most))]
    vmem = pl.BlockSpec(memory_space=pltpu.VMEM)
    return pl.pallas_call(
        functools.partial(net_kernel, counts),
        out_shape=(
            jax.ShapeDtypeStruct((2, 32, 128), F32),
            jax.ShapeDtypeStruct((64, 32, 128), BF),
            jax.ShapeDtypeStruct((ROWS, 128), BF),
        ),
        in_specs=[vmem] * 13,
        out_specs=(vmem, vmem, vmem),
        scratch_shapes=scratch,
        compiler_params=pltpu.CompilerParams(collective_id=1, has_side_effects=True, vmem_limit_bytes=56 * 2**20),
    )(*args, *tables)


def out_kernel(logits, features, g, o_logits, o_features, o_embed, o_first, o_second, o_bottom, o_return, o_final, o_read):
    o_logits[...] = logits[...]
    o_features[...] = features[...]
    for t in range(9):
        ta, tb = t // 3, t % 3
        for half in range(2):
            start = AT_RETURN + (t * 2 + half) * 128
            o_return[ta, tb, :, half * 128 : (half + 1) * 128] = g[start : start + 128, :].astype(F32)
        o_final[ta, tb] = g[AT_FINAL + t * 64 : AT_FINAL + (t + 1) * 64, :].astype(F32)
        o_bottom[ta, tb] = g[AT_BOTTOM + t * 256 : AT_BOTTOM + (t + 1) * 256, :].astype(F32)
        o_second[ta, tb] = g[AT_SECOND + t * 64 : AT_SECOND + (t + 1) * 64, :].astype(F32)
        start, low = (AT_FIRST + ta * 64, tb * 64) if tb < 2 else (AT_FIRST + (192 if ta < 2 else 256), ta % 2 * 64)
        o_first[ta, tb] = g[start : start + 64, low : low + 64].astype(F32)
    o_embed[...] = g[AT_FIRST + 256 : AT_FIRST + 272, 64:128].astype(F32)
    o_read[...] = g[AT_READ : AT_READ + 16, 0:64].astype(F32)[0:2]


def write_out(logits, features, g):
    shapes = [(2, 32, 128), (64, 32, 128), (16, 64), (3, 3, 64, 64), (3, 3, 64, 128), (3, 3, 256, 128), (3, 3, 128, 256), (3, 3, 64, 128), (2, 64)]
    vmem = pl.BlockSpec(memory_space=pltpu.VMEM)
    outs = pl.pallas_call(
        out_kernel,
        out_shape=tuple(jax.ShapeDtypeStruct(s, BF if n == 1 else F32) for n, s in enumerate(shapes)),
        in_specs=[vmem] * 3,
        out_specs=(vmem,) * 9,
        compiler_params=pltpu.CompilerParams(vmem_limit_bytes=32 * 2**20),
    )(logits, features, g)
    outs = list(outs)
    outs[2] = outs[2].T
    outs[4] = outs[4].transpose(0, 1, 3, 2)
    return tuple(outs)


def on_device(counts, *args):
    return write_out(*run_net(counts, *args))


def solution(mesh):
    counts = (mesh.shape["row"], mesh.shape["col"])
    cells = P(None, ("batch", "row"), "col")
    in_specs = (P(("batch", "row"), "col"),) + (P(),) * 7 + (cells,)
    out_specs = (cells, cells, P("batch", None)) + (P("batch", None, None, None),) * 5 + (P("batch", None),)
    return jax.shard_map(
        functools.partial(on_device, counts), mesh=mesh, in_specs=in_specs, out_specs=out_specs, check_vma=False
    )
```

```python
import functools

import jax
import jax.numpy as jnp
import numpy as np
from jax import lax
from jax.experimental import pallas as pl
from jax.experimental.pallas import tpu as pltpu
from jax.sharding import PartitionSpec as P

BF, F32 = jnp.bfloat16, jnp.float32
MESH = pl.DeviceIdType.MESH

DEEP, WIDE = 8, 32
CELLS = DEEP * WIDE

ROWS = 6144
PARTS = ((0, 1024, "row"), (1024, 1024, "col"), (2048, 1024, "row"), (3072, 2048, "col"), (5120, 1024, "row"))
AT_RETURN, AT_FINAL, AT_BOTTOM, AT_SECOND, AT_FIRST, AT_READ = 0, 2304, 2880, 5184, 5760, 6080


def ranged(values, start, size):
    return values.at[pl.ds(pl.multiple_of(start, 16), size), :]


def bounds(p):
    side = max(DEEP * p, 16)
    left = 2 * WIDE * p
    return WIDE * p, left, left + side, left + 2 * side


def shift_table():
    table = {}
    for dr in (-1, 0, 1):
        for dc in (-1, 0, 1):
            m = np.zeros((CELLS, CELLS), np.float32)
            for r in range(DEEP):
                for q in range(WIDE):
                    if 0 <= r + dr < DEEP and 0 <= q + dc < WIDE:
                        m[(r + dr) * WIDE + q + dc, r * WIDE + q] = 1
            table[dr, dc] = m
    return table


def pick_table():
    m = np.zeros((112, CELLS), np.float32)
    for q in range(WIDE):
        m[q, q] = 1
        m[32 + q, (DEEP - 1) * WIDE + q] = 1
    for r in range(DEEP):
        m[64 + r, r * WIDE] = 1
        m[80 + r, r * WIDE + WIDE - 1] = 1
    for k, cell in enumerate((0, WIDE - 1, CELLS - WIDE, CELLS - 1)):
        m[96 + k, cell] = 1
    return m


CORNERS = {(-1, -1): 3, (-1, 1): 2, (1, -1): 1, (1, 1): 0}


def halo_tables():
    blocks, where = [], {}
    for p in (4, 2, 1):
        for ea in range(p + 2):
            for eb in range(p + 2):
                dr, dc = (ea > p) - (ea < 1), (eb > p) - (eb < 1)
                if (dr, dc) == (0, 0):
                    continue
                sa, sb = (ea - 1) % p, (eb - 1) % p
                down, left, right, corner = bounds(p)
                m = np.zeros((384, CELLS), np.float32)
                for r in range(DEEP):
                    for q in range(WIDE):
                        rr, qq = r + dr, q + dc
                        row_in, col_in = 0 <= rr < DEEP, 0 <= qq < WIDE
                        if row_in and col_in:
                            continue
                        if col_in:
                            spot = (0 if rr < 0 else down) + sb * WIDE + qq
                        elif row_in:
                            spot = (left if qq < 0 else right) + sa * DEEP + rr
                        else:
                            spot = corner + CORNERS[dr, dc]
                        m[spot, r * WIDE + q] = 1
                used = []
                for tile in range(3):
                    block = m[tile * 128 : (tile + 1) * 128]
                    if block.any():
                        used.append((tile, len(blocks)))
                        blocks.append(block)
                where[p, ea, eb] = used
    return np.concatenate(blocks), where


def spread_table():
    m = np.zeros((512, 512), np.float32)
    for r in range(4):
        for w in range(128):
            m[r * 128 + w, (w % 4) * 128 + r * WIDE + w // 4] = 1
    return m


SHIFTS = shift_table()
SHIFT_AT = {key: n for n, key in enumerate(SHIFTS)}
SHIFT_ALL = np.concatenate(list(SHIFTS.values()))
PICK = pick_table()
HALO_ALL, HALO_AT = halo_tables()
SPREAD = spread_table()

EYE = SHIFT_AT[0, 0] * CELLS

UNDER = (((0,), (1, 2)), ((0, 1), (2,)))
OVER = ((2,), (1, 2), (0, 1), (0,))
BASE = (0, 1, 1, 2)


def mm(a, b):
    return jnp.dot(a, b, preferred_element_type=F32)


def nt(a, b):
    return lax.dot_general(a, b, (((1,), (1,)), ((), ())), preferred_element_type=F32)


def logistic(z):
    return 0.5 + 0.5 * jnp.tanh(0.5 * z)


def activated(v):
    stored = v.astype(BF)
    z = stored.astype(F32)
    return stored, (z * logistic(z)).astype(BF)


def sloped(incoming, stored):
    z = stored.astype(F32)
    s = logistic(z)
    return (incoming * (s * (1.0 + z * (1.0 - s)))).astype(BF)


def remote(src, dst, send, recv, target):
    return pltpu.make_async_remote_copy(
        src_ref=src, dst_ref=dst, send_sem=send, recv_sem=recv, device_id=target, device_id_type=MESH
    )


SIDES = ((-1, 0), (1, 0), (0, -1), (0, 1), (-1, -1), (-1, 1), (1, -1), (1, 1))


def net_kernel(counts, *refs):
    it = iter(refs)

    def take(n):
        return [next(it) for _ in range(n)]

    syn, embt, k1, k2t, k3, k4, k5, rdo, cot, cS, cQ, cT, cU = take(13)
    logits_ref, features_ref, embed_ref, grads_ref = take(4)
    xb, e0, z0, z1, f1, e1, z2, f2, e2, z3, e3, z4, e4, z5, f5, t5, t4, t3, t2, t1, fg, cp = take(22)
    w0, w1, w1b, w2, w2b, w3, w3b, w4, w4b, w5, w5b, r4, r4t = take(13)
    halos = [take(2) for _ in range(10)]
    sends, recvs = take(2)
    g_ref, whole, tall = take(3)
    stages = [take(5) for _ in PARTS]
    sum_sends, sum_recvs, embed_row, embed_col, embed_sends, embed_recvs = take(6)

    n_row, n_col = counts
    row, col = lax.axis_index("row"), lax.axis_index("col")
    there = {
        (-1, 0): row > 0,
        (1, 0): row < n_row - 1,
        (0, -1): col > 0,
        (0, 1): col < n_col - 1,
    }
    for dr in (-1, 1):
        for dc in (-1, 1):
            there[dr, dc] = jnp.logical_and(there[dr, 0], there[0, dc])

    def place(dr, dc):
        return {"row": (row + dr + n_row) % n_row, "col": (col + dc + n_col) % n_col}

    partners = [(d, 0) for d in range(1, n_row)] + [(0, d) for d in range(1, n_col)] + list(SIDES[4:])
    barrier = pltpu.get_barrier_semaphore()
    for partner in partners:
        pl.semaphore_signal(barrier, inc=1, device_id=place(*partner), device_id_type=MESH)

    def shift(dr, dc):
        n = SHIFT_AT[dr, dc]
        return cS[n * CELLS : (n + 1) * CELLS, :]

    lane = lax.broadcasted_iota(jnp.int32, (1, 128), 1)
    sixteen = lax.broadcasted_iota(jnp.int32, (16, 1), 0)

    def begin(n, p, width, ref, ahead=None):
        out, into = halos[n]
        down, left, right, corner = bounds(p)
        picked = {}
        for a in range(p):
            for b in range(p):
                if a in (0, p - 1) or b in (0, p - 1):
                    start = ((a + 1) * (p + 2) + b + 1) * width
                    picked[a, b] = nt(cQ[...], ref[start : start + width, :])
        for b in range(p):
            out[b * WIDE : (b + 1) * WIDE, 0:width] = picked[0, b][0:32].astype(BF)
            out[down + b * WIDE : down + (b + 1) * WIDE, 0:width] = picked[p - 1, b][32:64].astype(BF)
        for base, at, b in ((left, 64, 0), (right, 80, p - 1)):
            if p == 1:
                out[base : base + 16, 0:width] = picked[0, 0][at : at + 16].astype(BF)
            else:
                side = jnp.concatenate([picked[a, b][at : at + 8] for a in range(p)], axis=0)
                out[base : base + DEEP * p, 0:width] = side.astype(BF)
        ends = 0.0
        for k, spot in enumerate(((0, 0), (0, p - 1), (p - 1, 0), (p - 1, p - 1))):
            ends = ends + jnp.where(sixteen == k, picked[spot][96:112], 0.0)
        out[corner : corner + 16, 0:width] = ends.astype(BF)

        size = {(-1, 0): (0, down, down), (1, 0): (down, left, 0), (0, -1): (left, right, right), (0, 1): (right, corner, left)}
        copies = []
        for k, (dr, dc) in enumerate(SIDES):
            if (dr, dc) in size:
                start, stop, target = size[dr, dc]
            else:
                start, stop = corner, corner + 16
                target = corner + 16 * (1 + CORNERS[-dr, -dc])
            copies.append(
                remote(out.at[start:stop], into.at[target : target + stop - start], sends.at[n, k], recvs.at[n, k], place(dr, dc))
            )
        if ahead is not None:
            ahead()
        for copy in copies:
            copy.start()
        return copies

    def end(n, p, width, ref, copies):
        into = halos[n][1]
        down, left, right, corner = bounds(p)
        for copy in copies:
            copy.wait()
        ends = 0.0
        for side, k in CORNERS.items():
            tile = into[corner + 16 * (k + 1) : corner + 16 * (k + 2), 0:width].astype(F32)
            ends = ends + jnp.where(jnp.logical_and(sixteen == k, there[side]), tile, 0.0)
        into[corner : corner + 16, 0:width] = ends.astype(BF)
        tiles = []
        for tile in range(-(-(corner + 16) // 128)):
            at = lane + tile * 128
            keep = jnp.logical_and(at >= corner, at < corner + 16)
            for low, high, side in ((0, down, (-1, 0)), (down, left, (1, 0)), (left, right, (0, -1)), (right, corner, (0, 1))):
                keep = jnp.logical_or(keep, jnp.logical_and(jnp.logical_and(at >= low, at < high), there[side]))
            turned = nt(cS[EYE : EYE + width, 0:width], into[tile * 128 : (tile + 1) * 128, 0:width])
            tiles.append(jnp.where(keep, turned, 0.0).astype(BF))
        for ea in range(p + 2):
            for eb in range(p + 2):
                dr, dc = (ea > p) - (ea < 1), (eb > p) - (eb < 1)
                if (dr, dc) == (0, 0):
                    continue
                start = (((ea - 1) % p + 1) * (p + 2) + (eb - 1) % p + 1) * width
                moved = mm(ref[start : start + width, :], shift(dr, dc))
                for tile, block in HALO_AT[p, ea, eb]:
                    moved = moved + mm(tiles[tile], cT[block * 128 : (block + 1) * 128, :])
                start = (ea * (p + 2) + eb) * width
                ref[start : start + width, :] = moved.astype(BF)

    ways = {"row": (row, n_row, lambda d: place(d, 0)), "col": (col, n_col, lambda d: place(0, d))}
    flying = {}

    def sum_step(part, step):
        start, size, first = PARTS[part]
        s1, r1, h1, s2, r2 = stages[part]
        me1, n1, to1 = ways[first]
        me2, n2, to2 = ways["col" if first == "row" else "row"]
        c1, c2 = size // n1, size // n1 // n2
        for copy in flying.pop(part, ()):
            copy.wait()
        if step == 4:
            return
        if step == 0:
            s1[...] = g_ref[start : start + size, :].astype(BF)
        elif step == 1:
            total = g_ref[pl.ds(pl.multiple_of(start + me1 * c1, 16), c1), :]
            for d in range(n1 - 1):
                total = total + r1[d].astype(F32)
            h1[...] = total
            s2[...] = total.astype(BF)
        elif step == 2:
            total = h1[pl.ds(pl.multiple_of(me2 * c2, 16), c2), :]
            for d in range(n2 - 1):
                total = total + r2[d].astype(F32)
            whole[pl.ds(pl.multiple_of(start + me1 * c1 + me2 * c2, 16), c2), :] = total.astype(BF)
        copies = []
        for d in range(1, n1 if step in (0, 3) else n2):
            if step == 0:
                src, dst, to = ranged(s1, (me1 + d) % n1 * c1, c1), r1.at[d - 1], to1
            elif step == 1:
                src, dst, to = ranged(s2, (me2 + d) % n2 * c2, c2), r2.at[d - 1], to2
            elif step == 2:
                src = dst = ranged(whole, start + me1 * c1 + me2 * c2, c2)
                to = to2
            else:
                src = dst = ranged(whole, start + me1 * c1, c1)
                to = to1
            copies.append(remote(src, dst, sum_sends.at[part, step, d], sum_recvs.at[part, step, d], to(d)))
        for copy in copies:
            copy.start()
        flying[part] = copies

    def embed_step(step, value=None):
        if step > 0:
            for copy in flying.pop("embed"):
                copy.wait()
            slots = embed_row if step == 1 else embed_col
            value = sum(slots[d] for d in range(slots.shape[0]))
        if step == 2:
            return value
        slots, (me, count, to) = (embed_row, ways["row"]) if step == 0 else (embed_col, ways["col"])
        slots[me] = value
        copies = [
            remote(slots.at[me], slots.at[me], embed_sends.at[step, d], embed_recvs.at[step, d], to(d)) for d in range(1, count)
        ]
        for copy in copies:
            copy.start()
        flying["embed"] = copies

    bit = lax.broadcasted_iota(jnp.int32, (16, 1), 0)
    groups = []
    for a in range(4):
        for t in range(2):
            line = [(syn[16 * t + 4 * r + a : 16 * t + 4 * r + a + 1, :] >> bit) & 1 for r in range(4)]
            groups.append(jnp.concatenate(line, axis=1))
    bits = jnp.concatenate(groups, axis=0).astype(F32).astype(BF)
    phased = mm(bits, cU[...]).astype(BF)
    for a in range(4):
        for t in range(2):
            for b in range(4):
                start = ((a + 1) * 6 + b + 1) * 16
                xb[start : start + 16, t * 128 : (t + 1) * 128] = phased[(a * 2 + t) * 16 : (a * 2 + t + 1) * 16, b * 128 : (b + 1) * 128]
    copies = begin(0, 4, 16, xb, lambda: pl.semaphore_wait(barrier, len(partners)))

    eye = shift(0, 0)

    def beside(blocks, i, blank):
        return jnp.concatenate(blocks + [blank] if i == 0 else [blank] + blocks, axis=0)

    def added(k, rows, cols):
        return sum(k[ta, tb].astype(F32) for ta in rows for tb in cols).astype(BF)

    def arrange_first():
        repeat = (lax.broadcasted_iota(jnp.int32, (16, 96), 1) % 16 == lax.broadcasted_iota(jnp.int32, (16, 96), 0)).astype(F32).astype(BF)
        tiled = mm(nt(eye[:64, :64], embt[...]).astype(BF), repeat)
        own = lax.broadcasted_iota(jnp.int32, (64, 96), 1) // 16
        for j in range(6):
            w0[j * 64 : (j + 1) * 64, :] = jnp.where(own == j, tiled, 0.0).astype(BF)
        for ta in range(3):
            for i in range(2):
                w1[i * 64 : (i + 1) * 64, ta * 256 : (ta + 1) * 256] = sum(
                    mm(k1[ta, tb], eye[(tb + i) * 64 : (tb + i + 1) * 64, :]) for tb in range(3)
                ).astype(BF)

    def arrange_second():
        blank, empty = jnp.zeros((64, 128), BF), jnp.zeros((64, 64), BF)
        for ta in range(3):
            for i in range(2):
                line = beside([k2t[ta, tb] for tb in range(3)], i, blank)
                w2[i * 128 : (i + 1) * 128, ta * 256 : (ta + 1) * 256] = nt(eye[:128, :128], line).astype(BF)
                for tb in range(3):
                    w2b[i * 64 : (i + 1) * 64, ta * 512 + (tb + i) * 128 : ta * 512 + (tb + i + 1) * 128] = k2t[2 - ta, 2 - tb]
                hole = ta * 512 + (384 if i == 0 else 0)
                w2b[i * 64 : (i + 1) * 64, hole : hole + 128] = blank
                line = beside([k1[2 - ta, 2 - tb] for tb in range(3)], i, empty)
                w1b[i * 64 : (i + 1) * 64, ta * 256 : (ta + 1) * 256] = nt(eye[:64, :64], line).astype(BF)

    def arrange_bottom():
        for t in range(9):
            w3[:, t * 128 : (t + 1) * 128] = k3[t // 3, t % 3]
            w3b[:, t * 256 : (t + 1) * 256] = nt(eye[:128, :128], k3[2 - t // 3, 2 - t % 3]).astype(BF)

    def arrange_return():
        for pa in range(2):
            for pb in range(2):
                for s in range(2):
                    for u in range(2):
                        block = added(k4, UNDER[pa][s], UNDER[pb][u])
                        w4[(pa * 2 + pb) * 128 : (pa * 2 + pb + 1) * 128, (s * 2 + u) * 256 : (s * 2 + u + 1) * 256] = block
                        at = OVER.index(UNDER[pa][s]) * 4 + OVER.index(UNDER[pb][u])
                        w4b[:, at * 128 : (at + 1) * 128] = nt(eye, block).astype(BF)

    def arrange_final():
        for pa in range(2):
            for pb in range(2):
                for s in range(2):
                    for u in range(2):
                        start = pa * 128 + (1 - pb) * 64
                        w5[start : start + 64, (s * 2 + u) * 128 : (s * 2 + u + 1) * 128] = added(k5, UNDER[pa][s], UNDER[pb][u])
        for ea in range(4):
            for pair in range(2):
                stack = jnp.concatenate([added(k5, OVER[ea], OVER[2 * pair + i]) for i in range(2)], axis=0)
                at = ea * 2 + pair
                w5b[:, at * 128 : (at + 1) * 128] = nt(eye[:128, :128], stack).astype(BF)

    def arrange_readout():
        repeat = (lax.broadcasted_iota(jnp.int32, (64, 256), 1) % 64 == lax.broadcasted_iota(jnp.int32, (64, 256), 0)).astype(F32).astype(BF)
        tiled = mm(rdo[...], repeat)
        tiled = jnp.concatenate([tiled, jnp.zeros((2, 256), F32)] * 4, axis=0)
        own = lax.broadcasted_iota(jnp.int32, (16, 256), 1) // 64 == lax.broadcasted_iota(jnp.int32, (16, 256), 0) // 4
        r4[...] = jnp.where(own, tiled, 0.0).astype(BF)
        r4t[...] = nt(eye, r4[...]).astype(BF)

        wide = cot[...].astype(F32)
        groups = []
        for a in range(4):
            for t in range(2):
                line = jnp.concatenate([wide[:, 16 * t + 4 * r + a, :] for r in range(4)], axis=1)
                groups.append(jnp.concatenate([line, jnp.zeros((6, 512), F32)], axis=0))
        phased = mm(jnp.concatenate(groups, axis=0).astype(BF), cU[...])
        for a in range(4):
            for t in range(2):
                start = (a * 2 + t) * 8
                pieces = [phased[start : start + 4, b * 128 : (b + 1) * 128] for b in range(4)]
                cp[a * 16 : (a + 1) * 16, t * 128 : (t + 1) * 128] = jnp.concatenate(pieces, axis=0).astype(BF)

    arrange_first()
    arrange_readout()
    end(0, 4, 16, xb, copies)

    for ea in range(6):
        stored, active = activated(mm(w0[...], xb[ea * 96 : (ea + 1) * 96, :]))
        e0[ea * 384 : (ea + 1) * 384, :] = active
        if 1 <= ea <= 4:
            z0[(ea - 1) * 256 : ea * 256, :] = stored[64:320, :]

    for a in range(4):
        for pair in range(2):
            v = sum(
                mm(w1[:, ta * 256 : (ta + 1) * 256], e0[((a + ta) * 6 + 2 * pair) * 64 : ((a + ta) * 6 + 2 * pair + 4) * 64, :])
                for ta in range(3)
            )
            start = (a * 4 + 2 * pair) * 64
            z1[start : start + 128, :], f1[start : start + 128, :] = activated(v)

    def pooled(ref, side, width, a, b):
        spots = [((2 * a + i) * side + 2 * b + j) * width for i in range(2) for j in range(2)]
        return (sum(ref[s : s + width, :].astype(F32) for s in spots) * 0.25).astype(BF)

    for a in range(2):
        for b in range(2):
            start = ((a + 1) * 4 + b + 1) * 64
            e1[start : start + 64, :] = pooled(f1, 4, 64, a, b)
    copies = begin(1, 2, 64, e1)
    arrange_second()
    end(1, 2, 64, e1, copies)

    for a in range(2):
        v = sum(mm(w2[:, ta * 256 : (ta + 1) * 256], e1[(a + ta) * 256 : (a + ta + 1) * 256, :]) for ta in range(3))
        z2[a * 256 : (a + 1) * 256, :], f2[a * 256 : (a + 1) * 256, :] = activated(v)
    e2[4 * 128 : 5 * 128, :] = pooled(f2, 2, 128, 0, 0)
    copies = begin(2, 1, 128, e2)
    arrange_bottom()
    end(2, 1, 128, e2, copies)

    z3[...], e3[4 * 256 : 5 * 256, :] = activated(mm(w3[...], e2[...]))
    copies = begin(3, 1, 256, e3)
    arrange_return()
    end(3, 1, 256, e3, copies)

    for a in range(2):
        for b in range(2):
            n = a * 2 + b
            v = sum(
                mm(w4[n * 128 : (n + 1) * 128, s * 512 : (s + 1) * 512], e3[((a + s) * 3 + b) * 256 : ((a + s) * 3 + b + 2) * 256, :])
                for s in range(2)
            )
            v = v + f2[n * 128 : (n + 1) * 128, :].astype(F32)
            start = ((a + 1) * 4 + b + 1) * 128
            z4[n * 128 : (n + 1) * 128, :], e4[start : start + 128, :] = activated(v)
    copies = begin(4, 2, 128, e4)
    arrange_final()
    end(4, 2, 128, e4, copies)

    RUNS = ((0, 1, 64, 64), (1, 2, 0, 128), (3, 1, 0, 64))
    for a in range(4):
        for b, many, first, size in RUNS:
            base = (a % 2) * 128 + first
            v = sum(
                mm(w5[base : base + size, s * 256 : (s + 1) * 256], e4[((BASE[a] + s) * 4 + BASE[b]) * 128 : ((BASE[a] + s) * 4 + BASE[b] + 2) * 128, :])
                for s in range(2)
            )
            start = (a * 4 + b) * 64
            v = v + f1[start : start + size, :].astype(F32)
            z5[start : start + size, :], f5[start : start + size, :] = activated(v)

    for a in range(4):
        back = mm(r4t[...], cp[a * 16 : (a + 1) * 16, :])
        start = ((a + 1) * 6 + 1) * 64
        t5[start : start + 256, :] = sloped(back, z5[a * 256 : (a + 1) * 256, :])
    copies = begin(5, 4, 64, t5)

    groups = []
    total = jnp.zeros((16, 256), F32)
    for a in range(4):
        here = f5[a * 256 : (a + 1) * 256, :]
        value = mm(r4[...], here)
        total = total + nt(cp[a * 16 : (a + 1) * 16, :], here)
        for t in range(2):
            groups.append(jnp.concatenate([value[b * 4 : (b + 1) * 4, t * 128 : (t + 1) * 128] for b in range(4)], axis=1))
    value = jnp.concatenate(groups, axis=0)
    laid = 0.0
    for _ in range(3):
        piece = value.astype(BF)
        laid = laid + nt(piece, cU[...])
        value = value - piece.astype(F32)
    for a in range(4):
        for t in range(2):
            for r in range(4):
                h = 16 * t + 4 * r + a
                logits_ref[:, h : h + 1, :] = laid[(a * 2 + t) * 4 : (a * 2 + t) * 4 + 2, r * 128 : (r + 1) * 128].reshape(2, 1, 128)
    total = sum(total[b * 4 : (b + 1) * 4, b * 64 : (b + 1) * 64] for b in range(4))
    g_ref[AT_READ:ROWS, :] = jnp.zeros((ROWS - AT_READ, 128), F32)
    g_ref[AT_READ : AT_READ + 4, 0:64] = total

    sums = {}
    for a in range(4):
        for s in range(2):
            for b, many, first, size in RUNS:
                start = ((BASE[a] + s) * 4 + BASE[b]) * 128
                t_start = ((a + 1) * 6 + b + 1) * 64
                product = nt(t5[t_start : t_start + size, :], e4[start : start + 256, :])
                for m in range(many):
                    key = (a % 2, s, (b + m) % 2)
                    block = product[m * 64 : (m + 1) * 64, :]
                    sums[key] = sums[key] + block if key in sums else block

    def reads(parity, tap):
        return 0 if tap in UNDER[parity][0] else 1

    for ta in range(3):
        rowed = [sums[0, reads(0, ta), pb] + sums[1, reads(1, ta), pb] for pb in range(2)]
        for tb in range(3):
            value = sum(rowed[pb][:, reads(pb, tb) * 128 : (reads(pb, tb) + 1) * 128] for pb in range(2))
            start = AT_FINAL + (ta * 3 + tb) * 64
            g_ref[start : start + 64, :] = value

    end(5, 4, 64, t5, copies)
    for a in range(2):
        for b in range(2):
            v = sum(
                mm(w5b[:, m * 256 : (m + 1) * 256], t5[((2 * a + m) * 6 + 2 * b) * 64 : ((2 * a + m) * 6 + 2 * b + 4) * 64, :])
                for m in range(4)
            )
            start = ((a + 1) * 4 + b + 1) * 128
            n = a * 2 + b
            t4[start : start + 128, :] = sloped(v, z4[n * 128 : (n + 1) * 128, :])
    copies = begin(6, 2, 128, t4)

    for b in range(2):
        for u in range(2):
            parts = {}
            for a in range(2):
                for s in range(2):
                    start = ((a + 1) * 4 + b + 1) * 128
                    from_ = ((a + s) * 3 + b + u) * 256
                    parts[a, s] = nt(t4[start : start + 128, :], e3[from_ : from_ + 256, :])
            for ta in range(3):
                value = parts[0, reads(0, ta)] + parts[1, reads(1, ta)]
                for tb in UNDER[b][u]:
                    for half in range(2):
                        start = AT_RETURN + ((ta * 3 + tb) * 2 + half) * 128
                        piece = value[:, half * 128 : (half + 1) * 128]
                        g_ref[start : start + 128, :] = piece if b == 0 else g_ref[start : start + 128, :] + piece

    sum_step(0, 0)
    sum_step(1, 0)
    end(6, 2, 128, t4, copies)
    v = sum(mm(w4b[:, m * 512 : (m + 1) * 512], t4[m * 512 : (m + 1) * 512, :]) for m in range(4))
    t3[4 * 256 : 5 * 256, :] = sloped(v, z3[...])
    copies = begin(7, 1, 256, t3)
    for t in range(9):
        g_ref[AT_BOTTOM + t * 256 : AT_BOTTOM + (t + 1) * 256, :] = nt(t3[4 * 256 : 5 * 256, :], e2[t * 128 : (t + 1) * 128, :])
    sum_step(2, 0)
    sum_step(3, 0)
    end(7, 1, 256, t3, copies)

    through = mm(w3b[...], t3[...]) * 0.25
    for a in range(2):
        for b in range(2):
            n = a * 2 + b
            start = ((a + 1) * 4 + b + 1) * 128
            t2[start : start + 128, :] = sloped(t4[start : start + 128, :].astype(F32) + through, z2[n * 128 : (n + 1) * 128, :])
    copies = begin(8, 2, 128, t2)
    for ta in range(3):
        product = 0.0
        for a in range(2):
            start = ((a + 1) * 4 + 1) * 128
            product = product + nt(e1[(a + ta) * 256 : (a + ta + 1) * 256, :], t2[start : start + 256, :])
        g_ref[AT_SECOND + ta * 192 : AT_SECOND + (ta + 1) * 192, :] = product[0:192, 0:128] + product[64:256, 128:256]
    sum_step(0, 1)
    sum_step(1, 1)
    end(8, 2, 128, t2, copies)

    for a in range(2):
        v = sum(mm(w2b[:, ta * 512 : (ta + 1) * 512], t2[(a + ta) * 512 : (a + ta + 1) * 512, :]) for ta in range(3)) * 0.25
        for b in range(2):
            for i in range(2):
                for j in range(2):
                    fa, fb = 2 * a + i, 2 * b + j
                    start = ((fa + 1) * 6 + fb + 1) * 64
                    n = (fa * 4 + fb) * 64
                    t1[start : start + 64, :] = sloped(t5[start : start + 64, :].astype(F32) + v[b * 64 : (b + 1) * 64, :], z1[n : n + 64, :])
    copies = begin(9, 4, 64, t1)
    for ta in range(3):
        product = 0.0
        for a in range(4):
            for pair in range(2):
                start = ((a + 1) * 6 + 2 * pair + 1) * 64
                from_ = ((a + ta) * 6 + 2 * pair) * 64
                product = product + nt(t1[start : start + 128, :], e0[from_ : from_ + 256, :])
        value = product[0:64, 0:192] + product[64:128, 64:256]
        g_ref[AT_FIRST + ta * 64 : AT_FIRST + (ta + 1) * 64, :] = value[:, 0:128]
        start = AT_FIRST + (192 if ta < 2 else 256)
        g_ref[start : start + 64, ta % 2 * 64 : ta % 2 * 64 + 64] = value[:, 128:192]
    g_ref[AT_FIRST + 256 : AT_FIRST + 320, 64:128] = jnp.zeros((64, 64), F32)
    sum_step(4, 0)
    sum_step(2, 1)
    sum_step(3, 1)
    sum_step(0, 2)
    sum_step(1, 2)
    end(9, 4, 64, t1, copies)

    total = jnp.zeros((64, 256), F32)
    for a in range(4):
        for pair in range(2):
            v = sum(
                mm(w1b[:, ta * 256 : (ta + 1) * 256], t1[((a + ta) * 6 + 2 * pair) * 64 : ((a + ta) * 6 + 2 * pair + 4) * 64, :])
                for ta in range(3)
            )
            start = (a * 4 + 2 * pair) * 64
            fg[start : start + 128, :] = sloped(v, z0[start : start + 128, :])
        start = ((a + 1) * 6 + 1) * 16
        total = total + nt(xb[start : start + 64, :], fg[a * 256 : (a + 1) * 256, :])
    total = sum(total[b * 16 : (b + 1) * 16, b * 64 : (b + 1) * 64] for b in range(4))
    embed_step(0, total)

    def lay(a):
        for t in range(2):
            line = jnp.concatenate([fg[(a * 4 + b) * 64 : (a * 4 + b + 1) * 64, t * 128 : (t + 1) * 128] for b in range(4)], axis=1)
            laid = nt(line, cU[...])
            for r in range(4):
                tall[:, 16 * t + 4 * r + a, :] = laid[:, r * 128 : (r + 1) * 128]

    sum_step(4, 1)
    sum_step(2, 2)
    sum_step(3, 2)
    sum_step(0, 3)
    sum_step(1, 3)
    lay(0)
    lay(1)
    embed_step(1)
    sum_step(4, 2)
    sum_step(2, 3)
    sum_step(3, 3)
    lay(2)
    lay(3)
    features_ref[...] = tall[...].astype(BF)
    sum_step(4, 3)
    embed_ref[...] = embed_step(2)
    for part in range(len(PARTS)):
        sum_step(part, 4)
    grads_ref[...] = whole[...]


LEVELS = ((4, 16), (2, 64), (1, 128), (1, 256), (2, 128), (4, 64), (2, 128), (1, 256), (2, 128), (4, 64))


def run_net(counts, *args):
    syn, emb, k1, k2, *rest = args
    args = (syn, emb.T, k1, k2.transpose(0, 1, 3, 2), *rest)
    tables = [jnp.asarray(t, BF) for t in (SHIFT_ALL, PICK, HALO_ALL, SPREAD)]
    blocks = [16 * 36, 64 * 36, 1024, 1024, 1024, 64 * 16, 512, 512, 128 * 9, 256, 256 * 9, 512, 128 * 16, 1024, 1024]
    blocks += [64 * 36, 128 * 16, 256 * 9, 128 * 16, 64 * 36, 1024, 64]
    weights = [(384, 96), (128, 768), (128, 768), (256, 768), (128, 1536), (256, 1152), (128, 2304), (512, 1024), (256, 2048), (256, 512), (128, 1024), (16, 256), (256, 16)]
    scratch = [pltpu.VMEM((n, CELLS), BF) for n in blocks] + [pltpu.VMEM(s, BF) for s in weights]
    for p, width in LEVELS:
        out = bounds(p)[3] + 16
        into = max(out + 64, -(-out // 128) * 128)
        scratch += [pltpu.VMEM((rows, max(width, 128)), BF) for rows in (out, into)]
    scratch += [pltpu.SemaphoreType.DMA((10, 8)), pltpu.SemaphoreType.DMA((10, 8))]
    scratch += [pltpu.VMEM((ROWS, 128), F32), pltpu.VMEM((ROWS, 128), BF), pltpu.VMEM((64, 32, 128), F32)]
    n_row, n_col = counts
    most = max(n_row, n_col)
    for _, size, first in PARTS:
        n1, n2 = (n_row, n_col) if first == "row" else (n_col, n_row)
        c1, c2 = size // n1, size // n1 // n2
        scratch += [
            pltpu.VMEM((size, 128), BF),
            pltpu.VMEM((n1 - 1, c1, 128), BF),
            pltpu.VMEM((c1, 128), F32),
            pltpu.VMEM((c1, 128), BF),
            pltpu.VMEM((n2 - 1, c2, 128), BF),
        ]
    scratch += [pltpu.SemaphoreType.DMA((len(PARTS), 4, most)), pltpu.SemaphoreType.DMA((len(PARTS), 4, most))]
    scratch += [pltpu.VMEM((n_row, 16, 64), F32), pltpu.VMEM((n_col, 16, 64), F32)]
    scratch += [pltpu.SemaphoreType.DMA((2, most)), pltpu.SemaphoreType.DMA((2, most))]
    vmem = pl.BlockSpec(memory_space=pltpu.VMEM)
    return pl.pallas_call(
        functools.partial(net_kernel, counts),
        out_shape=(
            jax.ShapeDtypeStruct((2, 32, 128), F32),
            jax.ShapeDtypeStruct((64, 32, 128), BF),
            jax.ShapeDtypeStruct((16, 64), F32),
            jax.ShapeDtypeStruct((ROWS, 128), BF),
        ),
        in_specs=[vmem] * 13,
        out_specs=(vmem,) * 4,
        scratch_shapes=scratch,
        compiler_params=pltpu.CompilerParams(collective_id=1, has_side_effects=True, vmem_limit_bytes=56 * 2**20),
    )(*args, *tables)


def out_kernel(logits, features, embed, g, o_logits, o_features, o_embed, o_first, o_second, o_bottom, o_return, o_final, o_read):
    o_logits[...] = logits[...]
    o_features[...] = features[...]
    for t in range(9):
        ta, tb = t // 3, t % 3
        for half in range(2):
            start = AT_RETURN + (t * 2 + half) * 128
            o_return[ta, tb, :, half * 128 : (half + 1) * 128] = g[start : start + 128, :].astype(F32)
        o_final[ta, tb] = g[AT_FINAL + t * 64 : AT_FINAL + (t + 1) * 64, :].astype(F32)
        o_bottom[ta, tb] = g[AT_BOTTOM + t * 256 : AT_BOTTOM + (t + 1) * 256, :].astype(F32)
        o_second[ta, tb] = g[AT_SECOND + t * 64 : AT_SECOND + (t + 1) * 64, :].astype(F32)
        start, low = (AT_FIRST + ta * 64, tb * 64) if tb < 2 else (AT_FIRST + (192 if ta < 2 else 256), ta % 2 * 64)
        o_first[ta, tb] = g[start : start + 64, low : low + 64].astype(F32)
    o_embed[...] = embed[...]
    o_read[...] = g[AT_READ : AT_READ + 16, 0:64].astype(F32)[0:2]


def write_out(logits, features, embed, g):
    shapes = [(2, 32, 128), (64, 32, 128), (16, 64), (3, 3, 64, 64), (3, 3, 64, 128), (3, 3, 256, 128), (3, 3, 128, 256), (3, 3, 64, 128), (2, 64)]
    vmem = pl.BlockSpec(memory_space=pltpu.VMEM)
    outs = pl.pallas_call(
        out_kernel,
        out_shape=tuple(jax.ShapeDtypeStruct(s, BF if n == 1 else F32) for n, s in enumerate(shapes)),
        in_specs=[vmem] * 4,
        out_specs=(vmem,) * 9,
        compiler_params=pltpu.CompilerParams(vmem_limit_bytes=32 * 2**20),
    )(logits, features, embed, g)
    outs = list(outs)
    outs[2] = outs[2].T
    outs[4] = outs[4].transpose(0, 1, 3, 2)
    return tuple(outs)


def on_device(counts, *args):
    return write_out(*run_net(counts, *args))


def solution(mesh):
    counts = (mesh.shape["row"], mesh.shape["col"])
    cells = P(None, ("batch", "row"), "col")
    in_specs = (P(("batch", "row"), "col"),) + (P(),) * 7 + (cells,)
    out_specs = (cells, cells, P("batch", None)) + (P("batch", None, None, None),) * 5 + (P("batch", None),)
    return jax.shard_map(
        functools.partial(on_device, counts), mesh=mesh, in_specs=in_specs, out_specs=out_specs, check_vma=False
    )
```

```python
import functools

import jax
import jax.numpy as jnp
import numpy as np
from jax import lax
from jax.experimental import pallas as pl
from jax.experimental.pallas import tpu as pltpu
from jax.sharding import PartitionSpec as P

BF, F32 = jnp.bfloat16, jnp.float32
MESH = pl.DeviceIdType.MESH

DEEP, WIDE = 8, 32
CELLS = DEEP * WIDE
EXT = CELLS + 128

ROWS = 6144
PARTS = ((0, 1024, "row"), (1024, 1024, "col"), (2048, 1024, "row"), (3072, 2048, "col"), (5120, 1024, "row"))
AT_RETURN, AT_FINAL, AT_BOTTOM, AT_SECOND, AT_FIRST, AT_READ = 0, 2304, 2880, 5184, 5760, 6080


def ranged(values, start, size):
    return values.at[pl.ds(pl.multiple_of(start, 16), size), :]


def bounds(depth):
    left = 2 * WIDE * depth
    return WIDE * depth, left, left + 16, left + 32


def lane_of(r, q, depth):
    if not (-depth <= r < DEEP + depth and -depth <= q < WIDE + depth):
        return None
    row_in, col_in = 0 <= r < DEEP, 0 <= q < WIDE
    down, left, right, corner = bounds(depth)
    if row_in and col_in:
        return r * WIDE + q
    i = r + depth if r < 0 else r - DEEP
    j = q + depth if q < 0 else q - WIDE
    if col_in:
        return CELLS + (0 if r < 0 else down) + i * WIDE + q
    if row_in:
        return CELLS + (left if q < 0 else right) + j * DEEP + r
    return CELLS + corner + CORNERS[(-1 if r < 0 else 1, -1 if q < 0 else 1)] * depth * depth + i * depth + j


def shift_tables(depth, size):
    tables = []
    for dr in (-1, 0, 1):
        for dc in (-1, 0, 1):
            m = np.zeros((size, EXT), np.float32)
            for r in range(-1, DEEP + 1):
                for q in range(-1, WIDE + 1):
                    source = lane_of(r + dr, q + dc, depth)
                    if source is not None:
                        m[source, lane_of(r, q, 1)] = 1
            tables.append(m)
    return np.concatenate(tables)


def pick_table(depth):
    down, left, right, corner = bounds(depth)
    m = np.zeros((corner + 16, CELLS), np.float32)
    for i in range(depth):
        for q in range(WIDE):
            m[i * WIDE + q, i * WIDE + q] = 1
            m[down + i * WIDE + q, (DEEP - depth + i) * WIDE + q] = 1
        for r in range(DEEP):
            m[left + i * DEEP + r, r * WIDE + i] = 1
            m[right + i * DEEP + r, r * WIDE + WIDE - depth + i] = 1
        for j in range(depth):
            for k, (r, q) in enumerate(((0, 0), (0, WIDE - depth), (DEEP - depth, 0), (DEEP - depth, WIDE - depth))):
                m[corner + k * depth * depth + i * depth + j, (r + i) * WIDE + q + j] = 1
    return m


CORNERS = {(-1, -1): 3, (-1, 1): 2, (1, -1): 1, (1, 1): 0}


def spread_table():
    m = np.zeros((512, 512), np.float32)
    for r in range(4):
        for w in range(128):
            m[r * 128 + w, (w % 4) * 128 + r * WIDE + w // 4] = 1
    return m


SHIFT = shift_tables(1, EXT)
SHIFT_FAR = shift_tables(2, 512)
PICK, PICK_FAR = pick_table(1), pick_table(2)
SPREAD = spread_table()

UNDER = (((0,), (1, 2)), ((0, 1), (2,)))
OVER = ((2,), (1, 2), (0, 1), (0,))
BASE = (0, 1, 1, 2)


def mm(a, b):
    return jnp.dot(a, b, preferred_element_type=F32)


def nt(a, b):
    return lax.dot_general(a, b, (((1,), (1,)), ((), ())), preferred_element_type=F32)


def logistic(z):
    return 0.5 + 0.5 * jnp.tanh(0.5 * z)


def activated(v):
    stored = v.astype(BF)
    z = stored.astype(F32)
    return stored, (z * logistic(z)).astype(BF)


def sloped(incoming, stored):
    z = stored.astype(F32)
    s = logistic(z)
    return (incoming * (s * (1.0 + z * (1.0 - s)))).astype(BF)


def remote(src, dst, send, recv, target):
    return pltpu.make_async_remote_copy(
        src_ref=src, dst_ref=dst, send_sem=send, recv_sem=recv, device_id=target, device_id_type=MESH
    )


SIDES = ((-1, 0), (1, 0), (0, -1), (0, 1), (-1, -1), (-1, 1), (1, -1), (1, 1))


def net_kernel(counts, *refs):
    it = iter(refs)

    def take(n):
        return [next(it) for _ in range(n)]

    syn, embt, k1, k2t, k3, k4, k5, rdo, cot, eye, cQ, cQ2, cU, cS_hbm, cF_hbm = take(15)
    logits_ref, features_ref, embed_ref, grads_ref = take(4)
    xb, e0, z0, z1, f1, e1, z2, f2, e2, z3, e3, z4, e4, z5, f5, t5, t4, t3, t2, t1, fg, cp = take(22)
    w0, w1, w1b, w2, w2b, w3, w3b, w4, w4b, w5, w5b, r4, r4t = take(13)
    halos = [take(2) for _ in WIDTHS]
    cS, cF, far, loads = take(4)
    sends, recvs = take(2)
    g_ref, whole, tall = take(3)
    stages = [take(5) for _ in PARTS]
    sum_sends, sum_recvs, embed_row, embed_col, embed_sends, embed_recvs = take(6)

    n_row, n_col = counts
    row, col = lax.axis_index("row"), lax.axis_index("col")
    there = {
        (-1, 0): row > 0,
        (1, 0): row < n_row - 1,
        (0, -1): col > 0,
        (0, 1): col < n_col - 1,
    }
    for dr in (-1, 1):
        for dc in (-1, 1):
            there[dr, dc] = jnp.logical_and(there[dr, 0], there[0, dc])

    def place(dr, dc):
        return {"row": (row + dr + n_row) % n_row, "col": (col + dc + n_col) % n_col}

    load_near = pltpu.make_async_copy(cS_hbm, cS, loads.at[0])
    load_far = pltpu.make_async_copy(cF_hbm, cF, loads.at[1])
    load_near.start()
    load_far.start()

    partners = [(d, 0) for d in range(1, n_row)] + [(0, d) for d in range(1, n_col)] + list(SIDES[4:])
    barrier = pltpu.get_barrier_semaphore()
    for partner in partners:
        pl.semaphore_signal(barrier, inc=1, device_id=place(*partner), device_id_type=MESH)

    lane = lax.broadcasted_iota(jnp.int32, (1, 128), 1)
    sixteen = lax.broadcasted_iota(jnp.int32, (16, 1), 0)

    def inside(depth):
        down, left, right, corner = bounds(depth)
        spans = [(0, down, (-1, 0)), (down, left, (1, 0)), (left, left + DEEP * depth, (0, -1)), (right, right + DEEP * depth, (0, 1))]
        spans += [(corner + k * depth * depth, corner + (k + 1) * depth * depth, side) for side, k in CORNERS.items()]
        masks = []
        for tile in range(depth):
            at = lane + tile * 128
            keep = lane < 0
            for low, high, side in spans:
                keep = jnp.logical_or(keep, jnp.logical_and(jnp.logical_and(at >= low, at < high), there[side]))
            masks.append(keep)
        return masks

    near_masks, far_masks = inside(1), inside(2)

    def fenced(v):
        return jnp.concatenate([v[:, :CELLS], jnp.where(near_masks[0], v[:, CELLS:], 0.0)], axis=1)

    def begin(n, depth, pieces, ahead=None):
        out, into = halos[n]
        down, left, right, corner = bounds(depth)
        pick = (cQ if depth == 1 else cQ2)[...]
        start = 0
        for piece in pieces:
            out[:, start : start + piece.shape[0]] = nt(pick, piece).astype(BF)
            start += piece.shape[0]
        size = {(-1, 0): (0, down, down), (1, 0): (down, left, 0), (0, -1): (left, right, right), (0, 1): (right, corner, left)}
        copies = []
        for k, (dr, dc) in enumerate(SIDES):
            if (dr, dc) in size:
                low, high, target = size[dr, dc]
            else:
                low, high = corner, corner + 16
                target = 128 * depth + 16 * CORNERS[-dr, -dc]
            copies.append(
                remote(out.at[low:high], into.at[target : target + high - low], sends.at[n, k], recvs.at[n, k], place(dr, dc))
            )
        if ahead is not None:
            ahead()
        for copy in copies:
            copy.start()
        return copies

    def end(n, depth, copies):
        into = halos[n][1]
        corner = bounds(depth)[3]
        for copy in copies:
            copy.wait()
        ends = 0.0
        for k in range(4):
            tile = into[128 * depth + 16 * k : 128 * depth + 16 * (k + 1), :].astype(F32)
            ends = ends + jnp.where(sixteen // (depth * depth) == k, tile, 0.0)
        into[corner : corner + 16, :] = ends.astype(BF)

    def ring(n, depth, start, width):
        into = halos[n][1]
        tiles = []
        for tile, keep in enumerate(near_masks if depth == 1 else far_masks):
            turned = nt(eye[0:width, 0:width], into[tile * 128 : (tile + 1) * 128, start : start + width])
            tiles.append(jnp.where(keep, turned, 0.0).astype(BF))
        return tiles

    def extend(p, width, ref, size):
        for ea in range(p + 2):
            for eb in range(p + 2):
                dr, dc = (ea > p) - (ea < 1), (eb > p) - (eb < 1)
                if (dr, dc) == (0, 0):
                    continue
                start = (((ea - 1) % p + 1) * (p + 2) + (eb - 1) % p + 1) * width
                at = (dr * 3 + dc + 4) * EXT
                moved = mm(ref[start : start + width, :], cS[at : at + EXT, 0:size])
                start = (ea * (p + 2) + eb) * width
                ref[start : start + width, 0:size] = moved.astype(BF)

    ways = {"row": (row, n_row, lambda d: place(d, 0)), "col": (col, n_col, lambda d: place(0, d))}
    flying = {}

    def sum_step(part, step):
        start, size, first = PARTS[part]
        s1, r1, h1, s2, r2 = stages[part]
        me1, n1, to1 = ways[first]
        me2, n2, to2 = ways["col" if first == "row" else "row"]
        c1, c2 = size // n1, size // n1 // n2
        for copy in flying.pop(part, ()):
            copy.wait()
        if step == 4:
            return
        if step == 0:
            s1[...] = g_ref[start : start + size, :].astype(BF)
        elif step == 1:
            total = g_ref[pl.ds(pl.multiple_of(start + me1 * c1, 16), c1), :]
            for d in range(n1 - 1):
                total = total + r1[d].astype(F32)
            h1[...] = total
            s2[...] = total.astype(BF)
        elif step == 2:
            total = h1[pl.ds(pl.multiple_of(me2 * c2, 16), c2), :]
            for d in range(n2 - 1):
                total = total + r2[d].astype(F32)
            whole[pl.ds(pl.multiple_of(start + me1 * c1 + me2 * c2, 16), c2), :] = total.astype(BF)
        copies = []
        for d in range(1, n1 if step in (0, 3) else n2):
            if step == 0:
                src, dst, to = ranged(s1, (me1 + d) % n1 * c1, c1), r1.at[d - 1], to1
            elif step == 1:
                src, dst, to = ranged(s2, (me2 + d) % n2 * c2, c2), r2.at[d - 1], to2
            elif step == 2:
                src = dst = ranged(whole, start + me1 * c1 + me2 * c2, c2)
                to = to2
            else:
                src = dst = ranged(whole, start + me1 * c1, c1)
                to = to1
            copies.append(remote(src, dst, sum_sends.at[part, step, d], sum_recvs.at[part, step, d], to(d)))
        for copy in copies:
            copy.start()
        flying[part] = copies

    def embed_step(step, value=None):
        if step > 0:
            for copy in flying.pop("embed"):
                copy.wait()
            slots = embed_row if step == 1 else embed_col
            value = sum(slots[d] for d in range(slots.shape[0]))
        if step == 2:
            return value
        slots, (me, count, to) = (embed_row, ways["row"]) if step == 0 else (embed_col, ways["col"])
        slots[me] = value
        copies = [
            remote(slots.at[me], slots.at[me], embed_sends.at[step, d], embed_recvs.at[step, d], to(d)) for d in range(1, count)
        ]
        for copy in copies:
            copy.start()
        flying["embed"] = copies

    bit = lax.broadcasted_iota(jnp.int32, (16, 1), 0)
    groups = []
    for a in range(4):
        for t in range(2):
            line = [(syn[16 * t + 4 * r + a : 16 * t + 4 * r + a + 1, :] >> bit) & 1 for r in range(4)]
            groups.append(jnp.concatenate(line, axis=1))
    bits = jnp.concatenate(groups, axis=0).astype(F32).astype(BF)
    phased = mm(bits, cU[...]).astype(BF)
    for a in range(4):
        for t in range(2):
            for b in range(4):
                start = ((a + 1) * 6 + b + 1) * 16
                xb[start : start + 16, t * 128 : (t + 1) * 128] = phased[(a * 2 + t) * 16 : (a * 2 + t + 1) * 16, b * 128 : (b + 1) * 128]
    wide = cot[...].astype(F32)
    groups = []
    for a in range(4):
        for t in range(2):
            line = jnp.concatenate([wide[:, 16 * t + 4 * r + a, :] for r in range(4)], axis=1)
            groups.append(jnp.concatenate([line, jnp.zeros((6, 512), F32)], axis=0))
    phased = mm(jnp.concatenate(groups, axis=0).astype(BF), cU[...])
    for a in range(4):
        for t in range(2):
            start = (a * 2 + t) * 8
            pieces = [phased[start : start + 4, b * 128 : (b + 1) * 128] for b in range(4)]
            cp[a * 16 : (a + 1) * 16, t * 128 : (t + 1) * 128] = jnp.concatenate(pieces, axis=0).astype(BF)

    inner = [((a + 1) * 6 + 1) * 16 for a in range(4)]
    pieces = [jnp.concatenate([xb[i : i + 64, 0:CELLS] for i in inner], axis=0), cp[:, 0:CELLS]]
    copies = begin(0, 1, pieces, lambda: pl.semaphore_wait(barrier, len(partners)))

    def beside(blocks, i, blank):
        return jnp.concatenate(blocks + [blank] if i == 0 else [blank] + blocks, axis=0)

    def added(k, rows, cols):
        return sum(k[ta, tb].astype(F32) for ta in rows for tb in cols).astype(BF)

    def arrange_first():
        repeat = (lax.broadcasted_iota(jnp.int32, (16, 96), 1) % 16 == lax.broadcasted_iota(jnp.int32, (16, 96), 0)).astype(F32).astype(BF)
        tiled = mm(nt(eye[:64, :64], embt[...]).astype(BF), repeat)
        own = lax.broadcasted_iota(jnp.int32, (64, 96), 1) // 16
        for j in range(6):
            w0[j * 64 : (j + 1) * 64, :] = jnp.where(own == j, tiled, 0.0).astype(BF)
        for ta in range(3):
            for i in range(2):
                w1[i * 64 : (i + 1) * 64, ta * 256 : (ta + 1) * 256] = sum(
                    mm(k1[ta, tb], eye[(tb + i) * 64 : (tb + i + 1) * 64, :]) for tb in range(3)
                ).astype(BF)

    def arrange_second():
        blank, empty = jnp.zeros((64, 128), BF), jnp.zeros((64, 64), BF)
        for ta in range(3):
            for i in range(2):
                line = beside([k2t[ta, tb] for tb in range(3)], i, blank)
                w2[i * 128 : (i + 1) * 128, ta * 256 : (ta + 1) * 256] = nt(eye[:128, :128], line).astype(BF)
                for tb in range(3):
                    w2b[i * 64 : (i + 1) * 64, ta * 512 + (tb + i) * 128 : ta * 512 + (tb + i + 1) * 128] = k2t[2 - ta, 2 - tb]
                hole = ta * 512 + (384 if i == 0 else 0)
                w2b[i * 64 : (i + 1) * 64, hole : hole + 128] = blank
                line = beside([k1[2 - ta, 2 - tb] for tb in range(3)], i, empty)
                w1b[i * 64 : (i + 1) * 64, ta * 256 : (ta + 1) * 256] = nt(eye[:64, :64], line).astype(BF)

    def arrange_bottom():
        for t in range(9):
            w3[:, t * 128 : (t + 1) * 128] = k3[t // 3, t % 3]
            w3b[:, t * 256 : (t + 1) * 256] = nt(eye[:128, :128], k3[2 - t // 3, 2 - t % 3]).astype(BF)

    def arrange_return():
        for pa in range(2):
            for pb in range(2):
                for s in range(2):
                    for u in range(2):
                        block = added(k4, UNDER[pa][s], UNDER[pb][u])
                        w4[(pa * 2 + pb) * 128 : (pa * 2 + pb + 1) * 128, (s * 2 + u) * 256 : (s * 2 + u + 1) * 256] = block
                        at = OVER.index(UNDER[pa][s]) * 4 + OVER.index(UNDER[pb][u])
                        w4b[:, at * 128 : (at + 1) * 128] = nt(eye[...], block).astype(BF)

    def arrange_final():
        for pa in range(2):
            for pb in range(2):
                for s in range(2):
                    for u in range(2):
                        start = pa * 128 + (1 - pb) * 64
                        w5[start : start + 64, (s * 2 + u) * 128 : (s * 2 + u + 1) * 128] = added(k5, UNDER[pa][s], UNDER[pb][u])
        for ea in range(4):
            for pair in range(2):
                stack = jnp.concatenate([added(k5, OVER[ea], OVER[2 * pair + i]) for i in range(2)], axis=0)
                at = ea * 2 + pair
                w5b[:, at * 128 : (at + 1) * 128] = nt(eye[:128, :128], stack).astype(BF)

    def arrange_readout():
        repeat = (lax.broadcasted_iota(jnp.int32, (64, 256), 1) % 64 == lax.broadcasted_iota(jnp.int32, (64, 256), 0)).astype(F32).astype(BF)
        tiled = mm(rdo[...], repeat)
        tiled = jnp.concatenate([tiled, jnp.zeros((2, 256), F32)] * 4, axis=0)
        own = lax.broadcasted_iota(jnp.int32, (16, 256), 1) // 64 == lax.broadcasted_iota(jnp.int32, (16, 256), 0) // 4
        r4[...] = jnp.where(own, tiled, 0.0).astype(BF)
        r4t[...] = nt(eye[...], r4[...]).astype(BF)

    arrange_first()
    arrange_readout()
    load_near.wait()
    end(0, 1, copies)
    (tile,) = ring(0, 1, 0, 256)
    for a in range(4):
        xb[inner[a] : inner[a] + 64, CELLS:EXT] = tile[a * 64 : (a + 1) * 64, :]
    cp[:, CELLS:EXT] = ring(0, 1, 256, 64)[0]
    extend(4, 16, xb, EXT)

    for ea in range(6):
        stored, active = activated(mm(w0[...], xb[ea * 96 : (ea + 1) * 96, :]))
        e0[ea * 384 : (ea + 1) * 384, :] = active
        if 1 <= ea <= 4:
            z0[(ea - 1) * 256 : ea * 256, :] = stored[64:320, 0:CELLS]

    for a in range(4):
        for pair in range(2):
            v = sum(
                mm(w1[:, ta * 256 : (ta + 1) * 256], e0[((a + ta) * 6 + 2 * pair) * 64 : ((a + ta) * 6 + 2 * pair + 4) * 64, :])
                for ta in range(3)
            )
            start = (a * 4 + 2 * pair) * 64
            z1[start : start + 128, :], f1[start : start + 128, :] = activated(fenced(v))

    def pooled(ref, side, width, a, b, size):
        spots = [((2 * a + i) * side + 2 * b + j) * width for i in range(2) for j in range(2)]
        return (sum(ref[s : s + width, 0:size].astype(F32) for s in spots) * 0.25).astype(BF)

    for a in range(2):
        for b in range(2):
            start = ((a + 1) * 4 + b + 1) * 64
            e1[start : start + 64, :] = pooled(f1, 4, 64, a, b, EXT)
    extend(2, 64, e1, CELLS)
    arrange_second()

    for a in range(2):
        v = sum(mm(w2[:, ta * 256 : (ta + 1) * 256], e1[(a + ta) * 256 : (a + ta + 1) * 256, 0:CELLS]) for ta in range(3))
        z2[a * 256 : (a + 1) * 256, 0:CELLS], f2[a * 256 : (a + 1) * 256, 0:CELLS] = activated(v)
    e2[4 * 128 : 5 * 128, 0:CELLS] = pooled(f2, 2, 128, 0, 0, CELLS)
    copies = begin(1, 1, [e2[4 * 128 : 5 * 128, 0:CELLS]])
    later = begin(2, 1, [z2[0:256, 0:CELLS], z2[256:512, 0:CELLS]])
    arrange_bottom()
    arrange_final()
    end(1, 1, copies)
    e2[4 * 128 : 5 * 128, CELLS:EXT] = ring(1, 1, 0, 128)[0]
    extend(1, 128, e2, CELLS)

    z3[...], e3[4 * 256 : 5 * 256, 0:CELLS] = activated(mm(w3[...], e2[:, 0:CELLS]))
    copies = begin(3, 1, [e3[4 * 256 : 5 * 256, 0:CELLS]])
    arrange_return()
    end(2, 1, later)
    for a in range(2):
        z2[a * 256 : (a + 1) * 256, CELLS:EXT] = ring(2, 1, a * 256, 256)[0]
        f2[a * 256 : (a + 1) * 256, CELLS:EXT] = activated(z2[a * 256 : (a + 1) * 256, CELLS:EXT])[1]
    end(3, 1, copies)
    e3[4 * 256 : 5 * 256, CELLS:EXT] = ring(3, 1, 0, 256)[0]
    extend(1, 256, e3, EXT)

    for a in range(2):
        for b in range(2):
            n = a * 2 + b
            v = sum(
                mm(w4[n * 128 : (n + 1) * 128, s * 512 : (s + 1) * 512], e3[((a + s) * 3 + b) * 256 : ((a + s) * 3 + b + 2) * 256, :])
                for s in range(2)
            )
            v = v + f2[n * 128 : (n + 1) * 128, :].astype(F32)
            start = ((a + 1) * 4 + b + 1) * 128
            z4[n * 128 : (n + 1) * 128, :], e4[start : start + 128, :] = activated(fenced(v))
    extend(2, 128, e4, EXT)

    RUNS = ((0, 1, 64, 64), (1, 2, 0, 128), (3, 1, 0, 64))
    for a in range(4):
        for b, many, first, size in RUNS:
            base = (a % 2) * 128 + first
            v = sum(
                mm(w5[base : base + size, s * 256 : (s + 1) * 256], e4[((BASE[a] + s) * 4 + BASE[b]) * 128 : ((BASE[a] + s) * 4 + BASE[b] + 2) * 128, :])
                for s in range(2)
            )
            start = (a * 4 + b) * 64
            v = v + f1[start : start + size, :].astype(F32)
            z5[start : start + size, :] = v.astype(BF)

    for a in range(4):
        back = mm(r4t[...], cp[a * 16 : (a + 1) * 16, :])
        start = ((a + 1) * 6 + 1) * 64
        t5[start : start + 256, :] = sloped(back, z5[a * 256 : (a + 1) * 256, :])
    extend(4, 64, t5, CELLS)
    for a in range(2):
        for b in range(2):
            v = sum(
                mm(w5b[:, m * 256 : (m + 1) * 256], t5[((2 * a + m) * 6 + 2 * b) * 64 : ((2 * a + m) * 6 + 2 * b + 4) * 64, 0:CELLS])
                for m in range(4)
            )
            start = ((a + 1) * 4 + b + 1) * 128
            n = a * 2 + b
            t4[start : start + 128, 0:CELLS] = sloped(v, z4[n * 128 : (n + 1) * 128, 0:CELLS])
    copies = begin(4, 1, [t4[((a + 1) * 4 + 1) * 128 : ((a + 1) * 4 + 3) * 128, 0:CELLS] for a in range(2)])

    sums = {}
    for a in range(4):
        for s in range(2):
            for b, many, first, size in RUNS:
                start = ((BASE[a] + s) * 4 + BASE[b]) * 128
                t_start = ((a + 1) * 6 + b + 1) * 64
                product = nt(t5[t_start : t_start + size, 0:CELLS], e4[start : start + 256, 0:CELLS])
                for m in range(many):
                    key = (a % 2, s, (b + m) % 2)
                    block = product[m * 64 : (m + 1) * 64, :]
                    sums[key] = sums[key] + block if key in sums else block

    def reads(parity, tap):
        return 0 if tap in UNDER[parity][0] else 1

    for ta in range(3):
        rowed = [sums[0, reads(0, ta), pb] + sums[1, reads(1, ta), pb] for pb in range(2)]
        for tb in range(3):
            value = sum(rowed[pb][:, reads(pb, tb) * 128 : (reads(pb, tb) + 1) * 128] for pb in range(2))
            start = AT_FINAL + (ta * 3 + tb) * 64
            g_ref[start : start + 64, :] = value

    for b in range(2):
        for u in range(2):
            parts = {}
            for a in range(2):
                for s in range(2):
                    start = ((a + 1) * 4 + b + 1) * 128
                    from_ = ((a + s) * 3 + b + u) * 256
                    parts[a, s] = nt(t4[start : start + 128, 0:CELLS], e3[from_ : from_ + 256, 0:CELLS])
            for ta in range(3):
                value = parts[0, reads(0, ta)] + parts[1, reads(1, ta)]
                for tb in UNDER[b][u]:
                    for half in range(2):
                        start = AT_RETURN + ((ta * 3 + tb) * 2 + half) * 128
                        piece = value[:, half * 128 : (half + 1) * 128]
                        g_ref[start : start + 128, :] = piece if b == 0 else g_ref[start : start + 128, :] + piece

    sum_step(0, 0)
    sum_step(1, 0)
    total = jnp.zeros((16, 256), F32)
    for a in range(4):
        f5[a * 256 : (a + 1) * 256, :] = activated(z5[a * 256 : (a + 1) * 256, 0:CELLS])[1]
        total = total + nt(cp[a * 16 : (a + 1) * 16, 0:CELLS], f5[a * 256 : (a + 1) * 256, :])
    total = sum(total[b * 4 : (b + 1) * 4, b * 64 : (b + 1) * 64] for b in range(4))
    g_ref[AT_READ:ROWS, :] = jnp.zeros((ROWS - AT_READ, 128), F32)
    g_ref[AT_READ : AT_READ + 4, 0:64] = total

    end(4, 1, copies)
    for a in range(2):
        start = ((a + 1) * 4 + 1) * 128
        t4[start : start + 256, CELLS:EXT] = ring(4, 1, a * 256, 256)[0]
    extend(2, 128, t4, CELLS)
    v = sum(mm(w4b[:, m * 512 : (m + 1) * 512], t4[m * 512 : (m + 1) * 512, 0:CELLS]) for m in range(4))
    far[:, 0:CELLS] = sloped(v, z3[...])
    copies = begin(5, 2, [far[:, 0:CELLS]])
    for t in range(9):
        g_ref[AT_BOTTOM + t * 256 : AT_BOTTOM + (t + 1) * 256, :] = nt(far[:, 0:CELLS], e2[t * 128 : (t + 1) * 128, 0:CELLS])
    sum_step(2, 0)
    sum_step(3, 0)
    groups = []
    for a in range(4):
        here = f5[a * 256 : (a + 1) * 256, :]
        value = mm(r4[...], here)
        for t in range(2):
            groups.append(jnp.concatenate([value[b * 4 : (b + 1) * 4, t * 128 : (t + 1) * 128] for b in range(4)], axis=1))
    value = jnp.concatenate(groups, axis=0)
    laid = 0.0
    for _ in range(3):
        piece = value.astype(BF)
        laid = laid + nt(piece, cU[...])
        value = value - piece.astype(F32)
    for a in range(4):
        for t in range(2):
            for r in range(4):
                h = 16 * t + 4 * r + a
                logits_ref[:, h : h + 1, :] = laid[(a * 2 + t) * 4 : (a * 2 + t) * 4 + 2, r * 128 : (r + 1) * 128].reshape(2, 1, 128)
    load_far.wait()
    end(5, 2, copies)
    far[:, 256:384], far[:, 384:512] = ring(5, 2, 0, 256)
    for n in range(9):
        t3[n * 256 : (n + 1) * 256, :] = mm(far[...], cF[n * 512 : (n + 1) * 512, :]).astype(BF)

    through = mm(w3b[...], t3[...]) * 0.25
    for a in range(2):
        for b in range(2):
            n = a * 2 + b
            start = ((a + 1) * 4 + b + 1) * 128
            v = fenced(t4[start : start + 128, :].astype(F32) + through)
            t2[start : start + 128, :] = sloped(v, z2[n * 128 : (n + 1) * 128, :])
    for ta in range(3):
        product = 0.0
        for a in range(2):
            start = ((a + 1) * 4 + 1) * 128
            product = product + nt(e1[(a + ta) * 256 : (a + ta + 1) * 256, 0:CELLS], t2[start : start + 256, 0:CELLS])
        g_ref[AT_SECOND + ta * 192 : AT_SECOND + (ta + 1) * 192, :] = product[0:192, 0:128] + product[64:256, 128:256]
    sum_step(0, 1)
    sum_step(1, 1)
    extend(2, 128, t2, EXT)

    for a in range(2):
        v = sum(mm(w2b[:, ta * 512 : (ta + 1) * 512], t2[(a + ta) * 512 : (a + ta + 1) * 512, :]) for ta in range(3)) * 0.25
        for b in range(2):
            for i in range(2):
                for j in range(2):
                    fa, fb = 2 * a + i, 2 * b + j
                    start = ((fa + 1) * 6 + fb + 1) * 64
                    n = (fa * 4 + fb) * 64
                    t1[start : start + 64, :] = sloped(fenced(t5[start : start + 64, :].astype(F32) + v[b * 64 : (b + 1) * 64, :]), z1[n : n + 64, :])
    for ta in range(3):
        product = 0.0
        for a in range(4):
            for pair in range(2):
                start = ((a + 1) * 6 + 2 * pair + 1) * 64
                from_ = ((a + ta) * 6 + 2 * pair) * 64
                product = product + nt(t1[start : start + 128, 0:CELLS], e0[from_ : from_ + 256, 0:CELLS])
        value = product[0:64, 0:192] + product[64:128, 64:256]
        g_ref[AT_FIRST + ta * 64 : AT_FIRST + (ta + 1) * 64, :] = value[:, 0:128]
        start = AT_FIRST + (192 if ta < 2 else 256)
        g_ref[start : start + 64, ta % 2 * 64 : ta % 2 * 64 + 64] = value[:, 128:192]
    g_ref[AT_FIRST + 256 : AT_FIRST + 320, 64:128] = jnp.zeros((64, 64), F32)
    sum_step(4, 0)
    extend(4, 64, t1, CELLS)

    total = jnp.zeros((64, 256), F32)
    for a in range(4):
        for pair in range(2):
            v = sum(
                mm(w1b[:, ta * 256 : (ta + 1) * 256], t1[((a + ta) * 6 + 2 * pair) * 64 : ((a + ta) * 6 + 2 * pair + 4) * 64, 0:CELLS])
                for ta in range(3)
            )
            start = (a * 4 + 2 * pair) * 64
            fg[start : start + 128, :] = sloped(v, z0[start : start + 128, :])
        start = ((a + 1) * 6 + 1) * 16
        total = total + nt(xb[start : start + 64, 0:CELLS], fg[a * 256 : (a + 1) * 256, :])
    total = sum(total[b * 16 : (b + 1) * 16, b * 64 : (b + 1) * 64] for b in range(4))
    embed_step(0, total)

    def lay(a):
        for t in range(2):
            line = jnp.concatenate([fg[(a * 4 + b) * 64 : (a * 4 + b + 1) * 64, t * 128 : (t + 1) * 128] for b in range(4)], axis=1)
            laid = nt(line, cU[...])
            for r in range(4):
                tall[:, 16 * t + 4 * r + a, :] = laid[:, r * 128 : (r + 1) * 128]

    sum_step(2, 1)
    sum_step(3, 1)
    sum_step(0, 2)
    sum_step(1, 2)
    sum_step(4, 1)
    lay(0)
    lay(1)
    embed_step(1)
    sum_step(2, 2)
    sum_step(3, 2)
    sum_step(0, 3)
    sum_step(1, 3)
    sum_step(4, 2)
    lay(2)
    lay(3)
    features_ref[...] = tall[...].astype(BF)
    sum_step(2, 3)
    sum_step(3, 3)
    sum_step(4, 3)
    embed_ref[...] = embed_step(2)
    for part in range(len(PARTS)):
        sum_step(part, 4)
    grads_ref[...] = whole[...]


WIDTHS = ((384, 1), (128, 1), (512, 1), (256, 1), (512, 1), (256, 2))


def run_net(counts, *args):
    syn, emb, k1, k2, *rest = args
    args = (syn, emb.T, k1, k2.transpose(0, 1, 3, 2), *rest)
    tables = [jnp.asarray(t, BF) for t in (np.eye(CELLS), PICK, PICK_FAR, SPREAD, SHIFT, SHIFT_FAR)]
    wide, own = (EXT,), (CELLS,)
    blocks = [(16 * 36,) + wide, (64 * 36,) + wide, (1024,) + own, (1024,) + wide, (1024,) + wide, (1024,) + wide]
    blocks += [(512,) + wide, (512,) + wide, (128 * 9,) + wide, (256,) + own, (256 * 9,) + wide, (512,) + wide, (128 * 16,) + wide]
    blocks += [(1024,) + wide, (1024,) + own, (64 * 36,) + wide, (128 * 16,) + wide, (256 * 9,) + wide, (128 * 16,) + wide]
    blocks += [(64 * 36,) + wide, (1024,) + own, (64,) + wide]
    weights = [(384, 96), (128, 768), (128, 768), (256, 768), (128, 1536), (256, 1152), (128, 2304), (512, 1024), (256, 2048), (256, 512), (128, 1024), (16, 256), (256, 16)]
    scratch = [pltpu.VMEM(s, BF) for s in blocks + weights]
    for width, depth in WIDTHS:
        scratch += [pltpu.VMEM((bounds(depth)[3] + 16, width), BF), pltpu.VMEM((128 * depth + 64, width), BF)]
    scratch += [pltpu.VMEM(SHIFT.shape, BF), pltpu.VMEM(SHIFT_FAR.shape, BF), pltpu.VMEM((256, 512), BF), pltpu.SemaphoreType.DMA((2,))]
    scratch += [pltpu.SemaphoreType.DMA((len(WIDTHS), 8)), pltpu.SemaphoreType.DMA((len(WIDTHS), 8))]
    scratch += [pltpu.VMEM((ROWS, 128), F32), pltpu.VMEM((ROWS, 128), BF), pltpu.VMEM((64, 32, 128), F32)]
    n_row, n_col = counts
    most = max(n_row, n_col)
    for _, size, first in PARTS:
        n1, n2 = (n_row, n_col) if first == "row" else (n_col, n_row)
        c1, c2 = size // n1, size // n1 // n2
        scratch += [
            pltpu.VMEM((size, 128), BF),
            pltpu.VMEM((n1 - 1, c1, 128), BF),
            pltpu.VMEM((c1, 128), F32),
            pltpu.VMEM((c1, 128), BF),
            pltpu.VMEM((n2 - 1, c2, 128), BF),
        ]
    scratch += [pltpu.SemaphoreType.DMA((len(PARTS), 4, most)), pltpu.SemaphoreType.DMA((len(PARTS), 4, most))]
    scratch += [pltpu.VMEM((n_row, 16, 64), F32), pltpu.VMEM((n_col, 16, 64), F32)]
    scratch += [pltpu.SemaphoreType.DMA((2, most)), pltpu.SemaphoreType.DMA((2, most))]
    vmem = pl.BlockSpec(memory_space=pltpu.VMEM)
    return pl.pallas_call(
        functools.partial(net_kernel, counts),
        out_shape=(
            jax.ShapeDtypeStruct((2, 32, 128), F32),
            jax.ShapeDtypeStruct((64, 32, 128), BF),
            jax.ShapeDtypeStruct((16, 64), F32),
            jax.ShapeDtypeStruct((ROWS, 128), BF),
        ),
        in_specs=[vmem] * 13 + [pl.BlockSpec(memory_space=pl.ANY)] * 2,
        out_specs=(vmem,) * 4,
        scratch_shapes=scratch,
        compiler_params=pltpu.CompilerParams(collective_id=1, has_side_effects=True, vmem_limit_bytes=56 * 2**20),
    )(*args, *tables)


def out_kernel(logits, features, embed, g, o_logits, o_features, o_embed, o_first, o_second, o_bottom, o_return, o_final, o_read):
    o_logits[...] = logits[...]
    o_features[...] = features[...]
    for t in range(9):
        ta, tb = t // 3, t % 3
        for half in range(2):
            start = AT_RETURN + (t * 2 + half) * 128
            o_return[ta, tb, :, half * 128 : (half + 1) * 128] = g[start : start + 128, :].astype(F32)
        o_final[ta, tb] = g[AT_FINAL + t * 64 : AT_FINAL + (t + 1) * 64, :].astype(F32)
        o_bottom[ta, tb] = g[AT_BOTTOM + t * 256 : AT_BOTTOM + (t + 1) * 256, :].astype(F32)
        o_second[ta, tb] = g[AT_SECOND + t * 64 : AT_SECOND + (t + 1) * 64, :].astype(F32)
        start, low = (AT_FIRST + ta * 64, tb * 64) if tb < 2 else (AT_FIRST + (192 if ta < 2 else 256), ta % 2 * 64)
        o_first[ta, tb] = g[start : start + 64, low : low + 64].astype(F32)
    o_embed[...] = embed[...]
    o_read[...] = g[AT_READ : AT_READ + 16, 0:64].astype(F32)[0:2]


def write_out(logits, features, embed, g):
    shapes = [(2, 32, 128), (64, 32, 128), (16, 64), (3, 3, 64, 64), (3, 3, 64, 128), (3, 3, 256, 128), (3, 3, 128, 256), (3, 3, 64, 128), (2, 64)]
    vmem = pl.BlockSpec(memory_space=pltpu.VMEM)
    outs = pl.pallas_call(
        out_kernel,
        out_shape=tuple(jax.ShapeDtypeStruct(s, BF if n == 1 else F32) for n, s in enumerate(shapes)),
        in_specs=[vmem] * 4,
        out_specs=(vmem,) * 9,
        compiler_params=pltpu.CompilerParams(vmem_limit_bytes=32 * 2**20),
    )(logits, features, embed, g)
    outs = list(outs)
    outs[2] = outs[2].T
    outs[4] = outs[4].transpose(0, 1, 3, 2)
    return tuple(outs)


def on_device(counts, *args):
    return write_out(*run_net(counts, *args))


def solution(mesh):
    counts = (mesh.shape["row"], mesh.shape["col"])
    cells = P(None, ("batch", "row"), "col")
    in_specs = (P(("batch", "row"), "col"),) + (P(),) * 7 + (cells,)
    out_specs = (cells, cells, P("batch", None)) + (P("batch", None, None, None),) * 5 + (P("batch", None),)
    return jax.shard_map(
        functools.partial(on_device, counts), mesh=mesh, in_specs=in_specs, out_specs=out_specs, check_vma=False
    )
```

```python
import functools

import jax
import jax.numpy as jnp
import numpy as np
from jax import lax
from jax.experimental import pallas as pl
from jax.experimental.pallas import tpu as pltpu
from jax.sharding import PartitionSpec as P

BF, F32 = jnp.bfloat16, jnp.float32
MESH = pl.DeviceIdType.MESH

DEEP, WIDE = 8, 32
CELLS = DEEP * WIDE
EXT = CELLS + 128

ROWS = 6272
PARTS = ((0, 1536, "row"), (1536, 1408, "col"), (2944, 1152, "row"), (4096, 1152, "col"), (5248, 640, "row"), (5888, 384, "col"))
AT_RETURN, AT_FINAL, AT_BOTTOM, AT_SECOND, AT_FIRST, AT_READ = 0, 2304, 2944, 5248, 5888, 6208


def ranged(values, start, size):
    return values.at[pl.ds(pl.multiple_of(start, 16), size), :]


def bounds(depth):
    left = 2 * WIDE * depth
    return WIDE * depth, left, left + 16, left + 32


def lane_of(r, q, depth):
    if not (-depth <= r < DEEP + depth and -depth <= q < WIDE + depth):
        return None
    row_in, col_in = 0 <= r < DEEP, 0 <= q < WIDE
    down, left, right, corner = bounds(depth)
    if row_in and col_in:
        return r * WIDE + q
    i = r + depth if r < 0 else r - DEEP
    j = q + depth if q < 0 else q - WIDE
    if col_in:
        return CELLS + (0 if r < 0 else down) + i * WIDE + q
    if row_in:
        return CELLS + (left if q < 0 else right) + j * DEEP + r
    return CELLS + corner + CORNERS[(-1 if r < 0 else 1, -1 if q < 0 else 1)] * depth * depth + i * depth + j


def shift_tables(depth, size):
    tables = []
    for dr in (-1, 0, 1):
        for dc in (-1, 0, 1):
            m = np.zeros((size, EXT), np.float32)
            for r in range(-1, DEEP + 1):
                for q in range(-1, WIDE + 1):
                    source = lane_of(r + dr, q + dc, depth)
                    if source is not None:
                        m[source, lane_of(r, q, 1)] = 1
            tables.append(m)
    return np.concatenate(tables)


def pick_table(depth):
    down, left, right, corner = bounds(depth)
    m = np.zeros((corner + 16, CELLS), np.float32)
    for i in range(depth):
        for q in range(WIDE):
            m[i * WIDE + q, i * WIDE + q] = 1
            m[down + i * WIDE + q, (DEEP - depth + i) * WIDE + q] = 1
        for r in range(DEEP):
            m[left + i * DEEP + r, r * WIDE + i] = 1
            m[right + i * DEEP + r, r * WIDE + WIDE - depth + i] = 1
        for j in range(depth):
            for k, (r, q) in enumerate(((0, 0), (0, WIDE - depth), (DEEP - depth, 0), (DEEP - depth, WIDE - depth))):
                m[corner + k * depth * depth + i * depth + j, (r + i) * WIDE + q + j] = 1
    return m


CORNERS = {(-1, -1): 3, (-1, 1): 2, (1, -1): 1, (1, 1): 0}


def spread_table():
    m = np.zeros((512, 512), np.float32)
    for r in range(4):
        for w in range(128):
            m[r * 128 + w, (w % 4) * 128 + r * WIDE + w // 4] = 1
    return m


SHIFT = shift_tables(1, EXT)
SHIFT_FAR = shift_tables(2, 512)
PICK, PICK_FAR = pick_table(1), pick_table(2)
SPREAD = spread_table()

UNDER = (((0,), (1, 2)), ((0, 1), (2,)))
OVER = ((2,), (1, 2), (0, 1), (0,))
BASE = (0, 1, 1, 2)


def mm(a, b):
    return jnp.dot(a, b, preferred_element_type=F32)


def nt(a, b):
    return lax.dot_general(a, b, (((1,), (1,)), ((), ())), preferred_element_type=F32)


def logistic(z):
    return 0.5 + 0.5 * jnp.tanh(0.5 * z)


def activated(v):
    stored = v.astype(BF)
    z = stored.astype(F32)
    return stored, (z * logistic(z)).astype(BF)


def sloped(incoming, stored):
    z = stored.astype(F32)
    s = logistic(z)
    return (incoming * (s * (1.0 + z * (1.0 - s)))).astype(BF)


def remote(src, dst, send, recv, target):
    return pltpu.make_async_remote_copy(
        src_ref=src, dst_ref=dst, send_sem=send, recv_sem=recv, device_id=target, device_id_type=MESH
    )


SIDES = ((-1, -1), (-1, 1), (1, -1), (1, 1), (0, -1), (0, 1), (-1, 0), (1, 0))


def net_kernel(counts, *refs):
    it = iter(refs)

    def take(n):
        return [next(it) for _ in range(n)]

    syn, embt, rdo, cot, eye, cQ, cU = take(7)
    afar = take(8)
    logits_out, features_out, embed_ref, grads_out = take(4)
    xb, e0, z0, z1, f1, e1, z2, f2, e2, z3, e3, z4, e4, z5, f5, t5, t4, t3, t2, t1, fg, cp = take(22)
    w0, w1, w1b, w2, w2b, w3, w3b, w4, w4b, w5, w5b, r4, r4t = take(13)
    halos = [take(2) for _ in WIDTHS]
    near = take(8)
    k1, cS, k2t, k3, k5, k4, cQ2, cF = near
    far, loads, logits_ref, features_ref, stores = take(5)
    sends, recvs = take(2)
    g_ref, whole, tall = take(3)
    stages = [take(3) for _ in PARTS]
    sum_sends, sum_recvs, embed_row, embed_col, embed_sends, embed_recvs = take(6)

    n_row, n_col = counts
    row, col = lax.axis_index("row"), lax.axis_index("col")
    there = {
        (-1, 0): row > 0,
        (1, 0): row < n_row - 1,
        (0, -1): col > 0,
        (0, 1): col < n_col - 1,
    }
    for dr in (-1, 1):
        for dc in (-1, 1):
            there[dr, dc] = jnp.logical_and(there[dr, 0], there[0, dc])

    def place(dr, dc):
        return {"row": (row + dr + n_row) % n_row, "col": (col + dc + n_col) % n_col}

    loading = {}
    for n, (source, target) in enumerate(zip(afar, near)):
        loading[id(target)] = pltpu.make_async_copy(source, target, loads.at[n])
        loading[id(target)].start()

    def loaded(*targets):
        for target in targets:
            loading[id(target)].wait()

    storing = []

    def store(source, target):
        storing.append(pltpu.make_async_copy(source, target, stores.at[len(storing)]))
        storing[-1].start()

    partners = [(d, 0) for d in range(1, n_row)] + [(0, d) for d in range(1, n_col)] + list(SIDES[:4])
    barrier = pltpu.get_barrier_semaphore()
    for partner in partners:
        pl.semaphore_signal(barrier, inc=1, device_id=place(*partner), device_id_type=MESH)

    lane = lax.broadcasted_iota(jnp.int32, (1, 128), 1)
    sixteen = lax.broadcasted_iota(jnp.int32, (16, 1), 0)

    def inside(depth):
        down, left, right, corner = bounds(depth)
        spans = [(0, down, (-1, 0)), (down, left, (1, 0)), (left, left + DEEP * depth, (0, -1)), (right, right + DEEP * depth, (0, 1))]
        spans += [(corner + k * depth * depth, corner + (k + 1) * depth * depth, side) for side, k in CORNERS.items()]
        masks = []
        for tile in range(depth):
            at = lane + tile * 128
            keep = lane < 0
            for low, high, side in spans:
                keep = jnp.logical_or(keep, jnp.logical_and(jnp.logical_and(at >= low, at < high), there[side]))
            masks.append(keep)
        return masks

    near_masks, far_masks = inside(1), inside(2)

    def fenced(v):
        return jnp.concatenate([v[:, :CELLS], jnp.where(near_masks[0], v[:, CELLS:], 0.0)], axis=1)

    def begin(n, depth, pieces, ahead=None):
        out, into = halos[n]
        down, left, right, corner = bounds(depth)
        pick = (cQ if depth == 1 else cQ2)[...]
        start = 0
        for piece in pieces:
            out[:, start : start + piece.shape[0]] = nt(pick, piece).astype(BF)
            start += piece.shape[0]
        size = {(-1, 0): (0, down, down), (1, 0): (down, left, 0), (0, -1): (left, right, right), (0, 1): (right, corner, left)}
        copies = []
        for k, (dr, dc) in enumerate(SIDES):
            if (dr, dc) in size:
                low, high, target = size[dr, dc]
            else:
                low, high = corner, corner + 16
                target = 128 * depth + 16 * CORNERS[-dr, -dc]
            copies.append(
                remote(out.at[low:high], into.at[target : target + high - low], sends.at[n, k], recvs.at[n, k], place(dr, dc))
            )
        if ahead is not None:
            ahead()
        for copy in copies:
            copy.start()
        return copies

    def end(n, depth, copies):
        into = halos[n][1]
        corner = bounds(depth)[3]
        for copy in copies:
            copy.wait()
        ends = 0.0
        for k in range(4):
            tile = into[128 * depth + 16 * k : 128 * depth + 16 * (k + 1), :].astype(F32)
            ends = ends + jnp.where(sixteen // (depth * depth) == k, tile, 0.0)
        into[corner : corner + 16, :] = ends.astype(BF)

    def ring(n, depth, start, width):
        into = halos[n][1]
        tiles = []
        for tile, keep in enumerate(near_masks if depth == 1 else far_masks):
            turned = nt(eye[0:width, 0:width], into[tile * 128 : (tile + 1) * 128, start : start + width])
            tiles.append(jnp.where(keep, turned, 0.0).astype(BF))
        return tiles

    def extend(p, width, ref, size):
        for ea in range(p + 2):
            for eb in range(p + 2):
                dr, dc = (ea > p) - (ea < 1), (eb > p) - (eb < 1)
                if (dr, dc) == (0, 0):
                    continue
                start = (((ea - 1) % p + 1) * (p + 2) + (eb - 1) % p + 1) * width
                at = (dr * 3 + dc + 4) * EXT
                moved = mm(ref[start : start + width, :], cS[at : at + EXT, 0:size])
                start = (ea * (p + 2) + eb) * width
                ref[start : start + width, 0:size] = moved.astype(BF)

    ways = {"row": (row, n_row, lambda d: place(d, 0)), "col": (col, n_col, lambda d: place(0, d))}
    flying = {}

    def sum_step(part, step):
        start, size, first = PARTS[part]
        s1, r1, r2 = stages[part]
        me1, n1, to1 = ways[first]
        me2, n2, to2 = ways["col" if first == "row" else "row"]
        c1 = size // n1
        for copy in flying.pop(part, ()):
            copy.wait()
        if step == 3:
            store(whole.at[start : start + size], grads_out.at[start : start + size])
            return
        own = pl.ds(pl.multiple_of(start + me1 * c1, 16), c1)
        if step == 0:
            s1[...] = g_ref[start : start + size, :].astype(BF)
        elif step == 1:
            total = g_ref[own, :]
            for d in range(n1 - 1):
                total = total + r1[d].astype(F32)
            r2[me2] = total.astype(BF)
        else:
            whole[own, :] = sum(r2[d].astype(F32) for d in range(n2)).astype(BF)
        copies = []
        for d in range(1, n2 if step == 1 else n1):
            if step == 0:
                src, dst, to = ranged(s1, (me1 + d) % n1 * c1, c1), r1.at[d - 1], to1
            elif step == 1:
                src = dst = r2.at[me2]
                to = to2
            else:
                src = dst = ranged(whole, start + me1 * c1, c1)
                to = to1
            copies.append(remote(src, dst, sum_sends.at[part, step, d], sum_recvs.at[part, step, d], to(d)))
        for copy in copies:
            copy.start()
        flying[part] = copies

    def embed_step(step, value=None):
        if step > 0:
            for copy in flying.pop("embed"):
                copy.wait()
            slots = embed_row if step == 1 else embed_col
            value = sum(slots[d] for d in range(slots.shape[0]))
        if step == 2:
            return value
        slots, (me, count, to) = (embed_row, ways["row"]) if step == 0 else (embed_col, ways["col"])
        slots[me] = value
        copies = [
            remote(slots.at[me], slots.at[me], embed_sends.at[step, d], embed_recvs.at[step, d], to(d)) for d in range(1, count)
        ]
        for copy in copies:
            copy.start()
        flying["embed"] = copies

    bit = lax.broadcasted_iota(jnp.int32, (16, 1), 0)
    groups = []
    for a in range(4):
        for t in range(2):
            line = [(syn[16 * t + 4 * r + a : 16 * t + 4 * r + a + 1, :] >> bit) & 1 for r in range(4)]
            groups.append(jnp.concatenate(line, axis=1))
    bits = jnp.concatenate(groups, axis=0).astype(F32).astype(BF)
    phased = mm(bits, cU[...]).astype(BF)
    for a in range(4):
        for t in range(2):
            for b in range(4):
                start = ((a + 1) * 6 + b + 1) * 16
                xb[start : start + 16, t * 128 : (t + 1) * 128] = phased[(a * 2 + t) * 16 : (a * 2 + t + 1) * 16, b * 128 : (b + 1) * 128]
    wide = cot[...].astype(F32)
    groups = []
    for a in range(4):
        for t in range(2):
            line = jnp.concatenate([wide[:, 16 * t + 4 * r + a, :] for r in range(4)], axis=1)
            groups.append(jnp.concatenate([line, jnp.zeros((6, 512), F32)], axis=0))
    phased = mm(jnp.concatenate(groups, axis=0).astype(BF), cU[...])
    for a in range(4):
        for t in range(2):
            start = (a * 2 + t) * 8
            pieces = [phased[start : start + 4, b * 128 : (b + 1) * 128] for b in range(4)]
            cp[a * 16 : (a + 1) * 16, t * 128 : (t + 1) * 128] = jnp.concatenate(pieces, axis=0).astype(BF)

    inner = [((a + 1) * 6 + 1) * 16 for a in range(4)]
    pieces = [jnp.concatenate([xb[i : i + 64, 0:CELLS] for i in inner], axis=0), cp[:, 0:CELLS]]
    copies = begin(0, 1, pieces, lambda: pl.semaphore_wait(barrier, len(partners)))

    def beside(blocks, i, blank):
        return jnp.concatenate(blocks + [blank] if i == 0 else [blank] + blocks, axis=0)

    def added(k, rows, cols):
        return sum(k[ta, tb].astype(F32) for ta in rows for tb in cols).astype(BF)

    def arrange_first():
        repeat = (lax.broadcasted_iota(jnp.int32, (16, 96), 1) % 16 == lax.broadcasted_iota(jnp.int32, (16, 96), 0)).astype(F32).astype(BF)
        tiled = mm(nt(eye[:64, :64], embt[...]).astype(BF), repeat)
        own = lax.broadcasted_iota(jnp.int32, (64, 96), 1) // 16
        for j in range(6):
            w0[j * 64 : (j + 1) * 64, :] = jnp.where(own == j, tiled, 0.0).astype(BF)
        for ta in range(3):
            for i in range(2):
                w1[i * 64 : (i + 1) * 64, ta * 256 : (ta + 1) * 256] = sum(
                    mm(k1[ta, tb], eye[(tb + i) * 64 : (tb + i + 1) * 64, :]) for tb in range(3)
                ).astype(BF)

    def arrange_second():
        blank, empty = jnp.zeros((64, 128), BF), jnp.zeros((64, 64), BF)
        for ta in range(3):
            for i in range(2):
                line = beside([k2t[ta, tb] for tb in range(3)], i, blank)
                w2[i * 128 : (i + 1) * 128, ta * 256 : (ta + 1) * 256] = nt(eye[:128, :128], line).astype(BF)
                for tb in range(3):
                    w2b[i * 64 : (i + 1) * 64, ta * 512 + (tb + i) * 128 : ta * 512 + (tb + i + 1) * 128] = k2t[2 - ta, 2 - tb]
                hole = ta * 512 + (384 if i == 0 else 0)
                w2b[i * 64 : (i + 1) * 64, hole : hole + 128] = blank
                line = beside([k1[2 - ta, 2 - tb] for tb in range(3)], i, empty)
                w1b[i * 64 : (i + 1) * 64, ta * 256 : (ta + 1) * 256] = nt(eye[:64, :64], line).astype(BF)

    def arrange_bottom():
        for t in range(9):
            w3[:, t * 128 : (t + 1) * 128] = k3[t // 3, t % 3]
            w3b[:, t * 256 : (t + 1) * 256] = nt(eye[:128, :128], k3[2 - t // 3, 2 - t % 3]).astype(BF)

    def arrange_return():
        for pa in range(2):
            for pb in range(2):
                for s in range(2):
                    for u in range(2):
                        block = added(k4, UNDER[pa][s], UNDER[pb][u])
                        w4[(pa * 2 + pb) * 128 : (pa * 2 + pb + 1) * 128, (s * 2 + u) * 256 : (s * 2 + u + 1) * 256] = block
                        at = OVER.index(UNDER[pa][s]) * 4 + OVER.index(UNDER[pb][u])
                        w4b[:, at * 128 : (at + 1) * 128] = nt(eye[...], block).astype(BF)

    def arrange_final():
        for pa in range(2):
            for pb in range(2):
                for s in range(2):
                    for u in range(2):
                        start = pa * 128 + (1 - pb) * 64
                        w5[start : start + 64, (s * 2 + u) * 128 : (s * 2 + u + 1) * 128] = added(k5, UNDER[pa][s], UNDER[pb][u])
        for ea in range(4):
            for pair in range(2):
                stack = jnp.concatenate([added(k5, OVER[ea], OVER[2 * pair + i]) for i in range(2)], axis=0)
                at = ea * 2 + pair
                w5b[:, at * 128 : (at + 1) * 128] = nt(eye[:128, :128], stack).astype(BF)

    def arrange_readout():
        repeat = (lax.broadcasted_iota(jnp.int32, (64, 256), 1) % 64 == lax.broadcasted_iota(jnp.int32, (64, 256), 0)).astype(F32).astype(BF)
        tiled = mm(rdo[...], repeat)
        tiled = jnp.concatenate([tiled, jnp.zeros((2, 256), F32)] * 4, axis=0)
        own = lax.broadcasted_iota(jnp.int32, (16, 256), 1) // 64 == lax.broadcasted_iota(jnp.int32, (16, 256), 0) // 4
        r4[...] = jnp.where(own, tiled, 0.0).astype(BF)
        r4t[...] = nt(eye[...], r4[...]).astype(BF)

    loaded(k1)
    arrange_first()
    arrange_readout()
    loaded(cS)
    end(0, 1, copies)
    (tile,) = ring(0, 1, 0, 256)
    for a in range(4):
        xb[inner[a] : inner[a] + 64, CELLS:EXT] = tile[a * 64 : (a + 1) * 64, :]
    cp[:, CELLS:EXT] = ring(0, 1, 256, 64)[0]
    extend(4, 16, xb, EXT)

    for ea in range(6):
        stored, active = activated(mm(w0[...], xb[ea * 96 : (ea + 1) * 96, :]))
        e0[ea * 384 : (ea + 1) * 384, :] = active
        if 1 <= ea <= 4:
            z0[(ea - 1) * 256 : ea * 256, :] = stored[64:320, 0:CELLS]

    for a in range(4):
        for pair in range(2):
            v = sum(
                mm(w1[:, ta * 256 : (ta + 1) * 256], e0[((a + ta) * 6 + 2 * pair) * 64 : ((a + ta) * 6 + 2 * pair + 4) * 64, :])
                for ta in range(3)
            )
            start = (a * 4 + 2 * pair) * 64
            z1[start : start + 128, :], f1[start : start + 128, :] = activated(fenced(v))

    def pooled(ref, side, width, a, b, size):
        spots = [((2 * a + i) * side + 2 * b + j) * width for i in range(2) for j in range(2)]
        return (sum(ref[s : s + width, 0:size].astype(F32) for s in spots) * 0.25).astype(BF)

    for a in range(2):
        for b in range(2):
            start = ((a + 1) * 4 + b + 1) * 64
            e1[start : start + 64, :] = pooled(f1, 4, 64, a, b, EXT)
    extend(2, 64, e1, CELLS)
    loaded(k2t)
    arrange_second()

    for a in range(2):
        v = sum(mm(w2[:, ta * 256 : (ta + 1) * 256], e1[(a + ta) * 256 : (a + ta + 1) * 256, 0:CELLS]) for ta in range(3))
        z2[a * 256 : (a + 1) * 256, 0:CELLS], f2[a * 256 : (a + 1) * 256, 0:CELLS] = activated(v)
    e2[4 * 128 : 5 * 128, 0:CELLS] = pooled(f2, 2, 128, 0, 0, CELLS)
    copies = begin(1, 1, [e2[4 * 128 : 5 * 128, 0:CELLS]])
    later = begin(2, 1, [z2[0:256, 0:CELLS], z2[256:512, 0:CELLS]])
    loaded(k3, k5)
    arrange_bottom()
    arrange_final()
    end(1, 1, copies)
    e2[4 * 128 : 5 * 128, CELLS:EXT] = ring(1, 1, 0, 128)[0]
    extend(1, 128, e2, CELLS)

    z3[...], e3[4 * 256 : 5 * 256, 0:CELLS] = activated(mm(w3[...], e2[:, 0:CELLS]))
    copies = begin(3, 1, [e3[4 * 256 : 5 * 256, 0:CELLS]])
    loaded(k4)
    arrange_return()
    end(2, 1, later)
    for a in range(2):
        z2[a * 256 : (a + 1) * 256, CELLS:EXT] = ring(2, 1, a * 256, 256)[0]
        f2[a * 256 : (a + 1) * 256, CELLS:EXT] = activated(z2[a * 256 : (a + 1) * 256, CELLS:EXT])[1]
    end(3, 1, copies)
    e3[4 * 256 : 5 * 256, CELLS:EXT] = ring(3, 1, 0, 256)[0]
    extend(1, 256, e3, EXT)

    for a in range(2):
        for b in range(2):
            n = a * 2 + b
            v = sum(
                mm(w4[n * 128 : (n + 1) * 128, s * 512 : (s + 1) * 512], e3[((a + s) * 3 + b) * 256 : ((a + s) * 3 + b + 2) * 256, :])
                for s in range(2)
            )
            v = v + f2[n * 128 : (n + 1) * 128, :].astype(F32)
            start = ((a + 1) * 4 + b + 1) * 128
            z4[n * 128 : (n + 1) * 128, :], e4[start : start + 128, :] = activated(fenced(v))
    extend(2, 128, e4, EXT)

    RUNS = ((0, 1, 64, 64), (1, 2, 0, 128), (3, 1, 0, 64))
    for a in range(4):
        for b, many, first, size in RUNS:
            base = (a % 2) * 128 + first
            v = sum(
                mm(w5[base : base + size, s * 256 : (s + 1) * 256], e4[((BASE[a] + s) * 4 + BASE[b]) * 128 : ((BASE[a] + s) * 4 + BASE[b] + 2) * 128, :])
                for s in range(2)
            )
            start = (a * 4 + b) * 64
            v = v + f1[start : start + size, :].astype(F32)
            z5[start : start + size, :] = v.astype(BF)

    for a in range(4):
        back = mm(r4t[...], cp[a * 16 : (a + 1) * 16, :])
        start = ((a + 1) * 6 + 1) * 64
        t5[start : start + 256, :] = sloped(back, z5[a * 256 : (a + 1) * 256, :])
    extend(4, 64, t5, CELLS)
    for a in range(2):
        for b in range(2):
            v = sum(
                mm(w5b[:, m * 256 : (m + 1) * 256], t5[((2 * a + m) * 6 + 2 * b) * 64 : ((2 * a + m) * 6 + 2 * b + 4) * 64, 0:CELLS])
                for m in range(4)
            )
            start = ((a + 1) * 4 + b + 1) * 128
            n = a * 2 + b
            t4[start : start + 128, 0:CELLS] = sloped(v, z4[n * 128 : (n + 1) * 128, 0:CELLS])
    copies = begin(4, 1, [t4[((a + 1) * 4 + 1) * 128 : ((a + 1) * 4 + 3) * 128, 0:CELLS] for a in range(2)])

    sums = {}
    for a in range(4):
        for s in range(2):
            for b, many, first, size in RUNS:
                start = ((BASE[a] + s) * 4 + BASE[b]) * 128
                t_start = ((a + 1) * 6 + b + 1) * 64
                product = nt(t5[t_start : t_start + size, 0:CELLS], e4[start : start + 256, 0:CELLS])
                for m in range(many):
                    key = (a % 2, s, (b + m) % 2)
                    block = product[m * 64 : (m + 1) * 64, :]
                    sums[key] = sums[key] + block if key in sums else block

    def reads(parity, tap):
        return 0 if tap in UNDER[parity][0] else 1

    for ta in range(3):
        rowed = [sums[0, reads(0, ta), pb] + sums[1, reads(1, ta), pb] for pb in range(2)]
        for tb in range(3):
            value = sum(rowed[pb][:, reads(pb, tb) * 128 : (reads(pb, tb) + 1) * 128] for pb in range(2))
            start = AT_FINAL + (ta * 3 + tb) * 64
            g_ref[start : start + 64, :] = value

    for b in range(2):
        for u in range(2):
            parts = {}
            for a in range(2):
                for s in range(2):
                    start = ((a + 1) * 4 + b + 1) * 128
                    from_ = ((a + s) * 3 + b + u) * 256
                    parts[a, s] = nt(t4[start : start + 128, 0:CELLS], e3[from_ : from_ + 256, 0:CELLS])
            for ta in range(3):
                value = parts[0, reads(0, ta)] + parts[1, reads(1, ta)]
                for tb in UNDER[b][u]:
                    for half in range(2):
                        start = AT_RETURN + ((ta * 3 + tb) * 2 + half) * 128
                        piece = value[:, half * 128 : (half + 1) * 128]
                        g_ref[start : start + 128, :] = piece if b == 0 else g_ref[start : start + 128, :] + piece

    g_ref[AT_FINAL + 576 : AT_BOTTOM, :] = jnp.zeros((AT_BOTTOM - AT_FINAL - 576, 128), F32)
    sum_step(0, 0)
    sum_step(1, 0)
    total = jnp.zeros((16, 256), F32)
    for a in range(4):
        f5[a * 256 : (a + 1) * 256, :] = activated(z5[a * 256 : (a + 1) * 256, 0:CELLS])[1]
        total = total + nt(cp[a * 16 : (a + 1) * 16, 0:CELLS], f5[a * 256 : (a + 1) * 256, :])
    total = sum(total[b * 4 : (b + 1) * 4, b * 64 : (b + 1) * 64] for b in range(4))
    g_ref[AT_READ:ROWS, :] = jnp.zeros((ROWS - AT_READ, 128), F32)
    g_ref[AT_READ : AT_READ + 4, 0:64] = total

    end(4, 1, copies)
    for a in range(2):
        start = ((a + 1) * 4 + 1) * 128
        t4[start : start + 256, CELLS:EXT] = ring(4, 1, a * 256, 256)[0]
    extend(2, 128, t4, CELLS)
    v = sum(mm(w4b[:, m * 512 : (m + 1) * 512], t4[m * 512 : (m + 1) * 512, 0:CELLS]) for m in range(4))
    far[:, 0:CELLS] = sloped(v, z3[...])
    loaded(cQ2)
    copies = begin(5, 2, [far[:, 0:CELLS]])
    for t in range(9):
        g_ref[AT_BOTTOM + t * 256 : AT_BOTTOM + (t + 1) * 256, :] = nt(far[:, 0:CELLS], e2[t * 128 : (t + 1) * 128, 0:CELLS])
    sum_step(2, 0)
    sum_step(3, 0)
    groups = []
    for a in range(4):
        here = f5[a * 256 : (a + 1) * 256, :]
        value = mm(r4[...], here)
        for t in range(2):
            groups.append(jnp.concatenate([value[b * 4 : (b + 1) * 4, t * 128 : (t + 1) * 128] for b in range(4)], axis=1))
    value = jnp.concatenate(groups, axis=0)
    laid = 0.0
    for _ in range(3):
        piece = value.astype(BF)
        laid = laid + nt(piece, cU[...])
        value = value - piece.astype(F32)
    for a in range(4):
        for t in range(2):
            for r in range(4):
                h = 16 * t + 4 * r + a
                logits_ref[:, h : h + 1, :] = laid[(a * 2 + t) * 4 : (a * 2 + t) * 4 + 2, r * 128 : (r + 1) * 128].reshape(2, 1, 128)
    store(logits_ref, logits_out)
    loaded(cF)
    end(5, 2, copies)
    far[:, 256:384], far[:, 384:512] = ring(5, 2, 0, 256)
    for n in range(9):
        t3[n * 256 : (n + 1) * 256, :] = mm(far[...], cF[n * 512 : (n + 1) * 512, :]).astype(BF)

    through = mm(w3b[...], t3[...]) * 0.25
    for a in range(2):
        for b in range(2):
            n = a * 2 + b
            start = ((a + 1) * 4 + b + 1) * 128
            v = fenced(t4[start : start + 128, :].astype(F32) + through)
            t2[start : start + 128, :] = sloped(v, z2[n * 128 : (n + 1) * 128, :])
    sum_step(0, 1)
    sum_step(1, 1)
    for ta in range(3):
        product = 0.0
        for a in range(2):
            start = ((a + 1) * 4 + 1) * 128
            product = product + nt(e1[(a + ta) * 256 : (a + ta + 1) * 256, 0:CELLS], t2[start : start + 256, 0:CELLS])
        g_ref[AT_SECOND + ta * 192 : AT_SECOND + (ta + 1) * 192, :] = product[0:192, 0:128] + product[64:256, 128:256]
    g_ref[AT_SECOND + 576 : AT_FIRST, :] = jnp.zeros((AT_FIRST - AT_SECOND - 576, 128), F32)
    sum_step(4, 0)
    extend(2, 128, t2, EXT)

    for a in range(2):
        v = sum(mm(w2b[:, ta * 512 : (ta + 1) * 512], t2[(a + ta) * 512 : (a + ta + 1) * 512, :]) for ta in range(3)) * 0.25
        for b in range(2):
            for i in range(2):
                for j in range(2):
                    fa, fb = 2 * a + i, 2 * b + j
                    start = ((fa + 1) * 6 + fb + 1) * 64
                    n = (fa * 4 + fb) * 64
                    t1[start : start + 64, :] = sloped(fenced(t5[start : start + 64, :].astype(F32) + v[b * 64 : (b + 1) * 64, :]), z1[n : n + 64, :])
    sum_step(2, 1)
    sum_step(3, 1)
    for ta in range(3):
        product = 0.0
        for a in range(4):
            for pair in range(2):
                start = ((a + 1) * 6 + 2 * pair + 1) * 64
                from_ = ((a + ta) * 6 + 2 * pair) * 64
                product = product + nt(t1[start : start + 128, 0:CELLS], e0[from_ : from_ + 256, 0:CELLS])
        value = product[0:64, 0:192] + product[64:128, 64:256]
        g_ref[AT_FIRST + ta * 64 : AT_FIRST + (ta + 1) * 64, :] = value[:, 0:128]
        start = AT_FIRST + (192 if ta < 2 else 256)
        g_ref[start : start + 64, ta % 2 * 64 : ta % 2 * 64 + 64] = value[:, 128:192]
    g_ref[AT_FIRST + 256 : AT_FIRST + 320, 64:128] = jnp.zeros((64, 64), F32)
    sum_step(5, 0)
    extend(4, 64, t1, CELLS)

    total = jnp.zeros((64, 256), F32)
    for a in range(4):
        for pair in range(2):
            v = sum(
                mm(w1b[:, ta * 256 : (ta + 1) * 256], t1[((a + ta) * 6 + 2 * pair) * 64 : ((a + ta) * 6 + 2 * pair + 4) * 64, 0:CELLS])
                for ta in range(3)
            )
            start = (a * 4 + 2 * pair) * 64
            fg[start : start + 128, :] = sloped(v, z0[start : start + 128, :])
        start = ((a + 1) * 6 + 1) * 16
        total = total + nt(xb[start : start + 64, 0:CELLS], fg[a * 256 : (a + 1) * 256, :])
    total = sum(total[b * 16 : (b + 1) * 16, b * 64 : (b + 1) * 64] for b in range(4))
    embed_step(0, total)

    def lay(a):
        for t in range(2):
            line = jnp.concatenate([fg[(a * 4 + b) * 64 : (a * 4 + b + 1) * 64, t * 128 : (t + 1) * 128] for b in range(4)], axis=1)
            laid = nt(line, cU[...])
            for r in range(4):
                tall[:, 16 * t + 4 * r + a, :] = laid[:, r * 128 : (r + 1) * 128]

    sum_step(0, 2)
    sum_step(1, 2)
    sum_step(4, 1)
    lay(0)
    lay(1)
    sum_step(2, 2)
    sum_step(3, 2)
    embed_step(1)
    sum_step(5, 1)
    lay(2)
    lay(3)
    features_ref[...] = tall[...].astype(BF)
    store(features_ref, features_out)
    sum_step(4, 2)
    sum_step(0, 3)
    sum_step(1, 3)
    sum_step(5, 2)
    embed_ref[...] = embed_step(2)
    for part in (2, 3, 4, 5):
        sum_step(part, 3)
    for copy in storing:
        copy.wait()


WIDTHS = ((384, 1), (128, 1), (512, 1), (256, 1), (512, 1), (256, 2))


def run_net(counts, *args):
    syn, emb, k1, k2, *rest = args
    k3, k4, k5, rdo, cot = rest
    eye, pick, pick_far, spread, near, far = [jnp.asarray(t, BF) for t in (np.eye(CELLS), PICK, PICK_FAR, SPREAD, SHIFT, SHIFT_FAR)]
    afar = (k1, near, k2.transpose(0, 1, 3, 2), k3, k5, k4, pick_far, far)
    wide, own = (EXT,), (CELLS,)
    blocks = [(16 * 36,) + wide, (64 * 36,) + wide, (1024,) + own, (1024,) + wide, (1024,) + wide, (1024,) + wide]
    blocks += [(512,) + wide, (512,) + wide, (128 * 9,) + wide, (256,) + own, (256 * 9,) + wide, (512,) + wide, (128 * 16,) + wide]
    blocks += [(1024,) + wide, (1024,) + own, (64 * 36,) + wide, (128 * 16,) + wide, (256 * 9,) + wide, (128 * 16,) + wide]
    blocks += [(64 * 36,) + wide, (1024,) + own, (64,) + wide]
    weights = [(384, 96), (128, 768), (128, 768), (256, 768), (128, 1536), (256, 1152), (128, 2304), (512, 1024), (256, 2048), (256, 512), (128, 1024), (16, 256), (256, 16)]
    scratch = [pltpu.VMEM(s, BF) for s in blocks + weights]
    for width, depth in WIDTHS:
        scratch += [pltpu.VMEM((bounds(depth)[3] + 16, width), BF), pltpu.VMEM((128 * depth + 64, width), BF)]
    scratch += [pltpu.VMEM(x.shape, BF) for x in afar]
    scratch += [pltpu.VMEM((256, 512), BF), pltpu.SemaphoreType.DMA((8,)), pltpu.VMEM((2, 32, 128), F32), pltpu.VMEM((64, 32, 128), BF)]
    scratch += [pltpu.SemaphoreType.DMA((2 + len(PARTS),))]
    scratch += [pltpu.SemaphoreType.DMA((len(WIDTHS), 8)), pltpu.SemaphoreType.DMA((len(WIDTHS), 8))]
    scratch += [pltpu.VMEM((ROWS, 128), F32), pltpu.VMEM((ROWS, 128), BF), pltpu.VMEM((64, 32, 128), F32)]
    n_row, n_col = counts
    most = max(n_row, n_col)
    for _, size, first in PARTS:
        n1, n2 = (n_row, n_col) if first == "row" else (n_col, n_row)
        c1 = size // n1
        scratch += [pltpu.VMEM((size, 128), BF), pltpu.VMEM((n1 - 1, c1, 128), BF), pltpu.VMEM((n2, c1, 128), BF)]
    scratch += [pltpu.SemaphoreType.DMA((len(PARTS), 3, most)), pltpu.SemaphoreType.DMA((len(PARTS), 3, most))]
    scratch += [pltpu.VMEM((n_row, 16, 64), F32), pltpu.VMEM((n_col, 16, 64), F32)]
    scratch += [pltpu.SemaphoreType.DMA((2, most)), pltpu.SemaphoreType.DMA((2, most))]
    vmem, hbm = pl.BlockSpec(memory_space=pltpu.VMEM), pl.BlockSpec(memory_space=pl.ANY)
    return pl.pallas_call(
        functools.partial(net_kernel, counts),
        out_shape=(
            jax.ShapeDtypeStruct((2, 32, 128), F32),
            jax.ShapeDtypeStruct((64, 32, 128), BF),
            jax.ShapeDtypeStruct((16, 64), F32),
            jax.ShapeDtypeStruct((ROWS, 128), BF),
        ),
        in_specs=[vmem] * 7 + [hbm] * 8,
        out_specs=(hbm, hbm, vmem, hbm),
        scratch_shapes=scratch,
        compiler_params=pltpu.CompilerParams(collective_id=1, has_side_effects=True, vmem_limit_bytes=56 * 2**20),
    )(syn, emb.T, rdo, cot, eye, pick, spread, *afar)


def out_kernel(logits, features, embed, grads, *refs):
    outs, (g, mids, loads, stores) = refs[:9], (refs[9], refs[10:16], refs[16], refs[17])
    spans = ((0, AT_BOTTOM), (AT_BOTTOM, AT_SECOND), (AT_SECOND, ROWS))
    pulls = [pltpu.make_async_copy(grads.at[a:b], g.at[a:b], loads.at[n]) for n, (a, b) in enumerate(spans)]
    for copy in pulls:
        copy.start()
    pushes = [pltpu.make_async_copy(x, outs[n], stores.at[n]) for n, x in enumerate((logits, features, embed))]
    for copy in pushes:
        copy.start()

    def push(n):
        pushes.append(pltpu.make_async_copy(mids[n - 3], outs[n], stores.at[n]))
        pushes[-1].start()

    m_first, m_second, m_bottom, m_return, m_final, m_read = mids
    pulls[0].wait()
    for t in range(9):
        ta, tb = t // 3, t % 3
        for half in range(2):
            start = AT_RETURN + (t * 2 + half) * 128
            m_return[ta, tb, :, half * 128 : (half + 1) * 128] = g[start : start + 128, :].astype(F32)
        m_final[ta, tb] = g[AT_FINAL + t * 64 : AT_FINAL + (t + 1) * 64, :].astype(F32)
    push(6)
    push(7)
    pulls[1].wait()
    for t in range(9):
        m_bottom[t // 3, t % 3] = g[AT_BOTTOM + t * 256 : AT_BOTTOM + (t + 1) * 256, :].astype(F32)
    push(5)
    pulls[2].wait()
    for t in range(9):
        ta, tb = t // 3, t % 3
        m_second[ta, tb] = g[AT_SECOND + t * 64 : AT_SECOND + (t + 1) * 64, :].astype(F32)
        start, low = (AT_FIRST + ta * 64, tb * 64) if tb < 2 else (AT_FIRST + (192 if ta < 2 else 256), ta % 2 * 64)
        m_first[ta, tb] = g[start : start + 64, low : low + 64].astype(F32)
    m_read[...] = g[AT_READ : AT_READ + 16, 0:64].astype(F32)[0:2]
    push(3)
    push(4)
    push(8)
    for copy in pushes:
        copy.wait()


def write_out(logits, features, embed, g):
    shapes = [(2, 32, 128), (64, 32, 128), (16, 64), (3, 3, 64, 64), (3, 3, 64, 128), (3, 3, 256, 128), (3, 3, 128, 256), (3, 3, 64, 128), (2, 64)]
    hbm = pl.BlockSpec(memory_space=pl.ANY)
    outs = pl.pallas_call(
        out_kernel,
        out_shape=tuple(jax.ShapeDtypeStruct(s, BF if n == 1 else F32) for n, s in enumerate(shapes)),
        in_specs=[hbm] * 4,
        out_specs=(hbm,) * 9,
        scratch_shapes=[pltpu.VMEM((ROWS, 128), BF)]
        + [pltpu.VMEM(s, F32) for s in shapes[3:]]
        + [pltpu.SemaphoreType.DMA((3,)), pltpu.SemaphoreType.DMA((9,))],
        compiler_params=pltpu.CompilerParams(vmem_limit_bytes=60 * 2**20),
    )(logits, features, embed, g)
    outs = list(outs)
    outs[2] = outs[2].T
    outs[4] = outs[4].transpose(0, 1, 3, 2)
    return tuple(outs)


def on_device(counts, *args):
    return write_out(*run_net(counts, *args))


def solution(mesh):
    counts = (mesh.shape["row"], mesh.shape["col"])
    cells = P(None, ("batch", "row"), "col")
    in_specs = (P(("batch", "row"), "col"),) + (P(),) * 7 + (cells,)
    out_specs = (cells, cells, P("batch", None)) + (P("batch", None, None, None),) * 5 + (P("batch", None),)
    return jax.shard_map(
        functools.partial(on_device, counts), mesh=mesh, in_specs=in_specs, out_specs=out_specs, check_vma=False
    )
```

```python
import functools

import jax
import jax.numpy as jnp
import numpy as np
from jax import lax
from jax.experimental import pallas as pl
from jax.experimental.pallas import tpu as pltpu
from jax.sharding import PartitionSpec as P

BF, F32 = jnp.bfloat16, jnp.float32
MESH = pl.DeviceIdType.MESH

DEEP, WIDE = 8, 32
CELLS = DEEP * WIDE
EXT = CELLS + 128

ROWS = 6272
PARTS = (
    (0, 1408, True, "x", "col"),
    (1408, 1536, True, "col", "x"),
    (2944, 1024, True, "x", "col"),
    (3968, 1280, True, "col", "x"),
    (5248, 640, False, "row", "col"),
    (5888, 384, False, "col", "row"),
)
AT_RETURN, AT_FINAL, AT_BOTTOM, AT_SECOND, AT_FIRST, AT_READ = 0, 2304, 2944, 5248, 5888, 6208


def ranged(values, start, size):
    return values.at[pl.ds(pl.multiple_of(start, 16), size), :]


def bounds(depth):
    left = 2 * WIDE * depth
    return WIDE * depth, left, left + 16, left + 32


def lane_of(r, q, depth):
    if not (-depth <= r < DEEP + depth and -depth <= q < WIDE + depth):
        return None
    row_in, col_in = 0 <= r < DEEP, 0 <= q < WIDE
    down, left, right, corner = bounds(depth)
    if row_in and col_in:
        return r * WIDE + q
    i = r + depth if r < 0 else r - DEEP
    j = q + depth if q < 0 else q - WIDE
    if col_in:
        return CELLS + (0 if r < 0 else down) + i * WIDE + q
    if row_in:
        return CELLS + (left if q < 0 else right) + j * DEEP + r
    return CELLS + corner + CORNERS[(-1 if r < 0 else 1, -1 if q < 0 else 1)] * depth * depth + i * depth + j


def shift_tables(depth, size):
    tables = []
    for dr in (-1, 0, 1):
        for dc in (-1, 0, 1):
            m = np.zeros((size, EXT), np.float32)
            for r in range(-1, DEEP + 1):
                for q in range(-1, WIDE + 1):
                    source = lane_of(r + dr, q + dc, depth)
                    if source is not None:
                        m[source, lane_of(r, q, 1)] = 1
            tables.append(m)
    return np.concatenate(tables)


def pick_table(depth):
    down, left, right, corner = bounds(depth)
    m = np.zeros((corner + 16, CELLS), np.float32)
    for i in range(depth):
        for q in range(WIDE):
            m[i * WIDE + q, i * WIDE + q] = 1
            m[down + i * WIDE + q, (DEEP - depth + i) * WIDE + q] = 1
        for r in range(DEEP):
            m[left + i * DEEP + r, r * WIDE + i] = 1
            m[right + i * DEEP + r, r * WIDE + WIDE - depth + i] = 1
        for j in range(depth):
            for k, (r, q) in enumerate(((0, 0), (0, WIDE - depth), (DEEP - depth, 0), (DEEP - depth, WIDE - depth))):
                m[corner + k * depth * depth + i * depth + j, (r + i) * WIDE + q + j] = 1
    return m


CORNERS = {(-1, -1): 3, (-1, 1): 2, (1, -1): 1, (1, 1): 0}


def spread_table():
    m = np.zeros((512, 512), np.float32)
    for r in range(4):
        for w in range(128):
            m[r * 128 + w, (w % 4) * 128 + r * WIDE + w // 4] = 1
    return m


SHIFT = shift_tables(1, EXT)
SHIFT_FAR = shift_tables(2, 512)
PICK, PICK_FAR = pick_table(1), pick_table(2)
SPREAD = spread_table()

UNDER = (((0,), (1, 2)), ((0, 1), (2,)))
OVER = ((2,), (1, 2), (0, 1), (0,))
BASE = (0, 1, 1, 2)


def mm(a, b):
    return jnp.dot(a, b, preferred_element_type=F32)


def nt(a, b):
    return lax.dot_general(a, b, (((1,), (1,)), ((), ())), preferred_element_type=F32)


def logistic(z):
    return 0.5 + 0.5 * jnp.tanh(0.5 * z)


def activated(v):
    stored = v.astype(BF)
    z = stored.astype(F32)
    return stored, (z * logistic(z)).astype(BF)


def sloped(incoming, stored):
    z = stored.astype(F32)
    s = logistic(z)
    return (incoming * (s * (1.0 + z * (1.0 - s)))).astype(BF)


def remote(src, dst, send, recv, target):
    return pltpu.make_async_remote_copy(
        src_ref=src, dst_ref=dst, send_sem=send, recv_sem=recv, device_id=target, device_id_type=MESH
    )


SIDES = ((-1, -1), (-1, 1), (1, -1), (1, 1), (0, -1), (0, 1), (-1, 0), (1, 0))


def net_kernel(counts, *refs):
    it = iter(refs)

    def take(n):
        return [next(it) for _ in range(n)]

    syn, embt, rdo, cot, eye, cQ, cU = take(7)
    afar = take(8)
    logits_out, features_out, embed_ref, grads_out = take(4)
    xb, e0, z0, z1, f1, e1, z2, f2, e2, z3, e3, z4, e4, z5, f5, t5, t4, t3, t2, t1, fg, cp = take(22)
    w0, w1, w1b, w2, w2b, w3, w3b, w4, w4b, w5, w5b, r4, r4t = take(13)
    halos = [take(2) for _ in WIDTHS]
    near = take(8)
    k1, cS, k2t, k3, k5, k4, cQ2, cF = near
    far, wide2, loads, logits_ref, features_ref, stores = take(6)
    sends, recvs = take(2)
    g_ref, whole, tall = take(3)
    stages = [take(6) for _ in PARTS]
    sum_sends, sum_recvs, embed_row, embed_col, embed_sends, embed_recvs = take(6)

    n_row, n_col = counts
    row, col = lax.axis_index("row"), lax.axis_index("col")
    there = {
        (-1, 0): row > 0,
        (1, 0): row < n_row - 1,
        (0, -1): col > 0,
        (0, 1): col < n_col - 1,
    }
    for dr in (-1, 1):
        for dc in (-1, 1):
            there[dr, dc] = jnp.logical_and(there[dr, 0], there[0, dc])

    def place(dr, dc):
        return {"row": (row + dr + n_row) % n_row, "col": (col + dc + n_col) % n_col}

    loading = {}
    for n, (source, target) in enumerate(zip(afar, near)):
        loading[id(target)] = pltpu.make_async_copy(source, target, loads.at[n])
        loading[id(target)].start()

    def loaded(*targets):
        for target in targets:
            loading[id(target)].wait()

    storing = []

    def store(source, target):
        storing.append(pltpu.make_async_copy(source, target, stores.at[len(storing)]))
        storing[-1].start()

    partners = [(d, 0) for d in range(1, n_row)] + [(0, d) for d in range(1, n_col)] + list(SIDES[:4])
    barrier = pltpu.get_barrier_semaphore()
    for partner in partners:
        pl.semaphore_signal(barrier, inc=1, device_id=place(*partner), device_id_type=MESH)

    lane = lax.broadcasted_iota(jnp.int32, (1, 128), 1)
    sixteen = lax.broadcasted_iota(jnp.int32, (16, 1), 0)

    def inside(depth):
        down, left, right, corner = bounds(depth)
        spans = [(0, down, (-1, 0)), (down, left, (1, 0)), (left, left + DEEP * depth, (0, -1)), (right, right + DEEP * depth, (0, 1))]
        spans += [(corner + k * depth * depth, corner + (k + 1) * depth * depth, side) for side, k in CORNERS.items()]
        masks = []
        for tile in range(depth):
            at = lane + tile * 128
            keep = lane < 0
            for low, high, side in spans:
                keep = jnp.logical_or(keep, jnp.logical_and(jnp.logical_and(at >= low, at < high), there[side]))
            masks.append(keep)
        return masks

    near_masks, far_masks = inside(1), inside(2)

    def fenced(v):
        return jnp.concatenate([v[:, :CELLS], jnp.where(near_masks[0], v[:, CELLS:], 0.0)], axis=1)

    def begin(n, depth, pieces, ahead=None):
        out, into = halos[n]
        down, left, right, corner = bounds(depth)
        pick = (cQ if depth == 1 else cQ2)[...]
        start = 0
        for piece in pieces:
            out[:, start : start + piece.shape[0]] = nt(pick, piece).astype(BF)
            start += piece.shape[0]
        size = {(-1, 0): (0, down, down), (1, 0): (down, left, 0), (0, -1): (left, right, right), (0, 1): (right, corner, left)}
        copies = []
        for k, (dr, dc) in enumerate(SIDES):
            if (dr, dc) in size:
                low, high, target = size[dr, dc]
            else:
                low, high = corner, corner + 16
                target = 128 * depth + 16 * CORNERS[-dr, -dc]
            copies.append(
                remote(out.at[low:high], into.at[target : target + high - low], sends.at[n, k], recvs.at[n, k], place(dr, dc))
            )
        if ahead is not None:
            ahead()
        for copy in copies:
            copy.start()
        return copies

    def end(n, depth, copies):
        into = halos[n][1]
        corner = bounds(depth)[3]
        for copy in copies:
            copy.wait()
        ends = 0.0
        for k in range(4):
            tile = into[128 * depth + 16 * k : 128 * depth + 16 * (k + 1), :].astype(F32)
            ends = ends + jnp.where(sixteen // (depth * depth) == k, tile, 0.0)
        into[corner : corner + 16, :] = ends.astype(BF)

    def ring(n, depth, start, width):
        into = halos[n][1]
        tiles = []
        for tile, keep in enumerate(near_masks if depth == 1 else far_masks):
            turned = nt(eye[0:width, 0:width], into[tile * 128 : (tile + 1) * 128, start : start + width])
            tiles.append(jnp.where(keep, turned, 0.0).astype(BF))
        return tiles

    def extend(p, width, ref, size):
        for ea in range(p + 2):
            for eb in range(p + 2):
                dr, dc = (ea > p) - (ea < 1), (eb > p) - (eb < 1)
                if (dr, dc) == (0, 0):
                    continue
                start = (((ea - 1) % p + 1) * (p + 2) + (eb - 1) % p + 1) * width
                at = (dr * 3 + dc + 4) * EXT
                moved = mm(ref[start : start + width, :], cS[at : at + EXT, 0:size])
                start = (ea * (p + 2) + eb) * width
                ref[start : start + width, 0:size] = moved.astype(BF)

    core, n_x = row % 2, n_row // 2
    ways = {
        "row": (row, n_row, lambda d: place(d, 0)),
        "col": (col, n_col, lambda d: place(0, d)),
        "x": (row // 2, n_x, lambda d: {"row": (row // 2 + d) % n_x * 2 + core}),
    }
    flying = {}

    def sum_step(part, step):
        start, size, paired, first, second = PARTS[part]
        s0, r0, held, s1, r1, r2 = stages[part]
        me1, n1, to1 = ways[first]
        me2, n2, to2 = ways[second]
        for copy in flying.pop(part, ()):
            copy.wait()
        if step == 5:
            store(whole.at[start : start + size], grads_out.at[start : start + size])
            return
        half = size // 2 if paired else size
        base = start + core * half if paired else start
        c1 = half // n1
        own = pl.ds(pl.multiple_of(base + me1 * c1, 16), c1)
        partner = {"row": row + 1 - 2 * core}
        moves = []
        if step == 0:
            s0[...] = g_ref[pl.ds(pl.multiple_of(start + (1 - core) * half, 16), half), :].astype(BF)
            moves.append((s0, r0, partner))
        elif step == 1:
            total = g_ref[pl.ds(pl.multiple_of(base, 16), half), :] if paired else g_ref[base : base + half, :]
            if paired:
                total = total + r0[...].astype(F32)
            held[...] = total
            s1[...] = total.astype(BF)
            moves = [(ranged(s1, (me1 + d) % n1 * c1, c1), r1.at[d - 1], to1(d)) for d in range(1, n1)]
        elif step == 2:
            total = held[pl.ds(pl.multiple_of(me1 * c1, 16), c1), :]
            for d in range(n1 - 1):
                total = total + r1[d].astype(F32)
            r2[me2] = total.astype(BF)
            moves = [(r2.at[me2], r2.at[me2], to2(d)) for d in range(1, n2)]
        elif step == 3:
            whole[own, :] = sum(r2[d].astype(F32) for d in range(n2)).astype(BF)
            moves = [(whole.at[own, :], whole.at[own, :], to1(d)) for d in range(1, n1)]
        elif paired:
            mine = ranged(whole, base, half)
            moves.append((mine, mine, partner))
        copies = [
            remote(src, dst, sum_sends.at[part, step, k], sum_recvs.at[part, step, k], to) for k, (src, dst, to) in enumerate(moves)
        ]
        for copy in copies:
            copy.start()
        flying[part] = copies

    def embed_step(step, value=None):
        if step > 0:
            for copy in flying.pop("embed"):
                copy.wait()
            slots = embed_row if step == 1 else embed_col
            value = sum(slots[d] for d in range(slots.shape[0]))
        if step == 2:
            return value
        slots, (me, count, to) = (embed_row, ways["row"]) if step == 0 else (embed_col, ways["col"])
        slots[me] = value
        copies = [
            remote(slots.at[me], slots.at[me], embed_sends.at[step, d], embed_recvs.at[step, d], to(d)) for d in range(1, count)
        ]
        for copy in copies:
            copy.start()
        flying["embed"] = copies

    bit = lax.broadcasted_iota(jnp.int32, (16, 1), 0)
    groups = []
    for a in range(4):
        for t in range(2):
            line = [(syn[16 * t + 4 * r + a : 16 * t + 4 * r + a + 1, :] >> bit) & 1 for r in range(4)]
            groups.append(jnp.concatenate(line, axis=1))
    bits = jnp.concatenate(groups, axis=0).astype(F32).astype(BF)
    phased = mm(bits, cU[...]).astype(BF)
    for a in range(4):
        for t in range(2):
            for b in range(4):
                start = ((a + 1) * 6 + b + 1) * 16
                xb[start : start + 16, t * 128 : (t + 1) * 128] = phased[(a * 2 + t) * 16 : (a * 2 + t + 1) * 16, b * 128 : (b + 1) * 128]
    wide = cot[...].astype(F32)
    groups = []
    for a in range(4):
        for t in range(2):
            line = jnp.concatenate([wide[:, 16 * t + 4 * r + a, :] for r in range(4)], axis=1)
            groups.append(jnp.concatenate([line, jnp.zeros((6, 512), F32)], axis=0))
    phased = mm(jnp.concatenate(groups, axis=0).astype(BF), cU[...])
    for a in range(4):
        for t in range(2):
            start = (a * 2 + t) * 8
            pieces = [phased[start : start + 4, b * 128 : (b + 1) * 128] for b in range(4)]
            cp[a * 16 : (a + 1) * 16, t * 128 : (t + 1) * 128] = jnp.concatenate(pieces, axis=0).astype(BF)

    inner = [((a + 1) * 6 + 1) * 16 for a in range(4)]
    pieces = [jnp.concatenate([xb[i : i + 64, 0:CELLS] for i in inner], axis=0), cp[:, 0:CELLS]]
    copies = begin(0, 1, pieces, lambda: pl.semaphore_wait(barrier, len(partners)))

    def beside(blocks, i, blank):
        return jnp.concatenate(blocks + [blank] if i == 0 else [blank] + blocks, axis=0)

    def added(k, rows, cols):
        return sum(k[ta, tb].astype(F32) for ta in rows for tb in cols).astype(BF)

    def arrange_first():
        repeat = (lax.broadcasted_iota(jnp.int32, (16, 96), 1) % 16 == lax.broadcasted_iota(jnp.int32, (16, 96), 0)).astype(F32).astype(BF)
        tiled = mm(nt(eye[:64, :64], embt[...]).astype(BF), repeat)
        own = lax.broadcasted_iota(jnp.int32, (64, 96), 1) // 16
        for j in range(6):
            w0[j * 64 : (j + 1) * 64, :] = jnp.where(own == j, tiled, 0.0).astype(BF)
        for ta in range(3):
            for i in range(2):
                w1[i * 64 : (i + 1) * 64, ta * 256 : (ta + 1) * 256] = sum(
                    mm(k1[ta, tb], eye[(tb + i) * 64 : (tb + i + 1) * 64, :]) for tb in range(3)
                ).astype(BF)

    def arrange_second():
        blank, empty = jnp.zeros((64, 128), BF), jnp.zeros((64, 64), BF)
        for ta in range(3):
            for i in range(2):
                line = beside([k2t[ta, tb] for tb in range(3)], i, blank)
                w2[i * 128 : (i + 1) * 128, ta * 256 : (ta + 1) * 256] = nt(eye[:128, :128], line).astype(BF)
                for tb in range(3):
                    w2b[i * 64 : (i + 1) * 64, ta * 512 + (tb + i) * 128 : ta * 512 + (tb + i + 1) * 128] = k2t[2 - ta, 2 - tb]
                hole = ta * 512 + (384 if i == 0 else 0)
                w2b[i * 64 : (i + 1) * 64, hole : hole + 128] = blank
                line = beside([k1[2 - ta, 2 - tb] for tb in range(3)], i, empty)
                w1b[i * 64 : (i + 1) * 64, ta * 256 : (ta + 1) * 256] = nt(eye[:64, :64], line).astype(BF)

    def arrange_bottom():
        for t in range(9):
            w3[:, t * 128 : (t + 1) * 128] = k3[t // 3, t % 3]
            w3b[:, t * 256 : (t + 1) * 256] = nt(eye[:128, :128], k3[2 - t // 3, 2 - t % 3]).astype(BF)

    def arrange_return():
        for pa in range(2):
            for pb in range(2):
                for s in range(2):
                    for u in range(2):
                        block = added(k4, UNDER[pa][s], UNDER[pb][u])
                        w4[(pa * 2 + pb) * 128 : (pa * 2 + pb + 1) * 128, (s * 2 + u) * 256 : (s * 2 + u + 1) * 256] = block
                        at = OVER.index(UNDER[pa][s]) * 4 + OVER.index(UNDER[pb][u])
                        w4b[:, at * 128 : (at + 1) * 128] = nt(eye[...], block).astype(BF)

    def arrange_final():
        for pa in range(2):
            for pb in range(2):
                for s in range(2):
                    for u in range(2):
                        start = pa * 128 + (1 - pb) * 64
                        w5[start : start + 64, (s * 2 + u) * 128 : (s * 2 + u + 1) * 128] = added(k5, UNDER[pa][s], UNDER[pb][u])
        for ea in range(4):
            for pair in range(2):
                stack = jnp.concatenate([added(k5, OVER[ea], OVER[2 * pair + i]) for i in range(2)], axis=0)
                at = ea * 2 + pair
                w5b[:, at * 128 : (at + 1) * 128] = nt(eye[:128, :128], stack).astype(BF)

    def arrange_readout():
        repeat = (lax.broadcasted_iota(jnp.int32, (64, 256), 1) % 64 == lax.broadcasted_iota(jnp.int32, (64, 256), 0)).astype(F32).astype(BF)
        tiled = mm(rdo[...], repeat)
        tiled = jnp.concatenate([tiled, jnp.zeros((2, 256), F32)] * 4, axis=0)
        own = lax.broadcasted_iota(jnp.int32, (16, 256), 1) // 64 == lax.broadcasted_iota(jnp.int32, (16, 256), 0) // 4
        r4[...] = jnp.where(own, tiled, 0.0).astype(BF)
        r4t[...] = nt(eye[...], r4[...]).astype(BF)

    loaded(k1)
    arrange_first()
    arrange_readout()
    loaded(cS)
    end(0, 1, copies)
    (tile,) = ring(0, 1, 0, 256)
    for a in range(4):
        xb[inner[a] : inner[a] + 64, CELLS:EXT] = tile[a * 64 : (a + 1) * 64, :]
    cp[:, CELLS:EXT] = ring(0, 1, 256, 64)[0]
    extend(4, 16, xb, EXT)

    for ea in range(6):
        stored, active = activated(mm(w0[...], xb[ea * 96 : (ea + 1) * 96, :]))
        e0[ea * 384 : (ea + 1) * 384, :] = active
        if 1 <= ea <= 4:
            z0[(ea - 1) * 256 : ea * 256, :] = stored[64:320, 0:CELLS]

    for a in range(4):
        for pair in range(2):
            v = sum(
                mm(w1[:, ta * 256 : (ta + 1) * 256], e0[((a + ta) * 6 + 2 * pair) * 64 : ((a + ta) * 6 + 2 * pair + 4) * 64, :])
                for ta in range(3)
            )
            start = (a * 4 + 2 * pair) * 64
            z1[start : start + 128, :], f1[start : start + 128, :] = activated(fenced(v))

    def pooled(ref, side, width, a, b, size):
        spots = [((2 * a + i) * side + 2 * b + j) * width for i in range(2) for j in range(2)]
        return (sum(ref[s : s + width, 0:size].astype(F32) for s in spots) * 0.25).astype(BF)

    for a in range(2):
        for b in range(2):
            start = ((a + 1) * 4 + b + 1) * 64
            e1[start : start + 64, :] = pooled(f1, 4, 64, a, b, EXT)
    extend(2, 64, e1, CELLS)
    loaded(k2t)
    arrange_second()

    for a in range(2):
        v = sum(mm(w2[:, ta * 256 : (ta + 1) * 256], e1[(a + ta) * 256 : (a + ta + 1) * 256, 0:CELLS]) for ta in range(3))
        z2[a * 256 : (a + 1) * 256, 0:CELLS], f2[a * 256 : (a + 1) * 256, 0:CELLS] = activated(v)
    e2[4 * 128 : 5 * 128, 0:CELLS] = pooled(f2, 2, 128, 0, 0, CELLS)
    loaded(cQ2)
    copies = begin(1, 2, [e2[4 * 128 : 5 * 128, 0:CELLS]])
    later = begin(2, 1, [z2[0:256, 0:CELLS], z2[256:512, 0:CELLS]])
    loaded(k3, k5)
    arrange_bottom()
    arrange_final()
    loaded(k4)
    arrange_return()
    loaded(cF)
    end(1, 2, copies)
    wide2[:, 0:CELLS] = e2[4 * 128 : 5 * 128, 0:CELLS]
    wide2[:, 256:384], wide2[:, 384:512] = ring(1, 2, 0, 128)
    for n in range(9):
        e2[n * 128 : (n + 1) * 128, :] = mm(wide2[...], cF[n * 512 : (n + 1) * 512, :]).astype(BF)

    stored, e3[4 * 256 : 5 * 256, :] = activated(fenced(mm(w3[...], e2[...])))
    z3[...] = stored[:, 0:CELLS]
    end(2, 1, later)
    for a in range(2):
        z2[a * 256 : (a + 1) * 256, CELLS:EXT] = ring(2, 1, a * 256, 256)[0]
        f2[a * 256 : (a + 1) * 256, CELLS:EXT] = activated(z2[a * 256 : (a + 1) * 256, CELLS:EXT])[1]
    extend(1, 256, e3, EXT)

    for a in range(2):
        for b in range(2):
            n = a * 2 + b
            v = sum(
                mm(w4[n * 128 : (n + 1) * 128, s * 512 : (s + 1) * 512], e3[((a + s) * 3 + b) * 256 : ((a + s) * 3 + b + 2) * 256, :])
                for s in range(2)
            )
            v = v + f2[n * 128 : (n + 1) * 128, :].astype(F32)
            start = ((a + 1) * 4 + b + 1) * 128
            z4[n * 128 : (n + 1) * 128, :], e4[start : start + 128, :] = activated(fenced(v))
    extend(2, 128, e4, EXT)

    RUNS = ((0, 1, 64, 64), (1, 2, 0, 128), (3, 1, 0, 64))
    for a in range(4):
        for b, many, first, size in RUNS:
            base = (a % 2) * 128 + first
            v = sum(
                mm(w5[base : base + size, s * 256 : (s + 1) * 256], e4[((BASE[a] + s) * 4 + BASE[b]) * 128 : ((BASE[a] + s) * 4 + BASE[b] + 2) * 128, :])
                for s in range(2)
            )
            start = (a * 4 + b) * 64
            v = v + f1[start : start + size, :].astype(F32)
            z5[start : start + size, :] = v.astype(BF)

    for a in range(4):
        back = mm(r4t[...], cp[a * 16 : (a + 1) * 16, :])
        start = ((a + 1) * 6 + 1) * 64
        t5[start : start + 256, :] = sloped(back, z5[a * 256 : (a + 1) * 256, :])
    extend(4, 64, t5, CELLS)
    for a in range(2):
        for b in range(2):
            v = sum(
                mm(w5b[:, m * 256 : (m + 1) * 256], t5[((2 * a + m) * 6 + 2 * b) * 64 : ((2 * a + m) * 6 + 2 * b + 4) * 64, 0:CELLS])
                for m in range(4)
            )
            start = ((a + 1) * 4 + b + 1) * 128
            n = a * 2 + b
            t4[start : start + 128, 0:CELLS] = sloped(v, z4[n * 128 : (n + 1) * 128, 0:CELLS])
    copies = begin(3, 1, [t4[((a + 1) * 4 + 1) * 128 : ((a + 1) * 4 + 3) * 128, 0:CELLS] for a in range(2)])

    sums = {}
    for a in range(4):
        for s in range(2):
            for b, many, first, size in RUNS:
                start = ((BASE[a] + s) * 4 + BASE[b]) * 128
                t_start = ((a + 1) * 6 + b + 1) * 64
                product = nt(t5[t_start : t_start + size, 0:CELLS], e4[start : start + 256, 0:CELLS])
                for m in range(many):
                    key = (a % 2, s, (b + m) % 2)
                    block = product[m * 64 : (m + 1) * 64, :]
                    sums[key] = sums[key] + block if key in sums else block

    def reads(parity, tap):
        return 0 if tap in UNDER[parity][0] else 1

    for ta in range(3):
        rowed = [sums[0, reads(0, ta), pb] + sums[1, reads(1, ta), pb] for pb in range(2)]
        for tb in range(3):
            value = sum(rowed[pb][:, reads(pb, tb) * 128 : (reads(pb, tb) + 1) * 128] for pb in range(2))
            start = AT_FINAL + (ta * 3 + tb) * 64
            g_ref[start : start + 64, :] = value

    for b in range(2):
        for u in range(2):
            parts = {}
            for a in range(2):
                for s in range(2):
                    start = ((a + 1) * 4 + b + 1) * 128
                    from_ = ((a + s) * 3 + b + u) * 256
                    parts[a, s] = nt(t4[start : start + 128, 0:CELLS], e3[from_ : from_ + 256, 0:CELLS])
            for ta in range(3):
                value = parts[0, reads(0, ta)] + parts[1, reads(1, ta)]
                for tb in UNDER[b][u]:
                    for half in range(2):
                        start = AT_RETURN + ((ta * 3 + tb) * 2 + half) * 128
                        piece = value[:, half * 128 : (half + 1) * 128]
                        g_ref[start : start + 128, :] = piece if b == 0 else g_ref[start : start + 128, :] + piece

    g_ref[AT_FINAL + 576 : AT_BOTTOM, :] = jnp.zeros((AT_BOTTOM - AT_FINAL - 576, 128), F32)
    sum_step(0, 0)
    sum_step(1, 0)
    total = jnp.zeros((16, 256), F32)
    for a in range(4):
        f5[a * 256 : (a + 1) * 256, :] = activated(z5[a * 256 : (a + 1) * 256, 0:CELLS])[1]
        total = total + nt(cp[a * 16 : (a + 1) * 16, 0:CELLS], f5[a * 256 : (a + 1) * 256, :])
    total = sum(total[b * 4 : (b + 1) * 4, b * 64 : (b + 1) * 64] for b in range(4))
    g_ref[AT_READ:ROWS, :] = jnp.zeros((ROWS - AT_READ, 128), F32)
    g_ref[AT_READ : AT_READ + 4, 0:64] = total

    end(3, 1, copies)
    sum_step(0, 1)
    sum_step(1, 1)
    for a in range(2):
        start = ((a + 1) * 4 + 1) * 128
        t4[start : start + 256, CELLS:EXT] = ring(3, 1, a * 256, 256)[0]
    extend(2, 128, t4, CELLS)
    v = sum(mm(w4b[:, m * 512 : (m + 1) * 512], t4[m * 512 : (m + 1) * 512, 0:CELLS]) for m in range(4))
    far[:, 0:CELLS] = sloped(v, z3[...])
    copies = begin(4, 2, [far[:, 0:CELLS]])
    for t in range(9):
        g_ref[AT_BOTTOM + t * 256 : AT_BOTTOM + (t + 1) * 256, :] = nt(far[:, 0:CELLS], e2[t * 128 : (t + 1) * 128, 0:CELLS])
    sum_step(2, 0)
    sum_step(3, 0)
    groups = []
    for a in range(4):
        here = f5[a * 256 : (a + 1) * 256, :]
        value = mm(r4[...], here)
        for t in range(2):
            groups.append(jnp.concatenate([value[b * 4 : (b + 1) * 4, t * 128 : (t + 1) * 128] for b in range(4)], axis=1))
    value = jnp.concatenate(groups, axis=0)
    laid = 0.0
    for _ in range(3):
        piece = value.astype(BF)
        laid = laid + nt(piece, cU[...])
        value = value - piece.astype(F32)
    for a in range(4):
        for t in range(2):
            for r in range(4):
                h = 16 * t + 4 * r + a
                logits_ref[:, h : h + 1, :] = laid[(a * 2 + t) * 4 : (a * 2 + t) * 4 + 2, r * 128 : (r + 1) * 128].reshape(2, 1, 128)
    store(logits_ref, logits_out)
    sum_step(2, 1)
    sum_step(3, 1)
    end(4, 2, copies)
    far[:, 256:384], far[:, 384:512] = ring(4, 2, 0, 256)
    for n in range(9):
        t3[n * 256 : (n + 1) * 256, :] = mm(far[...], cF[n * 512 : (n + 1) * 512, :]).astype(BF)

    sum_step(0, 2)
    sum_step(1, 2)
    through = mm(w3b[...], t3[...]) * 0.25
    for a in range(2):
        for b in range(2):
            n = a * 2 + b
            start = ((a + 1) * 4 + b + 1) * 128
            v = fenced(t4[start : start + 128, :].astype(F32) + through)
            t2[start : start + 128, :] = sloped(v, z2[n * 128 : (n + 1) * 128, :])
    for ta in range(3):
        product = 0.0
        for a in range(2):
            start = ((a + 1) * 4 + 1) * 128
            product = product + nt(e1[(a + ta) * 256 : (a + ta + 1) * 256, 0:CELLS], t2[start : start + 256, 0:CELLS])
        g_ref[AT_SECOND + ta * 192 : AT_SECOND + (ta + 1) * 192, :] = product[0:192, 0:128] + product[64:256, 128:256]
    g_ref[AT_SECOND + 576 : AT_FIRST, :] = jnp.zeros((AT_FIRST - AT_SECOND - 576, 128), F32)
    sum_step(4, 1)
    extend(2, 128, t2, EXT)

    for a in range(2):
        v = sum(mm(w2b[:, ta * 512 : (ta + 1) * 512], t2[(a + ta) * 512 : (a + ta + 1) * 512, :]) for ta in range(3)) * 0.25
        for b in range(2):
            for i in range(2):
                for j in range(2):
                    fa, fb = 2 * a + i, 2 * b + j
                    start = ((fa + 1) * 6 + fb + 1) * 64
                    n = (fa * 4 + fb) * 64
                    t1[start : start + 64, :] = sloped(fenced(t5[start : start + 64, :].astype(F32) + v[b * 64 : (b + 1) * 64, :]), z1[n : n + 64, :])
    sum_step(2, 2)
    sum_step(3, 2)
    for ta in range(3):
        product = 0.0
        for a in range(4):
            for pair in range(2):
                start = ((a + 1) * 6 + 2 * pair + 1) * 64
                from_ = ((a + ta) * 6 + 2 * pair) * 64
                product = product + nt(t1[start : start + 128, 0:CELLS], e0[from_ : from_ + 256, 0:CELLS])
        value = product[0:64, 0:192] + product[64:128, 64:256]
        g_ref[AT_FIRST + ta * 64 : AT_FIRST + (ta + 1) * 64, :] = value[:, 0:128]
        start = AT_FIRST + (192 if ta < 2 else 256)
        g_ref[start : start + 64, ta % 2 * 64 : ta % 2 * 64 + 64] = value[:, 128:192]
    g_ref[AT_FIRST + 256 : AT_FIRST + 320, 64:128] = jnp.zeros((64, 64), F32)
    sum_step(5, 1)
    sum_step(0, 3)
    sum_step(1, 3)
    extend(4, 64, t1, CELLS)

    total = jnp.zeros((64, 256), F32)
    for a in range(4):
        for pair in range(2):
            v = sum(
                mm(w1b[:, ta * 256 : (ta + 1) * 256], t1[((a + ta) * 6 + 2 * pair) * 64 : ((a + ta) * 6 + 2 * pair + 4) * 64, 0:CELLS])
                for ta in range(3)
            )
            start = (a * 4 + 2 * pair) * 64
            fg[start : start + 128, :] = sloped(v, z0[start : start + 128, :])
        start = ((a + 1) * 6 + 1) * 16
        total = total + nt(xb[start : start + 64, 0:CELLS], fg[a * 256 : (a + 1) * 256, :])
    total = sum(total[b * 16 : (b + 1) * 16, b * 64 : (b + 1) * 64] for b in range(4))
    embed_step(0, total)

    def lay(a):
        for t in range(2):
            line = jnp.concatenate([fg[(a * 4 + b) * 64 : (a * 4 + b + 1) * 64, t * 128 : (t + 1) * 128] for b in range(4)], axis=1)
            laid = nt(line, cU[...])
            for r in range(4):
                tall[:, 16 * t + 4 * r + a, :] = laid[:, r * 128 : (r + 1) * 128]

    sum_step(4, 2)
    lay(0)
    lay(1)
    sum_step(5, 2)
    sum_step(2, 3)
    sum_step(3, 3)
    sum_step(0, 4)
    sum_step(1, 4)
    lay(2)
    lay(3)
    embed_step(1)
    features_ref[...] = tall[...].astype(BF)
    store(features_ref, features_out)
    sum_step(4, 3)
    sum_step(5, 3)
    sum_step(2, 4)
    sum_step(3, 4)
    embed_ref[...] = embed_step(2)
    for part in (0, 1, 4, 2, 3, 5):
        sum_step(part, 5)
    for copy in storing:
        copy.wait()


WIDTHS = ((384, 1), (128, 2), (512, 1), (512, 1), (256, 2))


def run_net(counts, *args):
    syn, emb, k1, k2, *rest = args
    k3, k4, k5, rdo, cot = rest
    eye, pick, pick_far, spread, near, far = [jnp.asarray(t, BF) for t in (np.eye(CELLS), PICK, PICK_FAR, SPREAD, SHIFT, SHIFT_FAR)]
    afar = (k1, near, k2.transpose(0, 1, 3, 2), k3, k5, k4, pick_far, far)
    wide, own = (EXT,), (CELLS,)
    blocks = [(16 * 36,) + wide, (64 * 36,) + wide, (1024,) + own, (1024,) + wide, (1024,) + wide, (1024,) + wide]
    blocks += [(512,) + wide, (512,) + wide, (128 * 9,) + wide, (256,) + own, (256 * 9,) + wide, (512,) + wide, (128 * 16,) + wide]
    blocks += [(1024,) + wide, (1024,) + own, (64 * 36,) + wide, (128 * 16,) + wide, (256 * 9,) + wide, (128 * 16,) + wide]
    blocks += [(64 * 36,) + wide, (1024,) + own, (64,) + wide]
    weights = [(384, 96), (128, 768), (128, 768), (256, 768), (128, 1536), (256, 1152), (128, 2304), (512, 1024), (256, 2048), (256, 512), (128, 1024), (16, 256), (256, 16)]
    scratch = [pltpu.VMEM(s, BF) for s in blocks + weights]
    for width, depth in WIDTHS:
        scratch += [pltpu.VMEM((bounds(depth)[3] + 16, width), BF), pltpu.VMEM((128 * depth + 64, width), BF)]
    scratch += [pltpu.VMEM(x.shape, BF) for x in afar]
    scratch += [pltpu.VMEM((256, 512), BF), pltpu.VMEM((128, 512), BF), pltpu.SemaphoreType.DMA((8,)), pltpu.VMEM((2, 32, 128), F32), pltpu.VMEM((64, 32, 128), BF)]
    scratch += [pltpu.SemaphoreType.DMA((2 + len(PARTS),))]
    scratch += [pltpu.SemaphoreType.DMA((len(WIDTHS), 8)), pltpu.SemaphoreType.DMA((len(WIDTHS), 8))]
    scratch += [pltpu.VMEM((ROWS, 128), F32), pltpu.VMEM((ROWS, 128), BF), pltpu.VMEM((64, 32, 128), F32)]
    n_row, n_col = counts
    most = max(n_row, n_col)
    along = {"row": n_row, "col": n_col, "x": n_row // 2}
    for _, size, paired, first, second in PARTS:
        half = size // 2 if paired else size
        n1, n2 = along[first], along[second]
        c1, pair = half // n1, half if paired else 16
        scratch += [
            pltpu.VMEM((pair, 128), BF),
            pltpu.VMEM((pair, 128), BF),
            pltpu.VMEM((half, 128), F32),
            pltpu.VMEM((half, 128), BF),
            pltpu.VMEM((n1 - 1, c1, 128), BF),
            pltpu.VMEM((n2, c1, 128), BF),
        ]
    scratch += [pltpu.SemaphoreType.DMA((len(PARTS), 5, most)), pltpu.SemaphoreType.DMA((len(PARTS), 5, most))]
    scratch += [pltpu.VMEM((n_row, 16, 64), F32), pltpu.VMEM((n_col, 16, 64), F32)]
    scratch += [pltpu.SemaphoreType.DMA((2, most)), pltpu.SemaphoreType.DMA((2, most))]
    vmem, hbm = pl.BlockSpec(memory_space=pltpu.VMEM), pl.BlockSpec(memory_space=pl.ANY)
    return pl.pallas_call(
        functools.partial(net_kernel, counts),
        out_shape=(
            jax.ShapeDtypeStruct((2, 32, 128), F32),
            jax.ShapeDtypeStruct((64, 32, 128), BF),
            jax.ShapeDtypeStruct((16, 64), F32),
            jax.ShapeDtypeStruct((ROWS, 128), BF),
        ),
        in_specs=[vmem] * 7 + [hbm] * 8,
        out_specs=(hbm, hbm, vmem, hbm),
        scratch_shapes=scratch,
        compiler_params=pltpu.CompilerParams(collective_id=1, has_side_effects=True, vmem_limit_bytes=56 * 2**20),
    )(syn, emb.T, rdo, cot, eye, pick, spread, *afar)


def out_kernel(logits, features, embed, grads, *refs):
    outs, (g, passed, mids, loads, stores) = refs[:9], (refs[9], refs[10:13], refs[13:19], refs[19], refs[20])
    spans = ((0, AT_BOTTOM), (AT_BOTTOM, AT_SECOND), (AT_SECOND, ROWS))
    pulls = [pltpu.make_async_copy(grads.at[a:b], g.at[a:b], loads.at[n]) for n, (a, b) in enumerate(spans)]
    for copy in pulls:
        copy.start()
    through = [pltpu.make_async_copy(x, passed[n], loads.at[3 + n]) for n, x in enumerate((logits, features, embed))]
    for copy in through:
        copy.start()
    pushes = [pltpu.make_async_copy(passed[n], outs[n], stores.at[n]) for n in range(3)]

    def push(n):
        pushes.append(pltpu.make_async_copy(mids[n - 3], outs[n], stores.at[n]))
        pushes[-1].start()

    m_first, m_second, m_bottom, m_return, m_final, m_read = mids
    pulls[0].wait()
    for t in range(9):
        ta, tb = t // 3, t % 3
        for half in range(2):
            start = AT_RETURN + (t * 2 + half) * 128
            m_return[ta, tb, :, half * 128 : (half + 1) * 128] = g[start : start + 128, :].astype(F32)
        m_final[ta, tb] = g[AT_FINAL + t * 64 : AT_FINAL + (t + 1) * 64, :].astype(F32)
    push(6)
    push(7)
    for pull, copy in zip(through, pushes):
        pull.wait()
        copy.start()
    pulls[1].wait()
    for t in range(9):
        m_bottom[t // 3, t % 3] = g[AT_BOTTOM + t * 256 : AT_BOTTOM + (t + 1) * 256, :].astype(F32)
    push(5)
    pulls[2].wait()
    for t in range(9):
        ta, tb = t // 3, t % 3
        m_second[ta, tb] = g[AT_SECOND + t * 64 : AT_SECOND + (t + 1) * 64, :].astype(F32)
        start, low = (AT_FIRST + ta * 64, tb * 64) if tb < 2 else (AT_FIRST + (192 if ta < 2 else 256), ta % 2 * 64)
        m_first[ta, tb] = g[start : start + 64, low : low + 64].astype(F32)
    m_read[...] = g[AT_READ : AT_READ + 16, 0:64].astype(F32)[0:2]
    push(3)
    push(4)
    push(8)
    for copy in pushes:
        copy.wait()


def write_out(logits, features, embed, g):
    shapes = [(2, 32, 128), (64, 32, 128), (16, 64), (3, 3, 64, 64), (3, 3, 64, 128), (3, 3, 256, 128), (3, 3, 128, 256), (3, 3, 64, 128), (2, 64)]
    hbm = pl.BlockSpec(memory_space=pl.ANY)
    outs = pl.pallas_call(
        out_kernel,
        out_shape=tuple(jax.ShapeDtypeStruct(s, BF if n == 1 else F32) for n, s in enumerate(shapes)),
        in_specs=[hbm] * 4,
        out_specs=(hbm,) * 9,
        scratch_shapes=[pltpu.VMEM((ROWS, 128), BF)]
        + [pltpu.VMEM(s, BF if n == 1 else F32) for n, s in enumerate(shapes)]
        + [pltpu.SemaphoreType.DMA((6,)), pltpu.SemaphoreType.DMA((9,))],
        compiler_params=pltpu.CompilerParams(vmem_limit_bytes=60 * 2**20),
    )(logits, features, embed, g)
    outs = list(outs)
    outs[2] = outs[2].T
    outs[4] = outs[4].transpose(0, 1, 3, 2)
    return tuple(outs)


def on_device(counts, *args):
    return write_out(*run_net(counts, *args))


def solution(mesh):
    counts = (mesh.shape["row"], mesh.shape["col"])
    cells = P(None, ("batch", "row"), "col")
    in_specs = (P(("batch", "row"), "col"),) + (P(),) * 7 + (cells,)
    out_specs = (cells, cells, P("batch", None)) + (P("batch", None, None, None),) * 5 + (P("batch", None),)
    return jax.shard_map(
        functools.partial(on_device, counts), mesh=mesh, in_specs=in_specs, out_specs=out_specs, check_vma=False
    )
```

```python
import functools

import jax
import jax.numpy as jnp
import numpy as np
from jax import lax
from jax.experimental import pallas as pl
from jax.experimental.pallas import tpu as pltpu
from jax.sharding import PartitionSpec as P

BF, F32 = jnp.bfloat16, jnp.float32
MESH = pl.DeviceIdType.MESH

DEEP, WIDE = 8, 32
CELLS = DEEP * WIDE
EXT = CELLS + 128

ROWS = 6272
PARTS = (
    (0, 1408, True, "x", "col"),
    (1408, 1536, True, "col", "x"),
    (2944, 1024, True, "x", "col"),
    (3968, 1280, True, "col", "x"),
    (5248, 640, False, "row", "col"),
    (5888, 384, False, "col", "row"),
)
AT_RETURN, AT_FINAL, AT_BOTTOM, AT_SECOND, AT_FIRST, AT_READ = 0, 2304, 2944, 5248, 5888, 6208


def ranged(values, start, size):
    return values.at[pl.ds(pl.multiple_of(start, 16), size), :]


def bounds(depth):
    left = 2 * WIDE * depth
    return WIDE * depth, left, left + 16, left + 32


def lane_of(r, q, depth):
    if not (-depth <= r < DEEP + depth and -depth <= q < WIDE + depth):
        return None
    row_in, col_in = 0 <= r < DEEP, 0 <= q < WIDE
    down, left, right, corner = bounds(depth)
    if row_in and col_in:
        return r * WIDE + q
    i = r + depth if r < 0 else r - DEEP
    j = q + depth if q < 0 else q - WIDE
    if col_in:
        return CELLS + (0 if r < 0 else down) + i * WIDE + q
    if row_in:
        return CELLS + (left if q < 0 else right) + j * DEEP + r
    return CELLS + corner + CORNERS[(-1 if r < 0 else 1, -1 if q < 0 else 1)] * depth * depth + i * depth + j


def shift_tables(depth, size):
    tables = []
    for dr in (-1, 0, 1):
        for dc in (-1, 0, 1):
            m = np.zeros((size, EXT), np.float32)
            for r in range(-1, DEEP + 1):
                for q in range(-1, WIDE + 1):
                    source = lane_of(r + dr, q + dc, depth)
                    if source is not None:
                        m[source, lane_of(r, q, 1)] = 1
            tables.append(m)
    return np.concatenate(tables)


def pick_table(depth):
    down, left, right, corner = bounds(depth)
    m = np.zeros((corner + 16, CELLS), np.float32)
    for i in range(depth):
        for q in range(WIDE):
            m[i * WIDE + q, i * WIDE + q] = 1
            m[down + i * WIDE + q, (DEEP - depth + i) * WIDE + q] = 1
        for r in range(DEEP):
            m[left + i * DEEP + r, r * WIDE + i] = 1
            m[right + i * DEEP + r, r * WIDE + WIDE - depth + i] = 1
        for j in range(depth):
            for k, (r, q) in enumerate(((0, 0), (0, WIDE - depth), (DEEP - depth, 0), (DEEP - depth, WIDE - depth))):
                m[corner + k * depth * depth + i * depth + j, (r + i) * WIDE + q + j] = 1
    return m


CORNERS = {(-1, -1): 3, (-1, 1): 2, (1, -1): 1, (1, 1): 0}


def spread_table():
    m = np.zeros((512, 512), np.float32)
    for r in range(4):
        for w in range(128):
            m[r * 128 + w, (w % 4) * 128 + r * WIDE + w // 4] = 1
    return m


SHIFT = shift_tables(1, EXT)
SHIFT_FAR = shift_tables(2, 512)
PICK, PICK_FAR = pick_table(1), pick_table(2)
SPREAD = spread_table()

UNDER = (((0,), (1, 2)), ((0, 1), (2,)))
OVER = ((2,), (1, 2), (0, 1), (0,))
BASE = (0, 1, 1, 2)


def mm(a, b):
    return jnp.dot(a, b, preferred_element_type=F32)


def nt(a, b):
    return lax.dot_general(a, b, (((1,), (1,)), ((), ())), preferred_element_type=F32)


def logistic(z):
    return 0.5 + 0.5 * jnp.tanh(0.5 * z)


def activated(v):
    stored = v.astype(BF)
    z = stored.astype(F32)
    return stored, (z * logistic(z)).astype(BF)


def sloped(incoming, stored):
    z = stored.astype(F32)
    s = logistic(z)
    return (incoming * (s * (1.0 + z * (1.0 - s)))).astype(BF)


def remote(src, dst, send, recv, target):
    return pltpu.make_async_remote_copy(
        src_ref=src, dst_ref=dst, send_sem=send, recv_sem=recv, device_id=target, device_id_type=MESH
    )


SIDES = ((-1, -1), (-1, 1), (1, -1), (1, 1), (0, -1), (0, 1), (-1, 0), (1, 0))


def net_kernel(counts, *refs):
    it = iter(refs)

    def take(n):
        return [next(it) for _ in range(n)]

    afar = take(15)
    logits_out, features_out, embed_ref, grads_out = take(4)
    xb, e0, z0, z1, f1, e1, z2, f2, e2, z3, e3, z4, e4, z5, f5, t5, t4, t3, t2, t1, fg, cp = take(22)
    w0, w1, w1b, w2, w2b, w3, w3b, w4, w4b, w5, w5b, r4, r4t = take(13)
    halos = [take(2) for _ in WIDTHS]
    near = take(15)
    syn, cU, cot, cQ, eye, embt, rdo, k1, cS, k2t, k3, k5, k4, cQ2, cF = near
    far, wide2, loads, logits_ref, features_ref, stores = take(6)
    sends, recvs = take(2)
    g_ref, whole, tall = take(3)
    stages = [take(6) for _ in PARTS]
    sum_sends, sum_recvs, embed_row, embed_col, embed_sends, embed_recvs = take(6)

    n_row, n_col = counts
    row, col = lax.axis_index("row"), lax.axis_index("col")
    there = {
        (-1, 0): row > 0,
        (1, 0): row < n_row - 1,
        (0, -1): col > 0,
        (0, 1): col < n_col - 1,
    }
    for dr in (-1, 1):
        for dc in (-1, 1):
            there[dr, dc] = jnp.logical_and(there[dr, 0], there[0, dc])

    def place(dr, dc):
        return {"row": (row + dr + n_row) % n_row, "col": (col + dc + n_col) % n_col}

    storing = []

    def store(source, target):
        storing.append(pltpu.make_async_copy(source, target, stores.at[len(storing)]))
        storing[-1].start()

    partners = [(d, 0) for d in range(1, n_row)] + [(0, d) for d in range(1, n_col)] + list(SIDES[:4])
    barrier = pltpu.get_barrier_semaphore()
    for partner in partners:
        pl.semaphore_signal(barrier, inc=1, device_id=place(*partner), device_id_type=MESH)

    loading = {}
    for n, (source, target) in enumerate(zip(afar, near)):
        loading[id(target)] = pltpu.make_async_copy(source, target, loads.at[n])
        loading[id(target)].start()

    def loaded(*targets):
        for target in targets:
            loading[id(target)].wait()

    lane = lax.broadcasted_iota(jnp.int32, (1, 128), 1)
    sixteen = lax.broadcasted_iota(jnp.int32, (16, 1), 0)

    def inside(depth):
        down, left, right, corner = bounds(depth)
        spans = [(0, down, (-1, 0)), (down, left, (1, 0)), (left, left + DEEP * depth, (0, -1)), (right, right + DEEP * depth, (0, 1))]
        spans += [(corner + k * depth * depth, corner + (k + 1) * depth * depth, side) for side, k in CORNERS.items()]
        masks = []
        for tile in range(depth):
            at = lane + tile * 128
            keep = lane < 0
            for low, high, side in spans:
                keep = jnp.logical_or(keep, jnp.logical_and(jnp.logical_and(at >= low, at < high), there[side]))
            masks.append(keep)
        return masks

    near_masks, far_masks = inside(1), inside(2)

    def fenced(v):
        return jnp.concatenate([v[:, :CELLS], jnp.where(near_masks[0], v[:, CELLS:], 0.0)], axis=1)

    def begin(n, depth, pieces, ahead=None):
        out, into = halos[n]
        down, left, right, corner = bounds(depth)
        pick = (cQ if depth == 1 else cQ2)[...]
        start = 0
        for piece in pieces:
            out[:, start : start + piece.shape[0]] = nt(pick, piece).astype(BF)
            start += piece.shape[0]
        size = {(-1, 0): (0, down, down), (1, 0): (down, left, 0), (0, -1): (left, right, right), (0, 1): (right, corner, left)}
        copies = []
        for k, (dr, dc) in enumerate(SIDES):
            if (dr, dc) in size:
                low, high, target = size[dr, dc]
            else:
                low, high = corner, corner + 16
                target = 128 * depth + 16 * CORNERS[-dr, -dc]
            copies.append(
                remote(out.at[low:high], into.at[target : target + high - low], sends.at[n, k], recvs.at[n, k], place(dr, dc))
            )
        if ahead is not None:
            ahead()
        for copy in copies:
            copy.start()
        return copies

    def end(n, depth, copies):
        into = halos[n][1]
        corner = bounds(depth)[3]
        for copy in copies:
            copy.wait()
        ends = 0.0
        for k in range(4):
            tile = into[128 * depth + 16 * k : 128 * depth + 16 * (k + 1), :].astype(F32)
            ends = ends + jnp.where(sixteen // (depth * depth) == k, tile, 0.0)
        into[corner : corner + 16, :] = ends.astype(BF)

    def ring(n, depth, start, width):
        into = halos[n][1]
        tiles = []
        for tile, keep in enumerate(near_masks if depth == 1 else far_masks):
            turned = nt(eye[0:width, 0:width], into[tile * 128 : (tile + 1) * 128, start : start + width])
            tiles.append(jnp.where(keep, turned, 0.0).astype(BF))
        return tiles

    def extend(p, width, ref, size):
        sides = {}
        for ea in range(p + 2):
            for eb in range(p + 2):
                way = (ea > p) - (ea < 1), (eb > p) - (eb < 1)
                if way != (0, 0):
                    source = (((ea - 1) % p + 1) * (p + 2) + (eb - 1) % p + 1) * width
                    sides.setdefault(way, []).append((source, (ea * (p + 2) + eb) * width))
        for (dr, dc), spots in sides.items():
            at = (dr * 3 + dc + 4) * EXT
            many = len(spots) * width
            first, target = spots[0]
            if dc == 0:
                held = ref[first : first + many, :]
            else:
                held = jnp.concatenate([ref[i : i + width, :] for i, _ in spots], axis=0)
            moved = mm(held, cS[at : at + EXT, 0:size]).astype(BF)
            if dc == 0:
                ref[target : target + many, 0:size] = moved
            else:
                for n, (_, target) in enumerate(spots):
                    ref[target : target + width, 0:size] = moved[n * width : (n + 1) * width, :]

    core, n_x = row % 2, n_row // 2
    ways = {
        "row": (row, n_row, lambda d: place(d, 0)),
        "col": (col, n_col, lambda d: place(0, d)),
        "x": (row // 2, n_x, lambda d: {"row": (row // 2 + d) % n_x * 2 + core}),
    }
    flying = {}

    def sum_step(part, step):
        start, size, paired, first, second = PARTS[part]
        s0, r0, held, s1, r1, r2 = stages[part]
        me1, n1, to1 = ways[first]
        me2, n2, to2 = ways[second]
        for copy in flying.pop(part, ()):
            copy.wait()
        if step == 5:
            store(whole.at[start : start + size], grads_out.at[start : start + size])
            return
        half = size // 2 if paired else size
        base = start + core * half if paired else start
        c1 = half // n1
        own = pl.ds(pl.multiple_of(base + me1 * c1, 16), c1)
        partner = {"row": row + 1 - 2 * core}
        moves = []
        if step == 0:
            s0[...] = g_ref[pl.ds(pl.multiple_of(start + (1 - core) * half, 16), half), :].astype(BF)
            moves.append((s0, r0, partner))
        elif step == 1:
            total = g_ref[pl.ds(pl.multiple_of(base, 16), half), :] if paired else g_ref[base : base + half, :]
            if paired:
                total = total + r0[...].astype(F32)
            held[...] = total
            s1[...] = total.astype(BF)
            moves = [(ranged(s1, (me1 + d) % n1 * c1, c1), r1.at[d - 1], to1(d)) for d in range(1, n1)]
        elif step == 2:
            total = held[pl.ds(pl.multiple_of(me1 * c1, 16), c1), :]
            for d in range(n1 - 1):
                total = total + r1[d].astype(F32)
            r2[me2] = total.astype(BF)
            moves = [(r2.at[me2], r2.at[me2], to2(d)) for d in range(1, n2)]
        elif step == 3:
            whole[own, :] = sum(r2[d].astype(F32) for d in range(n2)).astype(BF)
            moves = [(whole.at[own, :], whole.at[own, :], to1(d)) for d in range(1, n1)]
        elif paired:
            mine = ranged(whole, base, half)
            moves.append((mine, mine, partner))
        copies = [
            remote(src, dst, sum_sends.at[part, step, k], sum_recvs.at[part, step, k], to) for k, (src, dst, to) in enumerate(moves)
        ]
        for copy in copies:
            copy.start()
        flying[part] = copies

    def embed_step(step, value=None):
        if step > 0:
            for copy in flying.pop("embed"):
                copy.wait()
            slots = embed_row if step == 1 else embed_col
            value = sum(slots[d] for d in range(slots.shape[0]))
        if step == 2:
            return value
        slots, (me, count, to) = (embed_row, ways["row"]) if step == 0 else (embed_col, ways["col"])
        slots[me] = value
        copies = [
            remote(slots.at[me], slots.at[me], embed_sends.at[step, d], embed_recvs.at[step, d], to(d)) for d in range(1, count)
        ]
        for copy in copies:
            copy.start()
        flying["embed"] = copies

    loaded(syn, cU)
    bit = lax.broadcasted_iota(jnp.int32, (16, 1), 0)
    groups = []
    for a in range(4):
        for t in range(2):
            line = [(syn[16 * t + 4 * r + a : 16 * t + 4 * r + a + 1, :] >> bit) & 1 for r in range(4)]
            groups.append(jnp.concatenate(line, axis=1))
    bits = jnp.concatenate(groups, axis=0).astype(F32).astype(BF)
    phased = mm(bits, cU[...]).astype(BF)
    for a in range(4):
        for t in range(2):
            for b in range(4):
                start = ((a + 1) * 6 + b + 1) * 16
                xb[start : start + 16, t * 128 : (t + 1) * 128] = phased[(a * 2 + t) * 16 : (a * 2 + t + 1) * 16, b * 128 : (b + 1) * 128]
    loaded(cot)
    wide = cot[...].astype(F32)
    groups = []
    for a in range(4):
        for t in range(2):
            line = jnp.concatenate([wide[:, 16 * t + 4 * r + a, :] for r in range(4)], axis=1)
            groups.append(jnp.concatenate([line, jnp.zeros((6, 512), F32)], axis=0))
    phased = mm(jnp.concatenate(groups, axis=0).astype(BF), cU[...])
    for a in range(4):
        for t in range(2):
            start = (a * 2 + t) * 8
            pieces = [phased[start : start + 4, b * 128 : (b + 1) * 128] for b in range(4)]
            cp[a * 16 : (a + 1) * 16, t * 128 : (t + 1) * 128] = jnp.concatenate(pieces, axis=0).astype(BF)

    loaded(cQ)
    inner = [((a + 1) * 6 + 1) * 16 for a in range(4)]
    pieces = [jnp.concatenate([xb[i : i + 64, 0:CELLS] for i in inner], axis=0), cp[:, 0:CELLS]]
    copies = begin(0, 1, pieces, lambda: pl.semaphore_wait(barrier, len(partners)))

    def beside(blocks, i, blank):
        return jnp.concatenate(blocks + [blank] if i == 0 else [blank] + blocks, axis=0)

    def added(k, rows, cols):
        return sum(k[ta, tb].astype(F32) for ta in rows for tb in cols).astype(BF)

    def arrange_first():
        repeat = (lax.broadcasted_iota(jnp.int32, (16, 96), 1) % 16 == lax.broadcasted_iota(jnp.int32, (16, 96), 0)).astype(F32).astype(BF)
        tiled = mm(nt(eye[:64, :64], embt[...]).astype(BF), repeat)
        own = lax.broadcasted_iota(jnp.int32, (64, 96), 1) // 16
        for j in range(6):
            w0[j * 64 : (j + 1) * 64, :] = jnp.where(own == j, tiled, 0.0).astype(BF)
        for ta in range(3):
            for i in range(2):
                w1[i * 64 : (i + 1) * 64, ta * 256 : (ta + 1) * 256] = sum(
                    mm(k1[ta, tb], eye[(tb + i) * 64 : (tb + i + 1) * 64, :]) for tb in range(3)
                ).astype(BF)

    def arrange_second():
        blank, empty = jnp.zeros((64, 128), BF), jnp.zeros((64, 64), BF)
        for ta in range(3):
            for i in range(2):
                line = beside([k2t[ta, tb] for tb in range(3)], i, blank)
                w2[i * 128 : (i + 1) * 128, ta * 256 : (ta + 1) * 256] = nt(eye[:128, :128], line).astype(BF)
                for tb in range(3):
                    w2b[i * 64 : (i + 1) * 64, ta * 512 + (tb + i) * 128 : ta * 512 + (tb + i + 1) * 128] = k2t[2 - ta, 2 - tb]
                hole = ta * 512 + (384 if i == 0 else 0)
                w2b[i * 64 : (i + 1) * 64, hole : hole + 128] = blank
                line = beside([k1[2 - ta, 2 - tb] for tb in range(3)], i, empty)
                w1b[i * 64 : (i + 1) * 64, ta * 256 : (ta + 1) * 256] = nt(eye[:64, :64], line).astype(BF)

    def arrange_bottom():
        for t in range(9):
            w3[:, t * 128 : (t + 1) * 128] = k3[t // 3, t % 3]
            w3b[:, t * 256 : (t + 1) * 256] = nt(eye[:128, :128], k3[2 - t // 3, 2 - t % 3]).astype(BF)

    def arrange_return():
        for pa in range(2):
            for pb in range(2):
                for s in range(2):
                    for u in range(2):
                        block = added(k4, UNDER[pa][s], UNDER[pb][u])
                        w4[(pa * 2 + pb) * 128 : (pa * 2 + pb + 1) * 128, (s * 2 + u) * 256 : (s * 2 + u + 1) * 256] = block
                        at = OVER.index(UNDER[pa][s]) * 4 + OVER.index(UNDER[pb][u])
                        w4b[:, at * 128 : (at + 1) * 128] = nt(eye[...], block).astype(BF)

    def arrange_final():
        for pa in range(2):
            for pb in range(2):
                for s in range(2):
                    for u in range(2):
                        start = pa * 128 + (1 - pb) * 64
                        w5[start : start + 64, (s * 2 + u) * 128 : (s * 2 + u + 1) * 128] = added(k5, UNDER[pa][s], UNDER[pb][u])
        for ea in range(4):
            for pair in range(2):
                stack = jnp.concatenate([added(k5, OVER[ea], OVER[2 * pair + i]) for i in range(2)], axis=0)
                at = ea * 2 + pair
                w5b[:, at * 128 : (at + 1) * 128] = nt(eye[:128, :128], stack).astype(BF)

    def arrange_readout():
        repeat = (lax.broadcasted_iota(jnp.int32, (64, 256), 1) % 64 == lax.broadcasted_iota(jnp.int32, (64, 256), 0)).astype(F32).astype(BF)
        tiled = mm(rdo[...], repeat)
        tiled = jnp.concatenate([tiled, jnp.zeros((2, 256), F32)] * 4, axis=0)
        own = lax.broadcasted_iota(jnp.int32, (16, 256), 1) // 64 == lax.broadcasted_iota(jnp.int32, (16, 256), 0) // 4
        r4[...] = jnp.where(own, tiled, 0.0).astype(BF)
        r4t[...] = nt(eye[...], r4[...]).astype(BF)

    loaded(eye, embt, rdo, k1)
    arrange_first()
    arrange_readout()
    loaded(cS)
    end(0, 1, copies)
    (tile,) = ring(0, 1, 0, 256)
    for a in range(4):
        xb[inner[a] : inner[a] + 64, CELLS:EXT] = tile[a * 64 : (a + 1) * 64, :]
    cp[:, CELLS:EXT] = ring(0, 1, 256, 64)[0]
    extend(4, 16, xb, EXT)

    for ea in range(6):
        stored, active = activated(mm(w0[...], xb[ea * 96 : (ea + 1) * 96, :]))
        e0[ea * 384 : (ea + 1) * 384, :] = active
        if 1 <= ea <= 4:
            z0[(ea - 1) * 256 : ea * 256, :] = stored[64:320, 0:CELLS]

    for a in range(4):
        for pair in range(2):
            v = sum(
                mm(w1[:, ta * 256 : (ta + 1) * 256], e0[((a + ta) * 6 + 2 * pair) * 64 : ((a + ta) * 6 + 2 * pair + 4) * 64, :])
                for ta in range(3)
            )
            start = (a * 4 + 2 * pair) * 64
            z1[start : start + 128, :], f1[start : start + 128, :] = activated(fenced(v))

    def pooled(ref, side, width, a, b, size):
        spots = [((2 * a + i) * side + 2 * b + j) * width for i in range(2) for j in range(2)]
        return (sum(ref[s : s + width, 0:size].astype(F32) for s in spots) * 0.25).astype(BF)

    for a in range(2):
        for b in range(2):
            start = ((a + 1) * 4 + b + 1) * 64
            e1[start : start + 64, :] = pooled(f1, 4, 64, a, b, EXT)
    extend(2, 64, e1, CELLS)
    loaded(k2t)
    arrange_second()

    for a in range(2):
        v = sum(mm(w2[:, ta * 256 : (ta + 1) * 256], e1[(a + ta) * 256 : (a + ta + 1) * 256, 0:CELLS]) for ta in range(3))
        z2[a * 256 : (a + 1) * 256, 0:CELLS], f2[a * 256 : (a + 1) * 256, 0:CELLS] = activated(v)
    e2[4 * 128 : 5 * 128, 0:CELLS] = pooled(f2, 2, 128, 0, 0, CELLS)
    loaded(cQ2)
    copies = begin(1, 2, [e2[4 * 128 : 5 * 128, 0:CELLS]])
    later = begin(2, 1, [z2[0:256, 0:CELLS], z2[256:512, 0:CELLS]])
    loaded(k3, k5)
    arrange_bottom()
    arrange_final()
    loaded(k4)
    arrange_return()
    loaded(cF)
    end(1, 2, copies)
    wide2[:, 0:CELLS] = e2[4 * 128 : 5 * 128, 0:CELLS]
    wide2[:, 256:384], wide2[:, 384:512] = ring(1, 2, 0, 128)
    for n in range(9):
        e2[n * 128 : (n + 1) * 128, :] = mm(wide2[...], cF[n * 512 : (n + 1) * 512, :]).astype(BF)

    stored, e3[4 * 256 : 5 * 256, :] = activated(fenced(mm(w3[...], e2[...])))
    z3[...] = stored[:, 0:CELLS]
    end(2, 1, later)
    for a in range(2):
        z2[a * 256 : (a + 1) * 256, CELLS:EXT] = ring(2, 1, a * 256, 256)[0]
        f2[a * 256 : (a + 1) * 256, CELLS:EXT] = activated(z2[a * 256 : (a + 1) * 256, CELLS:EXT])[1]
    extend(1, 256, e3, EXT)

    for a in range(2):
        for b in range(2):
            n = a * 2 + b
            v = sum(
                mm(w4[n * 128 : (n + 1) * 128, s * 512 : (s + 1) * 512], e3[((a + s) * 3 + b) * 256 : ((a + s) * 3 + b + 2) * 256, :])
                for s in range(2)
            )
            v = v + f2[n * 128 : (n + 1) * 128, :].astype(F32)
            start = ((a + 1) * 4 + b + 1) * 128
            z4[n * 128 : (n + 1) * 128, :], e4[start : start + 128, :] = activated(fenced(v))
    extend(2, 128, e4, EXT)

    RUNS = ((0, 1, 64, 64), (1, 2, 0, 128), (3, 1, 0, 64))
    for a in range(4):
        for b, many, first, size in RUNS:
            base = (a % 2) * 128 + first
            v = sum(
                mm(w5[base : base + size, s * 256 : (s + 1) * 256], e4[((BASE[a] + s) * 4 + BASE[b]) * 128 : ((BASE[a] + s) * 4 + BASE[b] + 2) * 128, :])
                for s in range(2)
            )
            start = (a * 4 + b) * 64
            v = v + f1[start : start + size, :].astype(F32)
            z5[start : start + size, :] = v.astype(BF)

    for a in range(4):
        back = mm(r4t[...], cp[a * 16 : (a + 1) * 16, :])
        start = ((a + 1) * 6 + 1) * 64
        t5[start : start + 256, :] = sloped(back, z5[a * 256 : (a + 1) * 256, :])
    extend(4, 64, t5, CELLS)
    for a in range(2):
        for b in range(2):
            v = sum(
                mm(w5b[:, m * 256 : (m + 1) * 256], t5[((2 * a + m) * 6 + 2 * b) * 64 : ((2 * a + m) * 6 + 2 * b + 4) * 64, 0:CELLS])
                for m in range(4)
            )
            start = ((a + 1) * 4 + b + 1) * 128
            n = a * 2 + b
            t4[start : start + 128, 0:CELLS] = sloped(v, z4[n * 128 : (n + 1) * 128, 0:CELLS])
    copies = begin(3, 1, [t4[((a + 1) * 4 + 1) * 128 : ((a + 1) * 4 + 3) * 128, 0:CELLS] for a in range(2)])

    sums = {}
    for a in range(4):
        for s in range(2):
            for b, many, first, size in RUNS:
                start = ((BASE[a] + s) * 4 + BASE[b]) * 128
                t_start = ((a + 1) * 6 + b + 1) * 64
                product = nt(t5[t_start : t_start + size, 0:CELLS], e4[start : start + 256, 0:CELLS])
                for m in range(many):
                    key = (a % 2, s, (b + m) % 2)
                    block = product[m * 64 : (m + 1) * 64, :]
                    sums[key] = sums[key] + block if key in sums else block

    def reads(parity, tap):
        return 0 if tap in UNDER[parity][0] else 1

    for ta in range(3):
        rowed = [sums[0, reads(0, ta), pb] + sums[1, reads(1, ta), pb] for pb in range(2)]
        for tb in range(3):
            value = sum(rowed[pb][:, reads(pb, tb) * 128 : (reads(pb, tb) + 1) * 128] for pb in range(2))
            start = AT_FINAL + (ta * 3 + tb) * 64
            g_ref[start : start + 64, :] = value

    for b in range(2):
        for u in range(2):
            parts = {}
            for a in range(2):
                for s in range(2):
                    start = ((a + 1) * 4 + b + 1) * 128
                    from_ = ((a + s) * 3 + b + u) * 256
                    parts[a, s] = nt(t4[start : start + 128, 0:CELLS], e3[from_ : from_ + 256, 0:CELLS])
            for ta in range(3):
                value = parts[0, reads(0, ta)] + parts[1, reads(1, ta)]
                for tb in UNDER[b][u]:
                    for half in range(2):
                        start = AT_RETURN + ((ta * 3 + tb) * 2 + half) * 128
                        piece = value[:, half * 128 : (half + 1) * 128]
                        g_ref[start : start + 128, :] = piece if b == 0 else g_ref[start : start + 128, :] + piece

    g_ref[AT_FINAL + 576 : AT_BOTTOM, :] = jnp.zeros((AT_BOTTOM - AT_FINAL - 576, 128), F32)
    sum_step(0, 0)
    sum_step(1, 0)
    total = jnp.zeros((16, 256), F32)
    for a in range(4):
        f5[a * 256 : (a + 1) * 256, :] = activated(z5[a * 256 : (a + 1) * 256, 0:CELLS])[1]
        total = total + nt(cp[a * 16 : (a + 1) * 16, 0:CELLS], f5[a * 256 : (a + 1) * 256, :])
    total = sum(total[b * 4 : (b + 1) * 4, b * 64 : (b + 1) * 64] for b in range(4))
    g_ref[AT_READ:ROWS, :] = jnp.zeros((ROWS - AT_READ, 128), F32)
    g_ref[AT_READ : AT_READ + 4, 0:64] = total

    end(3, 1, copies)
    sum_step(0, 1)
    sum_step(1, 1)
    for a in range(2):
        start = ((a + 1) * 4 + 1) * 128
        t4[start : start + 256, CELLS:EXT] = ring(3, 1, a * 256, 256)[0]
    extend(2, 128, t4, CELLS)
    v = sum(mm(w4b[:, m * 512 : (m + 1) * 512], t4[m * 512 : (m + 1) * 512, 0:CELLS]) for m in range(4))
    far[:, 0:CELLS] = sloped(v, z3[...])
    copies = begin(4, 2, [far[:, 0:CELLS]])
    for t in range(9):
        g_ref[AT_BOTTOM + t * 256 : AT_BOTTOM + (t + 1) * 256, :] = nt(far[:, 0:CELLS], e2[t * 128 : (t + 1) * 128, 0:CELLS])
    sum_step(2, 0)
    sum_step(3, 0)
    groups = []
    for a in range(4):
        here = f5[a * 256 : (a + 1) * 256, :]
        value = mm(r4[...], here)
        for t in range(2):
            groups.append(jnp.concatenate([value[b * 4 : (b + 1) * 4, t * 128 : (t + 1) * 128] for b in range(4)], axis=1))
    value = jnp.concatenate(groups, axis=0)
    laid = 0.0
    for _ in range(3):
        piece = value.astype(BF)
        laid = laid + nt(piece, cU[...])
        value = value - piece.astype(F32)
    for a in range(4):
        for t in range(2):
            for r in range(4):
                h = 16 * t + 4 * r + a
                logits_ref[:, h : h + 1, :] = laid[(a * 2 + t) * 4 : (a * 2 + t) * 4 + 2, r * 128 : (r + 1) * 128].reshape(2, 1, 128)
    store(logits_ref, logits_out)
    sum_step(2, 1)
    sum_step(3, 1)
    end(4, 2, copies)
    far[:, 256:384], far[:, 384:512] = ring(4, 2, 0, 256)
    for n in range(9):
        t3[n * 256 : (n + 1) * 256, :] = mm(far[...], cF[n * 512 : (n + 1) * 512, :]).astype(BF)

    sum_step(0, 2)
    sum_step(1, 2)
    through = mm(w3b[...], t3[...]) * 0.25
    for a in range(2):
        for b in range(2):
            n = a * 2 + b
            start = ((a + 1) * 4 + b + 1) * 128
            v = fenced(t4[start : start + 128, :].astype(F32) + through)
            t2[start : start + 128, :] = sloped(v, z2[n * 128 : (n + 1) * 128, :])
    for ta in range(3):
        product = 0.0
        for a in range(2):
            start = ((a + 1) * 4 + 1) * 128
            product = product + nt(e1[(a + ta) * 256 : (a + ta + 1) * 256, 0:CELLS], t2[start : start + 256, 0:CELLS])
        g_ref[AT_SECOND + ta * 192 : AT_SECOND + (ta + 1) * 192, :] = product[0:192, 0:128] + product[64:256, 128:256]
    g_ref[AT_SECOND + 576 : AT_FIRST, :] = jnp.zeros((AT_FIRST - AT_SECOND - 576, 128), F32)
    sum_step(4, 1)
    extend(2, 128, t2, EXT)

    for a in range(2):
        v = sum(mm(w2b[:, ta * 512 : (ta + 1) * 512], t2[(a + ta) * 512 : (a + ta + 1) * 512, :]) for ta in range(3)) * 0.25
        for b in range(2):
            for i in range(2):
                for j in range(2):
                    fa, fb = 2 * a + i, 2 * b + j
                    start = ((fa + 1) * 6 + fb + 1) * 64
                    n = (fa * 4 + fb) * 64
                    t1[start : start + 64, :] = sloped(fenced(t5[start : start + 64, :].astype(F32) + v[b * 64 : (b + 1) * 64, :]), z1[n : n + 64, :])
    sum_step(2, 2)
    sum_step(3, 2)
    for ta in range(3):
        product = 0.0
        for a in range(4):
            for pair in range(2):
                start = ((a + 1) * 6 + 2 * pair + 1) * 64
                from_ = ((a + ta) * 6 + 2 * pair) * 64
                product = product + nt(t1[start : start + 128, 0:CELLS], e0[from_ : from_ + 256, 0:CELLS])
        value = product[0:64, 0:192] + product[64:128, 64:256]
        g_ref[AT_FIRST + ta * 64 : AT_FIRST + (ta + 1) * 64, :] = value[:, 0:128]
        start = AT_FIRST + (192 if ta < 2 else 256)
        g_ref[start : start + 64, ta % 2 * 64 : ta % 2 * 64 + 64] = value[:, 128:192]
    g_ref[AT_FIRST + 256 : AT_FIRST + 320, 64:128] = jnp.zeros((64, 64), F32)
    sum_step(5, 1)
    sum_step(0, 3)
    sum_step(1, 3)
    extend(4, 64, t1, CELLS)

    total = jnp.zeros((64, 256), F32)
    for a in range(4):
        for pair in range(2):
            v = sum(
                mm(w1b[:, ta * 256 : (ta + 1) * 256], t1[((a + ta) * 6 + 2 * pair) * 64 : ((a + ta) * 6 + 2 * pair + 4) * 64, 0:CELLS])
                for ta in range(3)
            )
            start = (a * 4 + 2 * pair) * 64
            fg[start : start + 128, :] = sloped(v, z0[start : start + 128, :])
        start = ((a + 1) * 6 + 1) * 16
        total = total + nt(xb[start : start + 64, 0:CELLS], fg[a * 256 : (a + 1) * 256, :])
    total = sum(total[b * 16 : (b + 1) * 16, b * 64 : (b + 1) * 64] for b in range(4))
    embed_step(0, total)

    def lay(a):
        for t in range(2):
            line = jnp.concatenate([fg[(a * 4 + b) * 64 : (a * 4 + b + 1) * 64, t * 128 : (t + 1) * 128] for b in range(4)], axis=1)
            laid = nt(line, cU[...])
            for r in range(4):
                tall[:, 16 * t + 4 * r + a, :] = laid[:, r * 128 : (r + 1) * 128]

    sum_step(4, 2)
    lay(0)
    lay(1)
    sum_step(5, 2)
    sum_step(2, 3)
    sum_step(3, 3)
    sum_step(0, 4)
    sum_step(1, 4)
    lay(2)
    lay(3)
    embed_step(1)
    features_ref[...] = tall[...].astype(BF)
    store(features_ref, features_out)
    sum_step(4, 3)
    sum_step(5, 3)
    sum_step(2, 4)
    sum_step(3, 4)
    embed_ref[...] = embed_step(2)
    for part in (0, 1, 4, 2, 3, 5):
        sum_step(part, 5)
    for copy in storing:
        copy.wait()


WIDTHS = ((384, 1), (128, 2), (512, 1), (512, 1), (256, 2))


def run_net(counts, *args):
    syn, emb, k1, k2, *rest = args
    k3, k4, k5, rdo, cot = rest
    eye, pick, pick_far, spread, near, far = [jnp.asarray(t, BF) for t in (np.eye(CELLS), PICK, PICK_FAR, SPREAD, SHIFT, SHIFT_FAR)]
    afar = (syn, spread, cot, pick, eye, emb.T, rdo, k1, near, k2.transpose(0, 1, 3, 2), k3, k5, k4, pick_far, far)
    wide, own = (EXT,), (CELLS,)
    blocks = [(16 * 36,) + wide, (64 * 36,) + wide, (1024,) + own, (1024,) + wide, (1024,) + wide, (1024,) + wide]
    blocks += [(512,) + wide, (512,) + wide, (128 * 9,) + wide, (256,) + own, (256 * 9,) + wide, (512,) + wide, (128 * 16,) + wide]
    blocks += [(1024,) + wide, (1024,) + own, (64 * 36,) + wide, (128 * 16,) + wide, (256 * 9,) + wide, (128 * 16,) + wide]
    blocks += [(64 * 36,) + wide, (1024,) + own, (64,) + wide]
    weights = [(384, 96), (128, 768), (128, 768), (256, 768), (128, 1536), (256, 1152), (128, 2304), (512, 1024), (256, 2048), (256, 512), (128, 1024), (16, 256), (256, 16)]
    scratch = [pltpu.VMEM(s, BF) for s in blocks + weights]
    for width, depth in WIDTHS:
        scratch += [pltpu.VMEM((bounds(depth)[3] + 16, width), BF), pltpu.VMEM((128 * depth + 64, width), BF)]
    scratch += [pltpu.VMEM(x.shape, x.dtype) for x in afar]
    scratch += [pltpu.VMEM((256, 512), BF), pltpu.VMEM((128, 512), BF), pltpu.SemaphoreType.DMA((15,)), pltpu.VMEM((2, 32, 128), F32), pltpu.VMEM((64, 32, 128), BF)]
    scratch += [pltpu.SemaphoreType.DMA((2 + len(PARTS),))]
    scratch += [pltpu.SemaphoreType.DMA((len(WIDTHS), 8)), pltpu.SemaphoreType.DMA((len(WIDTHS), 8))]
    scratch += [pltpu.VMEM((ROWS, 128), F32), pltpu.VMEM((ROWS, 128), BF), pltpu.VMEM((64, 32, 128), F32)]
    n_row, n_col = counts
    most = max(n_row, n_col)
    along = {"row": n_row, "col": n_col, "x": n_row // 2}
    for _, size, paired, first, second in PARTS:
        half = size // 2 if paired else size
        n1, n2 = along[first], along[second]
        c1, pair = half // n1, half if paired else 16
        scratch += [
            pltpu.VMEM((pair, 128), BF),
            pltpu.VMEM((pair, 128), BF),
            pltpu.VMEM((half, 128), F32),
            pltpu.VMEM((half, 128), BF),
            pltpu.VMEM((n1 - 1, c1, 128), BF),
            pltpu.VMEM((n2, c1, 128), BF),
        ]
    scratch += [pltpu.SemaphoreType.DMA((len(PARTS), 5, most)), pltpu.SemaphoreType.DMA((len(PARTS), 5, most))]
    scratch += [pltpu.VMEM((n_row, 16, 64), F32), pltpu.VMEM((n_col, 16, 64), F32)]
    scratch += [pltpu.SemaphoreType.DMA((2, most)), pltpu.SemaphoreType.DMA((2, most))]
    vmem, hbm = pl.BlockSpec(memory_space=pltpu.VMEM), pl.BlockSpec(memory_space=pl.ANY)
    return pl.pallas_call(
        functools.partial(net_kernel, counts),
        out_shape=(
            jax.ShapeDtypeStruct((2, 32, 128), F32),
            jax.ShapeDtypeStruct((64, 32, 128), BF),
            jax.ShapeDtypeStruct((16, 64), F32),
            jax.ShapeDtypeStruct((ROWS, 128), BF),
        ),
        in_specs=[hbm] * 15,
        out_specs=(hbm, hbm, vmem, hbm),
        scratch_shapes=scratch,
        compiler_params=pltpu.CompilerParams(collective_id=1, has_side_effects=True, vmem_limit_bytes=56 * 2**20),
    )(*afar)


def out_kernel(logits, features, embed, grads, *refs):
    outs, (g, passed, mids, loads, stores) = refs[:9], (refs[9], refs[10:13], refs[13:19], refs[19], refs[20])
    pulls, pushes = [], []

    def pull(source, target):
        pulls.append(pltpu.make_async_copy(source, target, loads.at[len(pulls)]))
        pulls[-1].start()
        return pulls[-1]

    def push(source, target):
        pushes.append(pltpu.make_async_copy(source, target, stores.at[len(pushes)]))
        pushes[-1].start()

    m_first, m_second, m_bottom, m_return, m_final, m_read = mids
    o_first, o_second, o_bottom, o_return, o_final, o_read = outs[3:]
    by_return = [pull(grads.at[n * 768 : (n + 1) * 768], g.at[n * 768 : (n + 1) * 768]) for n in range(3)]
    spots = [AT_BOTTOM + n * 768 for n in range(3)]
    by_bottom = [pull(grads.at[i : i + 768], g.at[i : i + 768]) for i in spots]
    through = [pull(features.at[n * 16 : (n + 1) * 16], passed[1].at[n * 16 : (n + 1) * 16]) for n in range(4)]
    tail = [pull(grads.at[AT_FINAL:AT_BOTTOM], g.at[AT_FINAL:AT_BOTTOM]), pull(grads.at[AT_SECOND:ROWS], g.at[AT_SECOND:ROWS])]
    small = [pull(logits, passed[0]), pull(embed, passed[2])]
    for ta in range(3):
        by_return[ta].wait()
        for tb in range(3):
            for half in range(2):
                start = AT_RETURN + ((ta * 3 + tb) * 2 + half) * 128
                m_return[ta, tb, :, half * 128 : (half + 1) * 128] = g[start : start + 128, :].astype(F32)
        push(m_return.at[ta], o_return.at[ta])
    for ta in range(3):
        by_bottom[ta].wait()
        for tb in range(3):
            start = AT_BOTTOM + (ta * 3 + tb) * 256
            m_bottom[ta, tb] = g[start : start + 256, :].astype(F32)
        push(m_bottom.at[ta], o_bottom.at[ta])
    for n in range(4):
        through[n].wait()
        push(passed[1].at[n * 16 : (n + 1) * 16], outs[1].at[n * 16 : (n + 1) * 16])
    for copy in tail:
        copy.wait()
    for t in range(9):
        ta, tb = t // 3, t % 3
        m_final[ta, tb] = g[AT_FINAL + t * 64 : AT_FINAL + (t + 1) * 64, :].astype(F32)
        m_second[ta, tb] = g[AT_SECOND + t * 64 : AT_SECOND + (t + 1) * 64, :].astype(F32)
        start, low = (AT_FIRST + ta * 64, tb * 64) if tb < 2 else (AT_FIRST + (192 if ta < 2 else 256), ta % 2 * 64)
        m_first[ta, tb] = g[start : start + 64, low : low + 64].astype(F32)
    m_read[...] = g[AT_READ : AT_READ + 16, 0:64].astype(F32)[0:2]
    for copy in small:
        copy.wait()
    for source, target in ((m_final, o_final), (m_second, o_second), (m_first, o_first), (m_read, o_read), (passed[0], outs[0]), (passed[2], outs[2])):
        push(source, target)
    for copy in pushes:
        copy.wait()


def write_out(logits, features, embed, g):
    shapes = [(2, 32, 128), (64, 32, 128), (16, 64), (3, 3, 64, 64), (3, 3, 64, 128), (3, 3, 256, 128), (3, 3, 128, 256), (3, 3, 64, 128), (2, 64)]
    hbm = pl.BlockSpec(memory_space=pl.ANY)
    outs = pl.pallas_call(
        out_kernel,
        out_shape=tuple(jax.ShapeDtypeStruct(s, BF if n == 1 else F32) for n, s in enumerate(shapes)),
        in_specs=[hbm] * 4,
        out_specs=(hbm,) * 9,
        scratch_shapes=[pltpu.VMEM((ROWS, 128), BF)]
        + [pltpu.VMEM(s, BF if n == 1 else F32) for n, s in enumerate(shapes)]
        + [pltpu.SemaphoreType.DMA((14,)), pltpu.SemaphoreType.DMA((16,))],
        compiler_params=pltpu.CompilerParams(vmem_limit_bytes=60 * 2**20),
    )(logits, features, embed, g)
    outs = list(outs)
    outs[2] = outs[2].T
    outs[4] = outs[4].transpose(0, 1, 3, 2)
    return tuple(outs)


def on_device(counts, *args):
    return write_out(*run_net(counts, *args))


def solution(mesh):
    counts = (mesh.shape["row"], mesh.shape["col"])
    cells = P(None, ("batch", "row"), "col")
    in_specs = (P(("batch", "row"), "col"),) + (P(),) * 7 + (cells,)
    out_specs = (cells, cells, P("batch", None)) + (P("batch", None, None, None),) * 5 + (P("batch", None),)
    return jax.shard_map(
        functools.partial(on_device, counts), mesh=mesh, in_specs=in_specs, out_specs=out_specs, check_vma=False
    )
```

```python
import functools

import jax
import jax.numpy as jnp
import numpy as np
from jax import lax
from jax.experimental import pallas as pl
from jax.experimental.pallas import tpu as pltpu
from jax.sharding import PartitionSpec as P

BF, F32 = jnp.bfloat16, jnp.float32
MESH = pl.DeviceIdType.MESH

DEEP, WIDE = 8, 32
CELLS = DEEP * WIDE
EXT = CELLS + 128

ROWS = 6272
PARTS = (
    (0, 1408, True, "x", "col"),
    (1408, 1536, True, "col", "x"),
    (2944, 1024, True, "x", "col"),
    (3968, 1280, True, "col", "x"),
    (5248, 640, False, "row", "col"),
    (5888, 384, False, "col", "row"),
)
AT_RETURN, AT_FINAL, AT_BOTTOM, AT_SECOND, AT_FIRST, AT_READ = 0, 2304, 2944, 5248, 5888, 6208


def ranged(values, start, size):
    return values.at[pl.ds(pl.multiple_of(start, 16), size), :]


def bounds(depth):
    left = 2 * WIDE * depth
    return WIDE * depth, left, left + 16, left + 32


def lane_of(r, q, depth):
    if not (-depth <= r < DEEP + depth and -depth <= q < WIDE + depth):
        return None
    row_in, col_in = 0 <= r < DEEP, 0 <= q < WIDE
    down, left, right, corner = bounds(depth)
    if row_in and col_in:
        return r * WIDE + q
    i = r + depth if r < 0 else r - DEEP
    j = q + depth if q < 0 else q - WIDE
    if col_in:
        return CELLS + (0 if r < 0 else down) + i * WIDE + q
    if row_in:
        return CELLS + (left if q < 0 else right) + j * DEEP + r
    return CELLS + corner + CORNERS[(-1 if r < 0 else 1, -1 if q < 0 else 1)] * depth * depth + i * depth + j


def shift_tables(depth, size):
    tables = []
    for dr in (-1, 0, 1):
        for dc in (-1, 0, 1):
            m = np.zeros((size, EXT), np.float32)
            for r in range(-1, DEEP + 1):
                for q in range(-1, WIDE + 1):
                    source = lane_of(r + dr, q + dc, depth)
                    if source is not None:
                        m[source, lane_of(r, q, 1)] = 1
            tables.append(m)
    return np.concatenate(tables)


def pick_table(depth):
    down, left, right, corner = bounds(depth)
    m = np.zeros((corner + 16, CELLS), np.float32)
    for i in range(depth):
        for q in range(WIDE):
            m[i * WIDE + q, i * WIDE + q] = 1
            m[down + i * WIDE + q, (DEEP - depth + i) * WIDE + q] = 1
        for r in range(DEEP):
            m[left + i * DEEP + r, r * WIDE + i] = 1
            m[right + i * DEEP + r, r * WIDE + WIDE - depth + i] = 1
        for j in range(depth):
            for k, (r, q) in enumerate(((0, 0), (0, WIDE - depth), (DEEP - depth, 0), (DEEP - depth, WIDE - depth))):
                m[corner + k * depth * depth + i * depth + j, (r + i) * WIDE + q + j] = 1
    return m


CORNERS = {(-1, -1): 3, (-1, 1): 2, (1, -1): 1, (1, 1): 0}


def spread_table():
    m = np.zeros((512, 512), np.float32)
    for r in range(4):
        for w in range(128):
            m[r * 128 + w, (w % 4) * 128 + r * WIDE + w // 4] = 1
    return m


SHIFT = shift_tables(1, EXT)
SHIFT_FAR = shift_tables(2, 512)
PICK, PICK_FAR = pick_table(1), pick_table(2)
SPREAD = spread_table()

UNDER = (((0,), (1, 2)), ((0, 1), (2,)))
OVER = ((2,), (1, 2), (0, 1), (0,))
BASE = (0, 1, 1, 2)


def mm(a, b):
    return jnp.dot(a, b, preferred_element_type=F32)


def nt(a, b):
    return lax.dot_general(a, b, (((1,), (1,)), ((), ())), preferred_element_type=F32)


def logistic(z):
    return 0.5 + 0.5 * jnp.tanh(0.5 * z)


def activated(v):
    stored = v.astype(BF)
    z = stored.astype(F32)
    return stored, (z * logistic(z)).astype(BF)


def sloped(incoming, stored):
    z = stored.astype(F32)
    s = logistic(z)
    return (incoming * (s * (1.0 + z * (1.0 - s)))).astype(BF)


def remote(src, dst, send, recv, target):
    return pltpu.make_async_remote_copy(
        src_ref=src, dst_ref=dst, send_sem=send, recv_sem=recv, device_id=target, device_id_type=MESH
    )


SIDES = ((-1, -1), (-1, 1), (1, -1), (1, 1), (0, -1), (0, 1), (-1, 0), (1, 0))


def net_kernel(counts, *refs):
    it = iter(refs)

    def take(n):
        return [next(it) for _ in range(n)]

    afar = take(15)
    logits_out, features_out, embed_ref, grads_out = take(4)
    xb, e0, z0, z1, f1, e1, z2, f2, e2, z3, e3, z4, e4, z5, f5, t5, t4, t3, t2, t1, fg, cp = take(22)
    w0, w1, w1b, w2, w2b, w3, w3b, w4, w4b, w5, w5b, r4, r4t = take(13)
    halos = [take(2) for _ in WIDTHS]
    near = take(15)
    syn, cU, cot, cQ, eye, embt, rdo, k1, cS, k2t, k3, k5, k4, cQ2, cF = near
    far, wide2, loads, logits_ref, features_ref, stores = take(6)
    sends, recvs = take(2)
    g_ref, whole, tall = take(3)
    stages = [take(6) for _ in PARTS]
    sum_sends, sum_recvs, embed_row, embed_col, embed_sends, embed_recvs = take(6)

    n_row, n_col = counts
    row, col = lax.axis_index("row"), lax.axis_index("col")
    there = {
        (-1, 0): row > 0,
        (1, 0): row < n_row - 1,
        (0, -1): col > 0,
        (0, 1): col < n_col - 1,
    }
    for dr in (-1, 1):
        for dc in (-1, 1):
            there[dr, dc] = jnp.logical_and(there[dr, 0], there[0, dc])

    def place(dr, dc):
        return {"row": (row + dr + n_row) % n_row, "col": (col + dc + n_col) % n_col}

    storing = []

    def store(source, target):
        storing.append(pltpu.make_async_copy(source, target, stores.at[len(storing)]))
        storing[-1].start()

    partners = [(d, 0) for d in range(1, n_row)] + [(0, d) for d in range(1, n_col)] + list(SIDES[:4])
    barrier = pltpu.get_barrier_semaphore()
    for partner in partners:
        pl.semaphore_signal(barrier, inc=1, device_id=place(*partner), device_id_type=MESH)

    loading = {}
    for n, (source, target) in enumerate(zip(afar, near)):
        loading[id(target)] = pltpu.make_async_copy(source, target, loads.at[n])
        loading[id(target)].start()

    def loaded(*targets):
        for target in targets:
            loading[id(target)].wait()

    lane = lax.broadcasted_iota(jnp.int32, (1, 128), 1)
    sixteen = lax.broadcasted_iota(jnp.int32, (16, 1), 0)

    def inside(depth):
        down, left, right, corner = bounds(depth)
        spans = [(0, down, (-1, 0)), (down, left, (1, 0)), (left, left + DEEP * depth, (0, -1)), (right, right + DEEP * depth, (0, 1))]
        spans += [(corner + k * depth * depth, corner + (k + 1) * depth * depth, side) for side, k in CORNERS.items()]
        masks = []
        for tile in range(depth):
            at = lane + tile * 128
            keep = lane < 0
            for low, high, side in spans:
                keep = jnp.logical_or(keep, jnp.logical_and(jnp.logical_and(at >= low, at < high), there[side]))
            masks.append(keep)
        return masks

    near_masks, far_masks = inside(1), inside(2)

    def fenced(v):
        return jnp.concatenate([v[:, :CELLS], jnp.where(near_masks[0], v[:, CELLS:], 0.0)], axis=1)

    def begin(n, depth, pieces, ahead=None):
        out, into = halos[n]
        down, left, right, corner = bounds(depth)
        pick = (cQ if depth == 1 else cQ2)[...]
        start = 0
        for piece in pieces:
            out[:, start : start + piece.shape[0]] = nt(pick, piece).astype(BF)
            start += piece.shape[0]
        size = {(-1, 0): (0, down, down), (1, 0): (down, left, 0), (0, -1): (left, right, right), (0, 1): (right, corner, left)}
        copies = []
        for k, (dr, dc) in enumerate(SIDES):
            if (dr, dc) in size:
                low, high, target = size[dr, dc]
            else:
                low, high = corner, corner + 16
                target = 128 * depth + 16 * CORNERS[-dr, -dc]
            copies.append(
                remote(out.at[low:high], into.at[target : target + high - low], sends.at[n, k], recvs.at[n, k], place(dr, dc))
            )
        if ahead is not None:
            ahead()
        for copy in copies:
            copy.start()
        return copies

    def end(n, depth, copies):
        into = halos[n][1]
        corner = bounds(depth)[3]
        for copy in copies:
            copy.wait()
        ends = 0.0
        for k in range(4):
            tile = into[128 * depth + 16 * k : 128 * depth + 16 * (k + 1), :].astype(F32)
            ends = ends + jnp.where(sixteen // (depth * depth) == k, tile, 0.0)
        into[corner : corner + 16, :] = ends.astype(BF)

    def ring(n, depth, start, width):
        into = halos[n][1]
        tiles = []
        for tile, keep in enumerate(near_masks if depth == 1 else far_masks):
            turned = nt(eye[0:width, 0:width], into[tile * 128 : (tile + 1) * 128, start : start + width])
            tiles.append(jnp.where(keep, turned, 0.0).astype(BF))
        return tiles

    def extend(p, width, ref, size):
        sides = {}
        for ea in range(p + 2):
            for eb in range(p + 2):
                way = (ea > p) - (ea < 1), (eb > p) - (eb < 1)
                if way != (0, 0):
                    source = (((ea - 1) % p + 1) * (p + 2) + (eb - 1) % p + 1) * width
                    sides.setdefault(way, []).append((source, (ea * (p + 2) + eb) * width))
        for (dr, dc), spots in sides.items():
            at = (dr * 3 + dc + 4) * EXT
            many = len(spots) * width
            first, target = spots[0]
            if dc == 0:
                held = ref[first : first + many, :]
            else:
                held = jnp.concatenate([ref[i : i + width, :] for i, _ in spots], axis=0)
            moved = mm(held, cS[at : at + EXT, 0:size]).astype(BF)
            if dc == 0:
                ref[target : target + many, 0:size] = moved
            else:
                for n, (_, target) in enumerate(spots):
                    ref[target : target + width, 0:size] = moved[n * width : (n + 1) * width, :]

    core, n_x = row % 2, n_row // 2
    ways = {
        "row": (row, n_row, lambda d: place(d, 0)),
        "col": (col, n_col, lambda d: place(0, d)),
        "x": (row // 2, n_x, lambda d: {"row": (row // 2 + d) % n_x * 2 + core}),
    }
    flying = {}

    def sum_step(part, step):
        start, size, paired, first, second = PARTS[part]
        s0, r0, held, s1, r1, r2 = stages[part]
        me1, n1, to1 = ways[first]
        me2, n2, to2 = ways[second]
        for copy in flying.pop(part, ()):
            copy.wait()
        if step == 5:
            store(whole.at[start : start + size], grads_out.at[start : start + size])
            return
        half = size // 2 if paired else size
        base = start + core * half if paired else start
        c1 = half // n1
        own = pl.ds(pl.multiple_of(base + me1 * c1, 16), c1)
        partner = {"row": row + 1 - 2 * core}
        moves = []
        if step == 0:
            s0[...] = g_ref[pl.ds(pl.multiple_of(start + (1 - core) * half, 16), half), :].astype(BF)
            moves.append((s0, r0, partner))
        elif step == 1:
            total = g_ref[pl.ds(pl.multiple_of(base, 16), half), :] if paired else g_ref[base : base + half, :]
            if paired:
                total = total + r0[...].astype(F32)
            held[...] = total
            s1[...] = total.astype(BF)
            moves = [(ranged(s1, (me1 + d) % n1 * c1, c1), r1.at[d - 1], to1(d)) for d in range(1, n1)]
        elif step == 2:
            total = held[pl.ds(pl.multiple_of(me1 * c1, 16), c1), :]
            for d in range(n1 - 1):
                total = total + r1[d].astype(F32)
            r2[me2] = total.astype(BF)
            moves = [(r2.at[me2], r2.at[me2], to2(d)) for d in range(1, n2)]
        elif step == 3:
            whole[own, :] = sum(r2[d].astype(F32) for d in range(n2)).astype(BF)
            moves = [(whole.at[own, :], whole.at[own, :], to1(d)) for d in range(1, n1)]
        elif paired:
            mine = ranged(whole, base, half)
            moves.append((mine, mine, partner))
        copies = [
            remote(src, dst, sum_sends.at[part, step, k], sum_recvs.at[part, step, k], to) for k, (src, dst, to) in enumerate(moves)
        ]
        for copy in copies:
            copy.start()
        flying[part] = copies

    def embed_step(step, value=None):
        if step > 0:
            for copy in flying.pop("embed"):
                copy.wait()
            slots = embed_row if step == 1 else embed_col
            value = sum(slots[d] for d in range(slots.shape[0]))
        if step == 2:
            return value
        slots, (me, count, to) = (embed_row, ways["row"]) if step == 0 else (embed_col, ways["col"])
        slots[me] = value
        copies = [
            remote(slots.at[me], slots.at[me], embed_sends.at[step, d], embed_recvs.at[step, d], to(d)) for d in range(1, count)
        ]
        for copy in copies:
            copy.start()
        flying["embed"] = copies

    loaded(syn, cU)
    bit = lax.broadcasted_iota(jnp.int32, (16, 1), 0)
    groups = []
    for a in range(4):
        for t in range(2):
            line = [(syn[16 * t + 4 * r + a : 16 * t + 4 * r + a + 1, :] >> bit) & 1 for r in range(4)]
            groups.append(jnp.concatenate(line, axis=1))
    bits = jnp.concatenate(groups, axis=0).astype(F32).astype(BF)
    phased = mm(bits, cU[...]).astype(BF)
    for a in range(4):
        for t in range(2):
            for b in range(4):
                start = ((a + 1) * 6 + b + 1) * 16
                xb[start : start + 16, t * 128 : (t + 1) * 128] = phased[(a * 2 + t) * 16 : (a * 2 + t + 1) * 16, b * 128 : (b + 1) * 128]
    loaded(cot)
    wide = cot[...].astype(F32)
    groups = []
    for a in range(4):
        for t in range(2):
            line = jnp.concatenate([wide[:, 16 * t + 4 * r + a, :] for r in range(4)], axis=1)
            groups.append(jnp.concatenate([line, jnp.zeros((6, 512), F32)], axis=0))
    phased = mm(jnp.concatenate(groups, axis=0).astype(BF), cU[...])
    for a in range(4):
        for t in range(2):
            start = (a * 2 + t) * 8
            pieces = [phased[start : start + 4, b * 128 : (b + 1) * 128] for b in range(4)]
            cp[a * 16 : (a + 1) * 16, t * 128 : (t + 1) * 128] = jnp.concatenate(pieces, axis=0).astype(BF)

    loaded(cQ)
    inner = [((a + 1) * 6 + 1) * 16 for a in range(4)]
    pieces = [jnp.concatenate([xb[i : i + 64, 0:CELLS] for i in inner], axis=0), cp[:, 0:CELLS]]
    copies = begin(0, 1, pieces, lambda: pl.semaphore_wait(barrier, len(partners)))

    def beside(blocks, i, blank):
        return jnp.concatenate(blocks + [blank] if i == 0 else [blank] + blocks, axis=0)

    def added(k, rows, cols):
        return sum(k[ta, tb].astype(F32) for ta in rows for tb in cols).astype(BF)

    def arrange_first():
        repeat = (lax.broadcasted_iota(jnp.int32, (16, 96), 1) % 16 == lax.broadcasted_iota(jnp.int32, (16, 96), 0)).astype(F32).astype(BF)
        tiled = mm(nt(eye[:64, :64], embt[...]).astype(BF), repeat)
        own = lax.broadcasted_iota(jnp.int32, (64, 96), 1) // 16
        for j in range(6):
            w0[j * 64 : (j + 1) * 64, :] = jnp.where(own == j, tiled, 0.0).astype(BF)
        for ta in range(3):
            for i in range(2):
                w1[i * 64 : (i + 1) * 64, ta * 256 : (ta + 1) * 256] = sum(
                    mm(k1[ta, tb], eye[(tb + i) * 64 : (tb + i + 1) * 64, :]) for tb in range(3)
                ).astype(BF)

    def arrange_second():
        blank, empty = jnp.zeros((64, 128), BF), jnp.zeros((64, 64), BF)
        for ta in range(3):
            for i in range(2):
                line = beside([k2t[ta, tb] for tb in range(3)], i, blank)
                w2[i * 128 : (i + 1) * 128, ta * 256 : (ta + 1) * 256] = nt(eye[:128, :128], line).astype(BF)
                for tb in range(3):
                    w2b[i * 64 : (i + 1) * 64, ta * 512 + (tb + i) * 128 : ta * 512 + (tb + i + 1) * 128] = k2t[2 - ta, 2 - tb]
                hole = ta * 512 + (384 if i == 0 else 0)
                w2b[i * 64 : (i + 1) * 64, hole : hole + 128] = blank
                line = beside([k1[2 - ta, 2 - tb] for tb in range(3)], i, empty)
                w1b[i * 64 : (i + 1) * 64, ta * 256 : (ta + 1) * 256] = nt(eye[:64, :64], line).astype(BF)

    def arrange_bottom():
        for t in range(9):
            w3[:, t * 128 : (t + 1) * 128] = k3[t // 3, t % 3]
            w3b[:, t * 256 : (t + 1) * 256] = nt(eye[:128, :128], k3[2 - t // 3, 2 - t % 3]).astype(BF)

    def arrange_return():
        for pa in range(2):
            for pb in range(2):
                for s in range(2):
                    for u in range(2):
                        block = added(k4, UNDER[pa][s], UNDER[pb][u])
                        w4[(pa * 2 + pb) * 128 : (pa * 2 + pb + 1) * 128, (s * 2 + u) * 256 : (s * 2 + u + 1) * 256] = block
                        at = OVER.index(UNDER[pa][s]) * 4 + OVER.index(UNDER[pb][u])
                        w4b[:, at * 128 : (at + 1) * 128] = nt(eye[...], block).astype(BF)

    def arrange_final():
        for pa in range(2):
            for pb in range(2):
                for s in range(2):
                    for u in range(2):
                        start = pa * 128 + (1 - pb) * 64
                        w5[start : start + 64, (s * 2 + u) * 128 : (s * 2 + u + 1) * 128] = added(k5, UNDER[pa][s], UNDER[pb][u])
        for ea in range(4):
            for pair in range(2):
                stack = jnp.concatenate([added(k5, OVER[ea], OVER[2 * pair + i]) for i in range(2)], axis=0)
                at = ea * 2 + pair
                w5b[:, at * 128 : (at + 1) * 128] = nt(eye[:128, :128], stack).astype(BF)

    def arrange_readout():
        repeat = (lax.broadcasted_iota(jnp.int32, (64, 256), 1) % 64 == lax.broadcasted_iota(jnp.int32, (64, 256), 0)).astype(F32).astype(BF)
        tiled = mm(rdo[...], repeat)
        tiled = jnp.concatenate([tiled, jnp.zeros((2, 256), F32)] * 4, axis=0)
        own = lax.broadcasted_iota(jnp.int32, (16, 256), 1) // 64 == lax.broadcasted_iota(jnp.int32, (16, 256), 0) // 4
        r4[...] = jnp.where(own, tiled, 0.0).astype(BF)
        r4t[...] = nt(eye[...], r4[...]).astype(BF)

    loaded(eye, embt, rdo, k1)
    arrange_first()
    arrange_readout()
    loaded(k2t)
    arrange_second()
    loaded(cS)
    end(0, 1, copies)
    (tile,) = ring(0, 1, 0, 256)
    for a in range(4):
        xb[inner[a] : inner[a] + 64, CELLS:EXT] = tile[a * 64 : (a + 1) * 64, :]
    cp[:, CELLS:EXT] = ring(0, 1, 256, 64)[0]
    extend(4, 16, xb, EXT)

    for ea in range(6):
        stored, active = activated(mm(w0[...], xb[ea * 96 : (ea + 1) * 96, :]))
        e0[ea * 384 : (ea + 1) * 384, :] = active
        if 1 <= ea <= 4:
            z0[(ea - 1) * 256 : ea * 256, :] = stored[64:320, 0:CELLS]

    for a in range(4):
        for pair in range(2):
            v = sum(
                mm(w1[:, ta * 256 : (ta + 1) * 256], e0[((a + ta) * 6 + 2 * pair) * 64 : ((a + ta) * 6 + 2 * pair + 4) * 64, :])
                for ta in range(3)
            )
            start = (a * 4 + 2 * pair) * 64
            z1[start : start + 128, :], f1[start : start + 128, :] = activated(fenced(v))

    def pooled(ref, side, width, a, b, size):
        spots = [((2 * a + i) * side + 2 * b + j) * width for i in range(2) for j in range(2)]
        return (sum(ref[s : s + width, 0:size].astype(F32) for s in spots) * 0.25).astype(BF)

    for a in range(2):
        for b in range(2):
            start = ((a + 1) * 4 + b + 1) * 64
            e1[start : start + 64, :] = pooled(f1, 4, 64, a, b, EXT)
    extend(2, 64, e1, CELLS)

    for a in range(2):
        v = sum(mm(w2[:, ta * 256 : (ta + 1) * 256], e1[(a + ta) * 256 : (a + ta + 1) * 256, 0:CELLS]) for ta in range(3))
        z2[a * 256 : (a + 1) * 256, 0:CELLS], f2[a * 256 : (a + 1) * 256, 0:CELLS] = activated(v)
    e2[4 * 128 : 5 * 128, 0:CELLS] = pooled(f2, 2, 128, 0, 0, CELLS)
    loaded(cQ2)
    copies = begin(1, 2, [e2[4 * 128 : 5 * 128, 0:CELLS]])
    later = begin(2, 1, [z2[0:256, 0:CELLS], z2[256:512, 0:CELLS]])
    loaded(k3, k5)
    arrange_bottom()
    arrange_final()
    loaded(k4)
    arrange_return()
    loaded(cF)
    end(1, 2, copies)
    wide2[:, 0:CELLS] = e2[4 * 128 : 5 * 128, 0:CELLS]
    wide2[:, 256:384], wide2[:, 384:512] = ring(1, 2, 0, 128)
    for n in range(9):
        e2[n * 128 : (n + 1) * 128, :] = mm(wide2[...], cF[n * 512 : (n + 1) * 512, :]).astype(BF)

    stored, e3[4 * 256 : 5 * 256, :] = activated(fenced(mm(w3[...], e2[...])))
    z3[...] = stored[:, 0:CELLS]
    end(2, 1, later)
    for a in range(2):
        z2[a * 256 : (a + 1) * 256, CELLS:EXT] = ring(2, 1, a * 256, 256)[0]
        f2[a * 256 : (a + 1) * 256, CELLS:EXT] = activated(z2[a * 256 : (a + 1) * 256, CELLS:EXT])[1]
    extend(1, 256, e3, EXT)

    for a in range(2):
        for b in range(2):
            n = a * 2 + b
            v = sum(
                mm(w4[n * 128 : (n + 1) * 128, s * 512 : (s + 1) * 512], e3[((a + s) * 3 + b) * 256 : ((a + s) * 3 + b + 2) * 256, :])
                for s in range(2)
            )
            v = v + f2[n * 128 : (n + 1) * 128, :].astype(F32)
            start = ((a + 1) * 4 + b + 1) * 128
            z4[n * 128 : (n + 1) * 128, :], e4[start : start + 128, :] = activated(fenced(v))
    extend(2, 128, e4, EXT)

    RUNS = ((0, 1, 64, 64), (1, 2, 0, 128), (3, 1, 0, 64))
    for a in range(4):
        for b, many, first, size in RUNS:
            base = (a % 2) * 128 + first
            v = sum(
                mm(w5[base : base + size, s * 256 : (s + 1) * 256], e4[((BASE[a] + s) * 4 + BASE[b]) * 128 : ((BASE[a] + s) * 4 + BASE[b] + 2) * 128, :])
                for s in range(2)
            )
            start = (a * 4 + b) * 64
            v = v + f1[start : start + size, :].astype(F32)
            z5[start : start + size, :] = v.astype(BF)

    for a in range(4):
        back = mm(r4t[...], cp[a * 16 : (a + 1) * 16, :])
        start = ((a + 1) * 6 + 1) * 64
        t5[start : start + 256, :] = sloped(back, z5[a * 256 : (a + 1) * 256, :])
    extend(4, 64, t5, CELLS)
    for a in range(2):
        for b in range(2):
            v = sum(
                mm(w5b[:, m * 256 : (m + 1) * 256], t5[((2 * a + m) * 6 + 2 * b) * 64 : ((2 * a + m) * 6 + 2 * b + 4) * 64, 0:CELLS])
                for m in range(4)
            )
            start = ((a + 1) * 4 + b + 1) * 128
            n = a * 2 + b
            t4[start : start + 128, 0:CELLS] = sloped(v, z4[n * 128 : (n + 1) * 128, 0:CELLS])
    copies = begin(3, 1, [t4[((a + 1) * 4 + 1) * 128 : ((a + 1) * 4 + 3) * 128, 0:CELLS] for a in range(2)])

    sums = {}
    for a in range(4):
        for s in range(2):
            for b, many, first, size in RUNS:
                start = ((BASE[a] + s) * 4 + BASE[b]) * 128
                t_start = ((a + 1) * 6 + b + 1) * 64
                product = nt(t5[t_start : t_start + size, 0:CELLS], e4[start : start + 256, 0:CELLS])
                for m in range(many):
                    key = (a % 2, s, (b + m) % 2)
                    block = product[m * 64 : (m + 1) * 64, :]
                    sums[key] = sums[key] + block if key in sums else block

    def reads(parity, tap):
        return 0 if tap in UNDER[parity][0] else 1

    for ta in range(3):
        rowed = [sums[0, reads(0, ta), pb] + sums[1, reads(1, ta), pb] for pb in range(2)]
        for tb in range(3):
            value = sum(rowed[pb][:, reads(pb, tb) * 128 : (reads(pb, tb) + 1) * 128] for pb in range(2))
            start = AT_FINAL + (ta * 3 + tb) * 64
            g_ref[start : start + 64, :] = value

    for b in range(2):
        for u in range(2):
            parts = {}
            for a in range(2):
                for s in range(2):
                    start = ((a + 1) * 4 + b + 1) * 128
                    from_ = ((a + s) * 3 + b + u) * 256
                    parts[a, s] = nt(t4[start : start + 128, 0:CELLS], e3[from_ : from_ + 256, 0:CELLS])
            for ta in range(3):
                value = parts[0, reads(0, ta)] + parts[1, reads(1, ta)]
                for tb in UNDER[b][u]:
                    for half in range(2):
                        start = AT_RETURN + ((ta * 3 + tb) * 2 + half) * 128
                        piece = value[:, half * 128 : (half + 1) * 128]
                        g_ref[start : start + 128, :] = piece if b == 0 else g_ref[start : start + 128, :] + piece

    g_ref[AT_FINAL + 576 : AT_BOTTOM, :] = jnp.zeros((AT_BOTTOM - AT_FINAL - 576, 128), F32)
    sum_step(0, 0)
    sum_step(1, 0)
    total = jnp.zeros((16, 256), F32)
    for a in range(4):
        f5[a * 256 : (a + 1) * 256, :] = activated(z5[a * 256 : (a + 1) * 256, 0:CELLS])[1]
        total = total + nt(cp[a * 16 : (a + 1) * 16, 0:CELLS], f5[a * 256 : (a + 1) * 256, :])
    total = sum(total[b * 4 : (b + 1) * 4, b * 64 : (b + 1) * 64] for b in range(4))
    g_ref[AT_READ:ROWS, :] = jnp.zeros((ROWS - AT_READ, 128), F32)
    g_ref[AT_READ : AT_READ + 4, 0:64] = total

    sum_step(0, 1)
    sum_step(1, 1)
    end(3, 1, copies)
    for a in range(2):
        start = ((a + 1) * 4 + 1) * 128
        t4[start : start + 256, CELLS:EXT] = ring(3, 1, a * 256, 256)[0]
    extend(2, 128, t4, CELLS)
    v = sum(mm(w4b[:, m * 512 : (m + 1) * 512], t4[m * 512 : (m + 1) * 512, 0:CELLS]) for m in range(4))
    far[:, 0:CELLS] = sloped(v, z3[...])
    copies = begin(4, 2, [far[:, 0:CELLS]])
    for t in range(9):
        g_ref[AT_BOTTOM + t * 256 : AT_BOTTOM + (t + 1) * 256, :] = nt(far[:, 0:CELLS], e2[t * 128 : (t + 1) * 128, 0:CELLS])
    sum_step(2, 0)
    sum_step(3, 0)
    groups = []
    for a in range(4):
        here = f5[a * 256 : (a + 1) * 256, :]
        value = mm(r4[...], here)
        for t in range(2):
            groups.append(jnp.concatenate([value[b * 4 : (b + 1) * 4, t * 128 : (t + 1) * 128] for b in range(4)], axis=1))
    value = jnp.concatenate(groups, axis=0)
    laid = 0.0
    for _ in range(3):
        piece = value.astype(BF)
        laid = laid + nt(piece, cU[...])
        value = value - piece.astype(F32)
    for a in range(4):
        for t in range(2):
            for r in range(4):
                h = 16 * t + 4 * r + a
                logits_ref[:, h : h + 1, :] = laid[(a * 2 + t) * 4 : (a * 2 + t) * 4 + 2, r * 128 : (r + 1) * 128].reshape(2, 1, 128)
    store(logits_ref, logits_out)
    sum_step(2, 1)
    sum_step(3, 1)
    end(4, 2, copies)
    far[:, 256:384], far[:, 384:512] = ring(4, 2, 0, 256)
    for n in range(9):
        t3[n * 256 : (n + 1) * 256, :] = mm(far[...], cF[n * 512 : (n + 1) * 512, :]).astype(BF)

    sum_step(0, 2)
    sum_step(1, 2)
    through = mm(w3b[...], t3[...]) * 0.25
    for a in range(2):
        for b in range(2):
            n = a * 2 + b
            start = ((a + 1) * 4 + b + 1) * 128
            v = fenced(t4[start : start + 128, :].astype(F32) + through)
            t2[start : start + 128, :] = sloped(v, z2[n * 128 : (n + 1) * 128, :])
    for ta in range(3):
        product = 0.0
        for a in range(2):
            start = ((a + 1) * 4 + 1) * 128
            product = product + nt(e1[(a + ta) * 256 : (a + ta + 1) * 256, 0:CELLS], t2[start : start + 256, 0:CELLS])
        g_ref[AT_SECOND + ta * 192 : AT_SECOND + (ta + 1) * 192, :] = product[0:192, 0:128] + product[64:256, 128:256]
    g_ref[AT_SECOND + 576 : AT_FIRST, :] = jnp.zeros((AT_FIRST - AT_SECOND - 576, 128), F32)
    sum_step(4, 1)
    extend(2, 128, t2, EXT)

    for a in range(2):
        v = sum(mm(w2b[:, ta * 512 : (ta + 1) * 512], t2[(a + ta) * 512 : (a + ta + 1) * 512, :]) for ta in range(3)) * 0.25
        for b in range(2):
            for i in range(2):
                for j in range(2):
                    fa, fb = 2 * a + i, 2 * b + j
                    start = ((fa + 1) * 6 + fb + 1) * 64
                    n = (fa * 4 + fb) * 64
                    t1[start : start + 64, :] = sloped(fenced(t5[start : start + 64, :].astype(F32) + v[b * 64 : (b + 1) * 64, :]), z1[n : n + 64, :])
    sum_step(2, 2)
    sum_step(3, 2)
    for ta in range(3):
        product = 0.0
        for a in range(4):
            for pair in range(2):
                start = ((a + 1) * 6 + 2 * pair + 1) * 64
                from_ = ((a + ta) * 6 + 2 * pair) * 64
                product = product + nt(t1[start : start + 128, 0:CELLS], e0[from_ : from_ + 256, 0:CELLS])
        value = product[0:64, 0:192] + product[64:128, 64:256]
        g_ref[AT_FIRST + ta * 64 : AT_FIRST + (ta + 1) * 64, :] = value[:, 0:128]
        start = AT_FIRST + (192 if ta < 2 else 256)
        g_ref[start : start + 64, ta % 2 * 64 : ta % 2 * 64 + 64] = value[:, 128:192]
    g_ref[AT_FIRST + 256 : AT_FIRST + 320, 64:128] = jnp.zeros((64, 64), F32)
    sum_step(5, 1)
    sum_step(0, 3)
    sum_step(1, 3)
    extend(4, 64, t1, CELLS)

    total = jnp.zeros((64, 256), F32)
    for a in range(4):
        for pair in range(2):
            v = sum(
                mm(w1b[:, ta * 256 : (ta + 1) * 256], t1[((a + ta) * 6 + 2 * pair) * 64 : ((a + ta) * 6 + 2 * pair + 4) * 64, 0:CELLS])
                for ta in range(3)
            )
            start = (a * 4 + 2 * pair) * 64
            fg[start : start + 128, :] = sloped(v, z0[start : start + 128, :])
        start = ((a + 1) * 6 + 1) * 16
        total = total + nt(xb[start : start + 64, 0:CELLS], fg[a * 256 : (a + 1) * 256, :])
    total = sum(total[b * 16 : (b + 1) * 16, b * 64 : (b + 1) * 64] for b in range(4))
    embed_step(0, total)

    def lay(a):
        for t in range(2):
            line = jnp.concatenate([fg[(a * 4 + b) * 64 : (a * 4 + b + 1) * 64, t * 128 : (t + 1) * 128] for b in range(4)], axis=1)
            laid = nt(line, cU[...])
            for r in range(4):
                tall[:, 16 * t + 4 * r + a, :] = laid[:, r * 128 : (r + 1) * 128]

    sum_step(4, 2)
    lay(0)
    lay(1)
    sum_step(2, 3)
    sum_step(3, 3)
    sum_step(5, 2)
    lay(2)
    lay(3)
    sum_step(0, 4)
    sum_step(1, 4)
    embed_step(1)
    features_ref[...] = tall[...].astype(BF)
    store(features_ref, features_out)
    sum_step(4, 3)
    sum_step(2, 4)
    sum_step(3, 4)
    sum_step(5, 3)
    embed_ref[...] = embed_step(2)
    for part in (0, 1, 4, 2, 3, 5):
        sum_step(part, 5)
    for copy in storing:
        copy.wait()


WIDTHS = ((384, 1), (128, 2), (512, 1), (512, 1), (256, 2))


def run_net(counts, *args):
    syn, emb, k1, k2, *rest = args
    k3, k4, k5, rdo, cot = rest
    eye, pick, pick_far, spread, near, far = [jnp.asarray(t, BF) for t in (np.eye(CELLS), PICK, PICK_FAR, SPREAD, SHIFT, SHIFT_FAR)]
    afar = (syn, spread, cot, pick, eye, emb.T, rdo, k1, near, k2.transpose(0, 1, 3, 2), k3, k5, k4, pick_far, far)
    wide, own = (EXT,), (CELLS,)
    blocks = [(16 * 36,) + wide, (64 * 36,) + wide, (1024,) + own, (1024,) + wide, (1024,) + wide, (1024,) + wide]
    blocks += [(512,) + wide, (512,) + wide, (128 * 9,) + wide, (256,) + own, (256 * 9,) + wide, (512,) + wide, (128 * 16,) + wide]
    blocks += [(1024,) + wide, (1024,) + own, (64 * 36,) + wide, (128 * 16,) + wide, (256 * 9,) + wide, (128 * 16,) + wide]
    blocks += [(64 * 36,) + wide, (1024,) + own, (64,) + wide]
    weights = [(384, 96), (128, 768), (128, 768), (256, 768), (128, 1536), (256, 1152), (128, 2304), (512, 1024), (256, 2048), (256, 512), (128, 1024), (16, 256), (256, 16)]
    scratch = [pltpu.VMEM(s, BF) for s in blocks + weights]
    for width, depth in WIDTHS:
        scratch += [pltpu.VMEM((bounds(depth)[3] + 16, width), BF), pltpu.VMEM((128 * depth + 64, width), BF)]
    scratch += [pltpu.VMEM(x.shape, x.dtype) for x in afar]
    scratch += [pltpu.VMEM((256, 512), BF), pltpu.VMEM((128, 512), BF), pltpu.SemaphoreType.DMA((15,)), pltpu.VMEM((2, 32, 128), F32), pltpu.VMEM((64, 32, 128), BF)]
    scratch += [pltpu.SemaphoreType.DMA((2 + len(PARTS),))]
    scratch += [pltpu.SemaphoreType.DMA((len(WIDTHS), 8)), pltpu.SemaphoreType.DMA((len(WIDTHS), 8))]
    scratch += [pltpu.VMEM((ROWS, 128), F32), pltpu.VMEM((ROWS, 128), BF), pltpu.VMEM((64, 32, 128), F32)]
    n_row, n_col = counts
    most = max(n_row, n_col)
    along = {"row": n_row, "col": n_col, "x": n_row // 2}
    for _, size, paired, first, second in PARTS:
        half = size // 2 if paired else size
        n1, n2 = along[first], along[second]
        c1, pair = half // n1, half if paired else 16
        scratch += [
            pltpu.VMEM((pair, 128), BF),
            pltpu.VMEM((pair, 128), BF),
            pltpu.VMEM((half, 128), F32),
            pltpu.VMEM((half, 128), BF),
            pltpu.VMEM((n1 - 1, c1, 128), BF),
            pltpu.VMEM((n2, c1, 128), BF),
        ]
    scratch += [pltpu.SemaphoreType.DMA((len(PARTS), 5, most)), pltpu.SemaphoreType.DMA((len(PARTS), 5, most))]
    scratch += [pltpu.VMEM((n_row, 16, 64), F32), pltpu.VMEM((n_col, 16, 64), F32)]
    scratch += [pltpu.SemaphoreType.DMA((2, most)), pltpu.SemaphoreType.DMA((2, most))]
    vmem, hbm = pl.BlockSpec(memory_space=pltpu.VMEM), pl.BlockSpec(memory_space=pl.ANY)
    return pl.pallas_call(
        functools.partial(net_kernel, counts),
        out_shape=(
            jax.ShapeDtypeStruct((2, 32, 128), F32),
            jax.ShapeDtypeStruct((64, 32, 128), BF),
            jax.ShapeDtypeStruct((16, 64), F32),
            jax.ShapeDtypeStruct((ROWS, 128), BF),
        ),
        in_specs=[hbm] * 15,
        out_specs=(hbm, hbm, vmem, hbm),
        scratch_shapes=scratch,
        compiler_params=pltpu.CompilerParams(collective_id=1, has_side_effects=True, vmem_limit_bytes=56 * 2**20),
    )(*afar)


def out_kernel(logits, features, embed, grads, *refs):
    outs, (g, passed, mids, loads, stores) = refs[:9], (refs[9], refs[10:13], refs[13:19], refs[19], refs[20])
    pulls, pushes = [], []

    def pull(source, target):
        pulls.append(pltpu.make_async_copy(source, target, loads.at[len(pulls)]))
        pulls[-1].start()
        return pulls[-1]

    def push(source, target):
        pushes.append(pltpu.make_async_copy(source, target, stores.at[len(pushes)]))
        pushes[-1].start()

    m_first, m_second, m_bottom, m_return, m_final, m_read = mids
    o_first, o_second, o_bottom, o_return, o_final, o_read = outs[3:]
    by_return = [pull(grads.at[n * 768 : (n + 1) * 768], g.at[n * 768 : (n + 1) * 768]) for n in range(3)]
    spots = [AT_BOTTOM + n * 768 for n in range(3)]
    by_bottom = [pull(grads.at[i : i + 768], g.at[i : i + 768]) for i in spots]
    through = [pull(features.at[n * 16 : (n + 1) * 16], passed[1].at[n * 16 : (n + 1) * 16]) for n in range(4)]
    tail = [pull(grads.at[AT_FINAL:AT_BOTTOM], g.at[AT_FINAL:AT_BOTTOM]), pull(grads.at[AT_SECOND:ROWS], g.at[AT_SECOND:ROWS])]
    small = [pull(logits, passed[0]), pull(embed, passed[2])]
    for ta in range(3):
        by_return[ta].wait()
        for tb in range(3):
            for half in range(2):
                start = AT_RETURN + ((ta * 3 + tb) * 2 + half) * 128
                m_return[ta, tb, :, half * 128 : (half + 1) * 128] = g[start : start + 128, :].astype(F32)
        push(m_return.at[ta], o_return.at[ta])
    for ta in range(3):
        by_bottom[ta].wait()
        for tb in range(3):
            start = AT_BOTTOM + (ta * 3 + tb) * 256
            m_bottom[ta, tb] = g[start : start + 256, :].astype(F32)
        push(m_bottom.at[ta], o_bottom.at[ta])
    for n in range(4):
        through[n].wait()
        push(passed[1].at[n * 16 : (n + 1) * 16], outs[1].at[n * 16 : (n + 1) * 16])
    for copy in tail:
        copy.wait()
    for t in range(9):
        ta, tb = t // 3, t % 3
        m_final[ta, tb] = g[AT_FINAL + t * 64 : AT_FINAL + (t + 1) * 64, :].astype(F32)
        m_second[ta, tb] = g[AT_SECOND + t * 64 : AT_SECOND + (t + 1) * 64, :].astype(F32)
        start, low = (AT_FIRST + ta * 64, tb * 64) if tb < 2 else (AT_FIRST + (192 if ta < 2 else 256), ta % 2 * 64)
        m_first[ta, tb] = g[start : start + 64, low : low + 64].astype(F32)
    m_read[...] = g[AT_READ : AT_READ + 16, 0:64].astype(F32)[0:2]
    for copy in small:
        copy.wait()
    for source, target in ((m_final, o_final), (m_second, o_second), (m_first, o_first), (m_read, o_read), (passed[0], outs[0]), (passed[2], outs[2])):
        push(source, target)
    for copy in pushes:
        copy.wait()


def write_out(logits, features, embed, g):
    shapes = [(2, 32, 128), (64, 32, 128), (16, 64), (3, 3, 64, 64), (3, 3, 64, 128), (3, 3, 256, 128), (3, 3, 128, 256), (3, 3, 64, 128), (2, 64)]
    hbm = pl.BlockSpec(memory_space=pl.ANY)
    outs = pl.pallas_call(
        out_kernel,
        out_shape=tuple(jax.ShapeDtypeStruct(s, BF if n == 1 else F32) for n, s in enumerate(shapes)),
        in_specs=[hbm] * 4,
        out_specs=(hbm,) * 9,
        scratch_shapes=[pltpu.VMEM((ROWS, 128), BF)]
        + [pltpu.VMEM(s, BF if n == 1 else F32) for n, s in enumerate(shapes)]
        + [pltpu.SemaphoreType.DMA((14,)), pltpu.SemaphoreType.DMA((16,))],
        compiler_params=pltpu.CompilerParams(vmem_limit_bytes=60 * 2**20),
    )(logits, features, embed, g)
    outs = list(outs)
    outs[2] = outs[2].T
    outs[4] = outs[4].transpose(0, 1, 3, 2)
    return tuple(outs)


def on_device(counts, *args):
    return write_out(*run_net(counts, *args))


def solution(mesh):
    counts = (mesh.shape["row"], mesh.shape["col"])
    cells = P(None, ("batch", "row"), "col")
    in_specs = (P(("batch", "row"), "col"),) + (P(),) * 7 + (cells,)
    out_specs = (cells, cells, P("batch", None)) + (P("batch", None, None, None),) * 5 + (P("batch", None),)
    return jax.shard_map(
        functools.partial(on_device, counts), mesh=mesh, in_specs=in_specs, out_specs=out_specs, check_vma=False
    )
```

```python
import functools

import jax
import jax.numpy as jnp
import numpy as np
from jax import lax
from jax.experimental import pallas as pl
from jax.experimental.pallas import tpu as pltpu
from jax.sharding import PartitionSpec as P

BF, F32 = jnp.bfloat16, jnp.float32
MESH = pl.DeviceIdType.MESH

DEEP, WIDE = 8, 32
CELLS = DEEP * WIDE
EXT = CELLS + 128

ROWS = 6272
PARTS = (
    (0, 1408, True, "x", "col"),
    (1408, 1536, True, "col", "x"),
    (2944, 1024, True, "x", "col"),
    (3968, 1280, True, "col", "x"),
    (5248, 640, False, "row", "col"),
    (5888, 384, False, "col", "row"),
)
AT_RETURN, AT_FINAL, AT_BOTTOM, AT_SECOND, AT_FIRST, AT_READ = 0, 2304, 2944, 5248, 5888, 6208


def ranged(values, start, size):
    return values.at[pl.ds(pl.multiple_of(start, 16), size), :]


def bounds(depth):
    left = 2 * WIDE * depth
    return WIDE * depth, left, left + 16, left + 32


def lane_of(r, q, depth):
    if not (-depth <= r < DEEP + depth and -depth <= q < WIDE + depth):
        return None
    row_in, col_in = 0 <= r < DEEP, 0 <= q < WIDE
    down, left, right, corner = bounds(depth)
    if row_in and col_in:
        return r * WIDE + q
    i = r + depth if r < 0 else r - DEEP
    j = q + depth if q < 0 else q - WIDE
    if col_in:
        return CELLS + (0 if r < 0 else down) + i * WIDE + q
    if row_in:
        return CELLS + (left if q < 0 else right) + j * DEEP + r
    return CELLS + corner + CORNERS[(-1 if r < 0 else 1, -1 if q < 0 else 1)] * depth * depth + i * depth + j


def shift_tables(depth, size):
    tables = []
    for dr in (-1, 0, 1):
        for dc in (-1, 0, 1):
            m = np.zeros((size, EXT), np.float32)
            for r in range(-1, DEEP + 1):
                for q in range(-1, WIDE + 1):
                    source = lane_of(r + dr, q + dc, depth)
                    if source is not None:
                        m[source, lane_of(r, q, 1)] = 1
            tables.append(m)
    return np.concatenate(tables)


def pick_table(depth):
    down, left, right, corner = bounds(depth)
    m = np.zeros((corner + 16, CELLS), np.float32)
    for i in range(depth):
        for q in range(WIDE):
            m[i * WIDE + q, i * WIDE + q] = 1
            m[down + i * WIDE + q, (DEEP - depth + i) * WIDE + q] = 1
        for r in range(DEEP):
            m[left + i * DEEP + r, r * WIDE + i] = 1
            m[right + i * DEEP + r, r * WIDE + WIDE - depth + i] = 1
        for j in range(depth):
            for k, (r, q) in enumerate(((0, 0), (0, WIDE - depth), (DEEP - depth, 0), (DEEP - depth, WIDE - depth))):
                m[corner + k * depth * depth + i * depth + j, (r + i) * WIDE + q + j] = 1
    return m


CORNERS = {(-1, -1): 3, (-1, 1): 2, (1, -1): 1, (1, 1): 0}


def spread_table():
    m = np.zeros((512, 512), np.float32)
    for r in range(4):
        for w in range(128):
            m[r * 128 + w, (w % 4) * 128 + r * WIDE + w // 4] = 1
    return m


SHIFT = shift_tables(1, EXT)
SHIFT_FAR = shift_tables(2, 512)
PICK, PICK_FAR = pick_table(1), pick_table(2)
SPREAD = spread_table()

UNDER = (((0,), (1, 2)), ((0, 1), (2,)))
OVER = ((2,), (1, 2), (0, 1), (0,))
BASE = (0, 1, 1, 2)


def mm(a, b):
    return jnp.dot(a, b, preferred_element_type=F32)


def nt(a, b):
    return lax.dot_general(a, b, (((1,), (1,)), ((), ())), preferred_element_type=F32)


def logistic(z):
    return 0.5 + 0.5 * jnp.tanh(0.5 * z)


def activated(v):
    stored = v.astype(BF)
    z = stored.astype(F32)
    return stored, (z * logistic(z)).astype(BF)


def sloped(incoming, stored):
    z = stored.astype(F32)
    s = logistic(z)
    return (incoming * (s * (1.0 + z * (1.0 - s)))).astype(BF)


def remote(src, dst, send, recv, target):
    return pltpu.make_async_remote_copy(
        src_ref=src, dst_ref=dst, send_sem=send, recv_sem=recv, device_id=target, device_id_type=MESH
    )


SIDES = ((-1, -1), (-1, 1), (1, -1), (1, 1), (0, -1), (0, 1), (-1, 0), (1, 0))


def net_kernel(counts, *refs):
    it = iter(refs)

    def take(n):
        return [next(it) for _ in range(n)]

    afar = take(15)
    logits_out, features_out, embed_ref, grads_out = take(4)
    xb, e0, z0, z1, f1, e1, z2, f2, e2, z3, e3, z4, e4, z5, f5, t5, t4, t3, t2, t1, fg, cp = take(22)
    w0, w1, w1b, w2, w2b, w3, w3b, w4, w4b, w5, w5b, r4, r4t = take(13)
    halos = [take(2) for _ in WIDTHS]
    near = take(15)
    syn, cU, cot, cQ, eye, embt, rdo, k1, cS, k2t, k3, k5, k4, cQ2, cF = near
    far, wide2, loads, logits_ref, features_ref, stores = take(6)
    sends, recvs = take(2)
    g_ref, whole, tall = take(3)
    stages = [take(6) for _ in PARTS]
    sum_sends, sum_recvs, embed_row, embed_col, embed_sends, embed_recvs = take(6)

    n_row, n_col = counts
    row, col = lax.axis_index("row"), lax.axis_index("col")
    there = {
        (-1, 0): row > 0,
        (1, 0): row < n_row - 1,
        (0, -1): col > 0,
        (0, 1): col < n_col - 1,
    }
    for dr in (-1, 1):
        for dc in (-1, 1):
            there[dr, dc] = jnp.logical_and(there[dr, 0], there[0, dc])

    def place(dr, dc):
        return {"row": (row + dr + n_row) % n_row, "col": (col + dc + n_col) % n_col}

    storing = []

    def store(source, target):
        storing.append(pltpu.make_async_copy(source, target, stores.at[len(storing)]))
        storing[-1].start()

    partners = [(d, 0) for d in range(1, n_row)] + [(0, d) for d in range(1, n_col)] + list(SIDES[:4])
    barrier = pltpu.get_barrier_semaphore()
    for partner in partners:
        pl.semaphore_signal(barrier, inc=1, device_id=place(*partner), device_id_type=MESH)

    loading = {}
    for n, (source, target) in enumerate(zip(afar, near)):
        loading[id(target)] = pltpu.make_async_copy(source, target, loads.at[n])
        loading[id(target)].start()

    def loaded(*targets):
        for target in targets:
            loading[id(target)].wait()

    lane = lax.broadcasted_iota(jnp.int32, (1, 128), 1)
    sixteen = lax.broadcasted_iota(jnp.int32, (16, 1), 0)

    def inside(depth):
        down, left, right, corner = bounds(depth)
        spans = [(0, down, (-1, 0)), (down, left, (1, 0)), (left, left + DEEP * depth, (0, -1)), (right, right + DEEP * depth, (0, 1))]
        spans += [(corner + k * depth * depth, corner + (k + 1) * depth * depth, side) for side, k in CORNERS.items()]
        masks = []
        for tile in range(depth):
            at = lane + tile * 128
            keep = lane < 0
            for low, high, side in spans:
                keep = jnp.logical_or(keep, jnp.logical_and(jnp.logical_and(at >= low, at < high), there[side]))
            masks.append(keep)
        return masks

    near_masks, far_masks = inside(1), inside(2)

    def fenced(v):
        return jnp.concatenate([v[:, :CELLS], jnp.where(near_masks[0], v[:, CELLS:], 0.0)], axis=1)

    def begin(n, depth, pieces, ahead=None):
        out, into = halos[n]
        down, left, right, corner = bounds(depth)
        pick = (cQ if depth == 1 else cQ2)[...]
        start = 0
        for piece in pieces:
            out[:, start : start + piece.shape[0]] = nt(pick, piece).astype(BF)
            start += piece.shape[0]
        size = {(-1, 0): (0, down, down), (1, 0): (down, left, 0), (0, -1): (left, right, right), (0, 1): (right, corner, left)}
        copies = []
        for k, (dr, dc) in enumerate(SIDES):
            if (dr, dc) in size:
                low, high, target = size[dr, dc]
            else:
                low, high = corner, corner + 16
                target = 128 * depth + 16 * CORNERS[-dr, -dc]
            copies.append(
                remote(out.at[low:high], into.at[target : target + high - low], sends.at[n, k], recvs.at[n, k], place(dr, dc))
            )
        if ahead is not None:
            ahead()
        for copy in copies:
            copy.start()
        return copies

    def end(n, depth, copies):
        into = halos[n][1]
        corner = bounds(depth)[3]
        for copy in copies:
            copy.wait()
        ends = 0.0
        for k in range(4):
            tile = into[128 * depth + 16 * k : 128 * depth + 16 * (k + 1), :].astype(F32)
            ends = ends + jnp.where(sixteen // (depth * depth) == k, tile, 0.0)
        into[corner : corner + 16, :] = ends.astype(BF)

    def ring(n, depth, start, width):
        into = halos[n][1]
        tiles = []
        for tile, keep in enumerate(near_masks if depth == 1 else far_masks):
            turned = nt(eye[0:width, 0:width], into[tile * 128 : (tile + 1) * 128, start : start + width])
            tiles.append(jnp.where(keep, turned, 0.0).astype(BF))
        return tiles

    def extend(p, width, ref, size):
        sides = {}
        for ea in range(p + 2):
            for eb in range(p + 2):
                way = (ea > p) - (ea < 1), (eb > p) - (eb < 1)
                if way != (0, 0):
                    source = (((ea - 1) % p + 1) * (p + 2) + (eb - 1) % p + 1) * width
                    sides.setdefault(way, []).append((source, (ea * (p + 2) + eb) * width))
        for (dr, dc), spots in sides.items():
            at = (dr * 3 + dc + 4) * EXT
            many = len(spots) * width
            first, target = spots[0]
            if dc == 0:
                held = ref[first : first + many, :]
            else:
                held = jnp.concatenate([ref[i : i + width, :] for i, _ in spots], axis=0)
            moved = mm(held, cS[at : at + EXT, 0:size]).astype(BF)
            if dc == 0:
                ref[target : target + many, 0:size] = moved
            else:
                for n, (_, target) in enumerate(spots):
                    ref[target : target + width, 0:size] = moved[n * width : (n + 1) * width, :]

    core, n_x = row % 2, n_row // 2
    ways = {
        "row": (row, n_row, lambda d: place(d, 0)),
        "col": (col, n_col, lambda d: place(0, d)),
        "x": (row // 2, n_x, lambda d: {"row": (row // 2 + d) % n_x * 2 + core}),
    }
    flying = {}

    def sum_step(part, step):
        start, size, paired, first, second = PARTS[part]
        s0, r0, held, s1, r1, r2 = stages[part]
        me1, n1, to1 = ways[first]
        me2, n2, to2 = ways[second]
        for copy in flying.pop(part, ()):
            copy.wait()
        if step == 5:
            store(whole.at[start : start + size], grads_out.at[start : start + size])
            return
        half = size // 2 if paired else size
        base = start + core * half if paired else start
        c1 = half // n1
        own = pl.ds(pl.multiple_of(base + me1 * c1, 16), c1)
        partner = {"row": row + 1 - 2 * core}
        moves = []
        if step == 0:
            s0[...] = g_ref[pl.ds(pl.multiple_of(start + (1 - core) * half, 16), half), :].astype(BF)
            moves.append((s0, r0, partner))
        elif step == 1:
            total = g_ref[pl.ds(pl.multiple_of(base, 16), half), :] if paired else g_ref[base : base + half, :]
            if paired:
                total = total + r0[...].astype(F32)
            held[...] = total
            s1[...] = total.astype(BF)
            moves = [(ranged(s1, (me1 + d) % n1 * c1, c1), r1.at[d - 1], to1(d)) for d in range(1, n1)]
        elif step == 2:
            total = held[pl.ds(pl.multiple_of(me1 * c1, 16), c1), :]
            for d in range(n1 - 1):
                total = total + r1[d].astype(F32)
            r2[me2] = total.astype(BF)
            moves = [(r2.at[me2], r2.at[me2], to2(d)) for d in range(1, n2)]
        elif step == 3:
            whole[own, :] = sum(r2[d].astype(F32) for d in range(n2)).astype(BF)
            moves = [(whole.at[own, :], whole.at[own, :], to1(d)) for d in range(1, n1)]
        elif paired:
            mine = ranged(whole, base, half)
            moves.append((mine, mine, partner))
        copies = [
            remote(src, dst, sum_sends.at[part, step, k], sum_recvs.at[part, step, k], to) for k, (src, dst, to) in enumerate(moves)
        ]
        for copy in copies:
            copy.start()
        flying[part] = copies

    def embed_step(step, value=None):
        if step > 0:
            for copy in flying.pop("embed"):
                copy.wait()
            slots = embed_row if step == 1 else embed_col
            value = sum(slots[d] for d in range(slots.shape[0]))
        if step == 2:
            return value
        slots, (me, count, to) = (embed_row, ways["row"]) if step == 0 else (embed_col, ways["col"])
        slots[me] = value
        copies = [
            remote(slots.at[me], slots.at[me], embed_sends.at[step, d], embed_recvs.at[step, d], to(d)) for d in range(1, count)
        ]
        for copy in copies:
            copy.start()
        flying["embed"] = copies

    loaded(syn, cU)
    bit = lax.broadcasted_iota(jnp.int32, (16, 1), 0)
    groups = []
    for a in range(4):
        for t in range(2):
            line = [(syn[16 * t + 4 * r + a : 16 * t + 4 * r + a + 1, :] >> bit) & 1 for r in range(4)]
            groups.append(jnp.concatenate(line, axis=1))
    bits = jnp.concatenate(groups, axis=0).astype(F32).astype(BF)
    phased = mm(bits, cU[...]).astype(BF)
    for a in range(4):
        for t in range(2):
            for b in range(4):
                start = ((a + 1) * 6 + b + 1) * 16
                xb[start : start + 16, t * 128 : (t + 1) * 128] = phased[(a * 2 + t) * 16 : (a * 2 + t + 1) * 16, b * 128 : (b + 1) * 128]
    loaded(cot)
    wide = cot[...].astype(F32)
    groups = []
    for a in range(4):
        for t in range(2):
            line = jnp.concatenate([wide[:, 16 * t + 4 * r + a, :] for r in range(4)], axis=1)
            groups.append(jnp.concatenate([line, jnp.zeros((6, 512), F32)], axis=0))
    phased = mm(jnp.concatenate(groups, axis=0).astype(BF), cU[...])
    for a in range(4):
        for t in range(2):
            start = (a * 2 + t) * 8
            pieces = [phased[start : start + 4, b * 128 : (b + 1) * 128] for b in range(4)]
            cp[a * 16 : (a + 1) * 16, t * 128 : (t + 1) * 128] = jnp.concatenate(pieces, axis=0).astype(BF)

    loaded(cQ)
    inner = [((a + 1) * 6 + 1) * 16 for a in range(4)]
    pieces = [jnp.concatenate([xb[i : i + 64, 0:CELLS] for i in inner], axis=0), cp[:, 0:CELLS]]
    copies = begin(0, 1, pieces, lambda: pl.semaphore_wait(barrier, len(partners)))

    def beside(blocks, i, blank):
        return jnp.concatenate(blocks + [blank] if i == 0 else [blank] + blocks, axis=0)

    def added(k, rows, cols):
        return sum(k[ta, tb].astype(F32) for ta in rows for tb in cols).astype(BF)

    def arrange_first():
        repeat = (lax.broadcasted_iota(jnp.int32, (16, 96), 1) % 16 == lax.broadcasted_iota(jnp.int32, (16, 96), 0)).astype(F32).astype(BF)
        tiled = mm(nt(eye[:64, :64], embt[...]).astype(BF), repeat)
        own = lax.broadcasted_iota(jnp.int32, (64, 96), 1) // 16
        for j in range(6):
            w0[j * 64 : (j + 1) * 64, :] = jnp.where(own == j, tiled, 0.0).astype(BF)
        for ta in range(3):
            for i in range(2):
                w1[i * 64 : (i + 1) * 64, ta * 256 : (ta + 1) * 256] = sum(
                    mm(k1[ta, tb], eye[(tb + i) * 64 : (tb + i + 1) * 64, :]) for tb in range(3)
                ).astype(BF)

    def arrange_second():
        blank, empty = jnp.zeros((64, 128), BF), jnp.zeros((64, 64), BF)
        for ta in range(3):
            for i in range(2):
                line = beside([k2t[ta, tb] for tb in range(3)], i, blank)
                w2[i * 128 : (i + 1) * 128, ta * 256 : (ta + 1) * 256] = nt(eye[:128, :128], line).astype(BF)
                for tb in range(3):
                    w2b[i * 64 : (i + 1) * 64, ta * 512 + (tb + i) * 128 : ta * 512 + (tb + i + 1) * 128] = k2t[2 - ta, 2 - tb]
                hole = ta * 512 + (384 if i == 0 else 0)
                w2b[i * 64 : (i + 1) * 64, hole : hole + 128] = blank
                line = beside([k1[2 - ta, 2 - tb] for tb in range(3)], i, empty)
                w1b[i * 64 : (i + 1) * 64, ta * 256 : (ta + 1) * 256] = nt(eye[:64, :64], line).astype(BF)

    def arrange_bottom():
        for t in range(9):
            w3[:, t * 128 : (t + 1) * 128] = k3[t // 3, t % 3]
            w3b[:, t * 256 : (t + 1) * 256] = nt(eye[:128, :128], k3[2 - t // 3, 2 - t % 3]).astype(BF)

    def arrange_return():
        for pa in range(2):
            for pb in range(2):
                for s in range(2):
                    for u in range(2):
                        block = added(k4, UNDER[pa][s], UNDER[pb][u])
                        w4[(pa * 2 + pb) * 128 : (pa * 2 + pb + 1) * 128, (s * 2 + u) * 256 : (s * 2 + u + 1) * 256] = block
                        at = OVER.index(UNDER[pa][s]) * 4 + OVER.index(UNDER[pb][u])
                        w4b[:, at * 128 : (at + 1) * 128] = nt(eye[...], block).astype(BF)

    def arrange_final():
        for pa in range(2):
            for pb in range(2):
                for s in range(2):
                    for u in range(2):
                        start = pa * 128 + (1 - pb) * 64
                        w5[start : start + 64, (s * 2 + u) * 128 : (s * 2 + u + 1) * 128] = added(k5, UNDER[pa][s], UNDER[pb][u])
        for ea in range(4):
            for pair in range(2):
                stack = jnp.concatenate([added(k5, OVER[ea], OVER[2 * pair + i]) for i in range(2)], axis=0)
                at = ea * 2 + pair
                w5b[:, at * 128 : (at + 1) * 128] = nt(eye[:128, :128], stack).astype(BF)

    def arrange_readout():
        repeat = (lax.broadcasted_iota(jnp.int32, (64, 256), 1) % 64 == lax.broadcasted_iota(jnp.int32, (64, 256), 0)).astype(F32).astype(BF)
        tiled = mm(rdo[...], repeat)
        tiled = jnp.concatenate([tiled, jnp.zeros((2, 256), F32)] * 4, axis=0)
        own = lax.broadcasted_iota(jnp.int32, (16, 256), 1) // 64 == lax.broadcasted_iota(jnp.int32, (16, 256), 0) // 4
        r4[...] = jnp.where(own, tiled, 0.0).astype(BF)
        r4t[...] = nt(eye[...], r4[...]).astype(BF)

    loaded(eye, embt, rdo, k1)
    arrange_first()
    arrange_readout()
    loaded(k2t)
    arrange_second()
    loaded(cS)
    end(0, 1, copies)
    (tile,) = ring(0, 1, 0, 256)
    for a in range(4):
        xb[inner[a] : inner[a] + 64, CELLS:EXT] = tile[a * 64 : (a + 1) * 64, :]
    cp[:, CELLS:EXT] = ring(0, 1, 256, 64)[0]
    extend(4, 16, xb, EXT)

    for ea in range(6):
        stored, active = activated(mm(w0[...], xb[ea * 96 : (ea + 1) * 96, :]))
        e0[ea * 384 : (ea + 1) * 384, :] = active
        if 1 <= ea <= 4:
            z0[(ea - 1) * 256 : ea * 256, :] = stored[64:320, 0:CELLS]

    for a in range(4):
        for pair in range(2):
            v = sum(
                mm(w1[:, ta * 256 : (ta + 1) * 256], e0[((a + ta) * 6 + 2 * pair) * 64 : ((a + ta) * 6 + 2 * pair + 4) * 64, :])
                for ta in range(3)
            )
            start = (a * 4 + 2 * pair) * 64
            z1[start : start + 128, :], f1[start : start + 128, :] = activated(fenced(v))

    def pooled(ref, side, width, a, b, size):
        spots = [((2 * a + i) * side + 2 * b + j) * width for i in range(2) for j in range(2)]
        return (sum(ref[s : s + width, 0:size].astype(F32) for s in spots) * 0.25).astype(BF)

    for a in range(2):
        for b in range(2):
            start = ((a + 1) * 4 + b + 1) * 64
            e1[start : start + 64, :] = pooled(f1, 4, 64, a, b, EXT)
    extend(2, 64, e1, CELLS)

    for a in range(2):
        v = sum(mm(w2[:, ta * 256 : (ta + 1) * 256], e1[(a + ta) * 256 : (a + ta + 1) * 256, 0:CELLS]) for ta in range(3))
        z2[a * 256 : (a + 1) * 256, 0:CELLS], f2[a * 256 : (a + 1) * 256, 0:CELLS] = activated(v)
    e2[4 * 128 : 5 * 128, 0:CELLS] = pooled(f2, 2, 128, 0, 0, CELLS)
    loaded(cQ2)
    copies = begin(1, 2, [e2[4 * 128 : 5 * 128, 0:CELLS]])
    later = begin(2, 1, [z2[0:256, 0:CELLS], z2[256:512, 0:CELLS]])
    loaded(k3, k5)
    arrange_bottom()
    arrange_final()
    loaded(k4)
    arrange_return()
    loaded(cF)
    end(1, 2, copies)
    wide2[:, 0:CELLS] = e2[4 * 128 : 5 * 128, 0:CELLS]
    wide2[:, 256:384], wide2[:, 384:512] = ring(1, 2, 0, 128)
    for n in range(9):
        e2[n * 128 : (n + 1) * 128, :] = mm(wide2[...], cF[n * 512 : (n + 1) * 512, :]).astype(BF)

    stored, e3[4 * 256 : 5 * 256, :] = activated(fenced(mm(w3[...], e2[...])))
    z3[...] = stored[:, 0:CELLS]
    end(2, 1, later)
    for a in range(2):
        z2[a * 256 : (a + 1) * 256, CELLS:EXT] = ring(2, 1, a * 256, 256)[0]
        f2[a * 256 : (a + 1) * 256, CELLS:EXT] = activated(z2[a * 256 : (a + 1) * 256, CELLS:EXT])[1]
    extend(1, 256, e3, EXT)

    for a in range(2):
        for b in range(2):
            n = a * 2 + b
            v = sum(
                mm(w4[n * 128 : (n + 1) * 128, s * 512 : (s + 1) * 512], e3[((a + s) * 3 + b) * 256 : ((a + s) * 3 + b + 2) * 256, :])
                for s in range(2)
            )
            v = v + f2[n * 128 : (n + 1) * 128, :].astype(F32)
            start = ((a + 1) * 4 + b + 1) * 128
            z4[n * 128 : (n + 1) * 128, :], e4[start : start + 128, :] = activated(fenced(v))
    extend(2, 128, e4, EXT)

    RUNS = ((0, 1, 64, 64), (1, 2, 0, 128), (3, 1, 0, 64))
    for a in range(4):
        for b, many, first, size in RUNS:
            base = (a % 2) * 128 + first
            v = sum(
                mm(w5[base : base + size, s * 256 : (s + 1) * 256], e4[((BASE[a] + s) * 4 + BASE[b]) * 128 : ((BASE[a] + s) * 4 + BASE[b] + 2) * 128, :])
                for s in range(2)
            )
            start = (a * 4 + b) * 64
            v = v + f1[start : start + size, :].astype(F32)
            z5[start : start + size, :] = v.astype(BF)

    for a in range(4):
        back = mm(r4t[...], cp[a * 16 : (a + 1) * 16, :])
        start = ((a + 1) * 6 + 1) * 64
        t5[start : start + 256, :] = sloped(back, z5[a * 256 : (a + 1) * 256, :])
    extend(4, 64, t5, CELLS)
    for a in range(2):
        for b in range(2):
            v = sum(
                mm(w5b[:, m * 256 : (m + 1) * 256], t5[((2 * a + m) * 6 + 2 * b) * 64 : ((2 * a + m) * 6 + 2 * b + 4) * 64, 0:CELLS])
                for m in range(4)
            )
            start = ((a + 1) * 4 + b + 1) * 128
            n = a * 2 + b
            t4[start : start + 128, 0:CELLS] = sloped(v, z4[n * 128 : (n + 1) * 128, 0:CELLS])
    copies = begin(3, 1, [t4[((a + 1) * 4 + 1) * 128 : ((a + 1) * 4 + 3) * 128, 0:CELLS] for a in range(2)])

    sums = {}
    for a in range(4):
        for s in range(2):
            for b, many, first, size in RUNS:
                start = ((BASE[a] + s) * 4 + BASE[b]) * 128
                t_start = ((a + 1) * 6 + b + 1) * 64
                product = nt(t5[t_start : t_start + size, 0:CELLS], e4[start : start + 256, 0:CELLS])
                for m in range(many):
                    key = (a % 2, s, (b + m) % 2)
                    block = product[m * 64 : (m + 1) * 64, :]
                    sums[key] = sums[key] + block if key in sums else block

    def reads(parity, tap):
        return 0 if tap in UNDER[parity][0] else 1

    for ta in range(3):
        rowed = [sums[0, reads(0, ta), pb] + sums[1, reads(1, ta), pb] for pb in range(2)]
        for tb in range(3):
            value = sum(rowed[pb][:, reads(pb, tb) * 128 : (reads(pb, tb) + 1) * 128] for pb in range(2))
            start = AT_FINAL + (ta * 3 + tb) * 64
            g_ref[start : start + 64, :] = value

    for b in range(2):
        for u in range(2):
            parts = {}
            for a in range(2):
                for s in range(2):
                    start = ((a + 1) * 4 + b + 1) * 128
                    from_ = ((a + s) * 3 + b + u) * 256
                    parts[a, s] = nt(t4[start : start + 128, 0:CELLS], e3[from_ : from_ + 256, 0:CELLS])
            for ta in range(3):
                value = parts[0, reads(0, ta)] + parts[1, reads(1, ta)]
                for tb in UNDER[b][u]:
                    for half in range(2):
                        start = AT_RETURN + ((ta * 3 + tb) * 2 + half) * 128
                        piece = value[:, half * 128 : (half + 1) * 128]
                        g_ref[start : start + 128, :] = piece if b == 0 else g_ref[start : start + 128, :] + piece

    g_ref[AT_FINAL + 576 : AT_BOTTOM, :] = jnp.zeros((AT_BOTTOM - AT_FINAL - 576, 128), F32)
    sum_step(0, 0)
    sum_step(1, 0)
    total = jnp.zeros((16, 256), F32)
    for a in range(4):
        f5[a * 256 : (a + 1) * 256, :] = activated(z5[a * 256 : (a + 1) * 256, 0:CELLS])[1]
        total = total + nt(cp[a * 16 : (a + 1) * 16, 0:CELLS], f5[a * 256 : (a + 1) * 256, :])
    total = sum(total[b * 4 : (b + 1) * 4, b * 64 : (b + 1) * 64] for b in range(4))
    g_ref[AT_READ:ROWS, :] = jnp.zeros((ROWS - AT_READ, 128), F32)
    g_ref[AT_READ : AT_READ + 4, 0:64] = total

    sum_step(0, 1)
    sum_step(1, 1)
    end(3, 1, copies)
    for a in range(2):
        start = ((a + 1) * 4 + 1) * 128
        t4[start : start + 256, CELLS:EXT] = ring(3, 1, a * 256, 256)[0]
    extend(2, 128, t4, CELLS)
    v = sum(mm(w4b[:, m * 512 : (m + 1) * 512], t4[m * 512 : (m + 1) * 512, 0:CELLS]) for m in range(4))
    far[:, 0:CELLS] = sloped(v, z3[...])
    copies = begin(4, 2, [far[:, 0:CELLS]])
    for t in range(9):
        g_ref[AT_BOTTOM + t * 256 : AT_BOTTOM + (t + 1) * 256, :] = nt(far[:, 0:CELLS], e2[t * 128 : (t + 1) * 128, 0:CELLS])
    sum_step(2, 0)
    sum_step(3, 0)
    groups = []
    for a in range(4):
        here = f5[a * 256 : (a + 1) * 256, :]
        value = mm(r4[...], here)
        for t in range(2):
            groups.append(jnp.concatenate([value[b * 4 : (b + 1) * 4, t * 128 : (t + 1) * 128] for b in range(4)], axis=1))
    value = jnp.concatenate(groups, axis=0)
    laid = 0.0
    for _ in range(3):
        piece = value.astype(BF)
        laid = laid + nt(piece, cU[...])
        value = value - piece.astype(F32)
    for a in range(4):
        for t in range(2):
            for r in range(4):
                h = 16 * t + 4 * r + a
                logits_ref[:, h : h + 1, :] = laid[(a * 2 + t) * 4 : (a * 2 + t) * 4 + 2, r * 128 : (r + 1) * 128].reshape(2, 1, 128)
    store(logits_ref, logits_out)
    sum_step(2, 1)
    sum_step(3, 1)
    end(4, 2, copies)
    far[:, 256:384], far[:, 384:512] = ring(4, 2, 0, 256)
    for n in range(9):
        t3[n * 256 : (n + 1) * 256, :] = mm(far[...], cF[n * 512 : (n + 1) * 512, :]).astype(BF)

    sum_step(0, 2)
    sum_step(1, 2)
    through = mm(w3b[...], t3[...]) * 0.25
    for a in range(2):
        for b in range(2):
            n = a * 2 + b
            start = ((a + 1) * 4 + b + 1) * 128
            v = fenced(t4[start : start + 128, :].astype(F32) + through)
            t2[start : start + 128, :] = sloped(v, z2[n * 128 : (n + 1) * 128, :])
    for ta in range(3):
        product = 0.0
        for a in range(2):
            start = ((a + 1) * 4 + 1) * 128
            product = product + nt(e1[(a + ta) * 256 : (a + ta + 1) * 256, 0:CELLS], t2[start : start + 256, 0:CELLS])
        g_ref[AT_SECOND + ta * 192 : AT_SECOND + (ta + 1) * 192, :] = product[0:192, 0:128] + product[64:256, 128:256]
    g_ref[AT_SECOND + 576 : AT_FIRST, :] = jnp.zeros((AT_FIRST - AT_SECOND - 576, 128), F32)
    sum_step(4, 1)
    extend(2, 128, t2, EXT)

    for a in range(2):
        v = sum(mm(w2b[:, ta * 512 : (ta + 1) * 512], t2[(a + ta) * 512 : (a + ta + 1) * 512, :]) for ta in range(3)) * 0.25
        for b in range(2):
            for i in range(2):
                for j in range(2):
                    fa, fb = 2 * a + i, 2 * b + j
                    start = ((fa + 1) * 6 + fb + 1) * 64
                    n = (fa * 4 + fb) * 64
                    t1[start : start + 64, :] = sloped(fenced(t5[start : start + 64, :].astype(F32) + v[b * 64 : (b + 1) * 64, :]), z1[n : n + 64, :])
    for ta in range(3):
        product = 0.0
        for a in range(4):
            for pair in range(2):
                start = ((a + 1) * 6 + 2 * pair + 1) * 64
                from_ = ((a + ta) * 6 + 2 * pair) * 64
                product = product + nt(t1[start : start + 128, 0:CELLS], e0[from_ : from_ + 256, 0:CELLS])
        value = product[0:64, 0:192] + product[64:128, 64:256]
        g_ref[AT_FIRST + ta * 64 : AT_FIRST + (ta + 1) * 64, :] = value[:, 0:128]
        start = AT_FIRST + (192 if ta < 2 else 256)
        g_ref[start : start + 64, ta % 2 * 64 : ta % 2 * 64 + 64] = value[:, 128:192]
    g_ref[AT_FIRST + 256 : AT_FIRST + 320, 64:128] = jnp.zeros((64, 64), F32)
    sum_step(5, 1)
    sum_step(2, 2)
    sum_step(3, 2)
    sum_step(0, 3)
    sum_step(1, 3)
    extend(4, 64, t1, CELLS)

    total = jnp.zeros((64, 256), F32)
    for a in range(4):
        for pair in range(2):
            v = sum(
                mm(w1b[:, ta * 256 : (ta + 1) * 256], t1[((a + ta) * 6 + 2 * pair) * 64 : ((a + ta) * 6 + 2 * pair + 4) * 64, 0:CELLS])
                for ta in range(3)
            )
            start = (a * 4 + 2 * pair) * 64
            fg[start : start + 128, :] = sloped(v, z0[start : start + 128, :])
        start = ((a + 1) * 6 + 1) * 16
        total = total + nt(xb[start : start + 64, 0:CELLS], fg[a * 256 : (a + 1) * 256, :])
    total = sum(total[b * 16 : (b + 1) * 16, b * 64 : (b + 1) * 64] for b in range(4))
    embed_step(0, total)

    def lay(a):
        for t in range(2):
            line = jnp.concatenate([fg[(a * 4 + b) * 64 : (a * 4 + b + 1) * 64, t * 128 : (t + 1) * 128] for b in range(4)], axis=1)
            laid = nt(line, cU[...])
            for r in range(4):
                tall[:, 16 * t + 4 * r + a, :] = laid[:, r * 128 : (r + 1) * 128]

    sum_step(4, 2)
    lay(0)
    lay(1)
    sum_step(2, 3)
    sum_step(3, 3)
    sum_step(5, 2)
    lay(2)
    lay(3)
    sum_step(0, 4)
    sum_step(1, 4)
    embed_step(1)
    features_ref[...] = tall[...].astype(BF)
    store(features_ref, features_out)
    sum_step(4, 3)
    sum_step(2, 4)
    sum_step(3, 4)
    sum_step(5, 3)
    embed_ref[...] = embed_step(2)
    for part in (0, 1, 4, 2, 3, 5):
        sum_step(part, 5)
    for copy in storing:
        copy.wait()


WIDTHS = ((384, 1), (128, 2), (512, 1), (512, 1), (256, 2))


def run_net(counts, *args):
    syn, emb, k1, k2, *rest = args
    k3, k4, k5, rdo, cot = rest
    eye, pick, pick_far, spread, near, far = [jnp.asarray(t, BF) for t in (np.eye(CELLS), PICK, PICK_FAR, SPREAD, SHIFT, SHIFT_FAR)]
    afar = (syn, spread, cot, pick, eye, emb.T, rdo, k1, near, k2.transpose(0, 1, 3, 2), k3, k5, k4, pick_far, far)
    wide, own = (EXT,), (CELLS,)
    blocks = [(16 * 36,) + wide, (64 * 36,) + wide, (1024,) + own, (1024,) + wide, (1024,) + wide, (1024,) + wide]
    blocks += [(512,) + wide, (512,) + wide, (128 * 9,) + wide, (256,) + own, (256 * 9,) + wide, (512,) + wide, (128 * 16,) + wide]
    blocks += [(1024,) + wide, (1024,) + own, (64 * 36,) + wide, (128 * 16,) + wide, (256 * 9,) + wide, (128 * 16,) + wide]
    blocks += [(64 * 36,) + wide, (1024,) + own, (64,) + wide]
    weights = [(384, 96), (128, 768), (128, 768), (256, 768), (128, 1536), (256, 1152), (128, 2304), (512, 1024), (256, 2048), (256, 512), (128, 1024), (16, 256), (256, 16)]
    scratch = [pltpu.VMEM(s, BF) for s in blocks + weights]
    for width, depth in WIDTHS:
        scratch += [pltpu.VMEM((bounds(depth)[3] + 16, width), BF), pltpu.VMEM((128 * depth + 64, width), BF)]
    scratch += [pltpu.VMEM(x.shape, x.dtype) for x in afar]
    scratch += [pltpu.VMEM((256, 512), BF), pltpu.VMEM((128, 512), BF), pltpu.SemaphoreType.DMA((15,)), pltpu.VMEM((2, 32, 128), F32), pltpu.VMEM((64, 32, 128), BF)]
    scratch += [pltpu.SemaphoreType.DMA((2 + len(PARTS),))]
    scratch += [pltpu.SemaphoreType.DMA((len(WIDTHS), 8)), pltpu.SemaphoreType.DMA((len(WIDTHS), 8))]
    scratch += [pltpu.VMEM((ROWS, 128), F32), pltpu.VMEM((ROWS, 128), BF), pltpu.VMEM((64, 32, 128), F32)]
    n_row, n_col = counts
    most = max(n_row, n_col)
    along = {"row": n_row, "col": n_col, "x": n_row // 2}
    for _, size, paired, first, second in PARTS:
        half = size // 2 if paired else size
        n1, n2 = along[first], along[second]
        c1, pair = half // n1, half if paired else 16
        scratch += [
            pltpu.VMEM((pair, 128), BF),
            pltpu.VMEM((pair, 128), BF),
            pltpu.VMEM((half, 128), F32),
            pltpu.VMEM((half, 128), BF),
            pltpu.VMEM((n1 - 1, c1, 128), BF),
            pltpu.VMEM((n2, c1, 128), BF),
        ]
    scratch += [pltpu.SemaphoreType.DMA((len(PARTS), 5, most)), pltpu.SemaphoreType.DMA((len(PARTS), 5, most))]
    scratch += [pltpu.VMEM((n_row, 16, 64), F32), pltpu.VMEM((n_col, 16, 64), F32)]
    scratch += [pltpu.SemaphoreType.DMA((2, most)), pltpu.SemaphoreType.DMA((2, most))]
    vmem, hbm = pl.BlockSpec(memory_space=pltpu.VMEM), pl.BlockSpec(memory_space=pl.ANY)
    return pl.pallas_call(
        functools.partial(net_kernel, counts),
        out_shape=(
            jax.ShapeDtypeStruct((2, 32, 128), F32),
            jax.ShapeDtypeStruct((64, 32, 128), BF),
            jax.ShapeDtypeStruct((16, 64), F32),
            jax.ShapeDtypeStruct((ROWS, 128), BF),
        ),
        in_specs=[hbm] * 15,
        out_specs=(hbm, hbm, vmem, hbm),
        scratch_shapes=scratch,
        compiler_params=pltpu.CompilerParams(collective_id=1, has_side_effects=True, vmem_limit_bytes=56 * 2**20),
    )(*afar)


def out_kernel(logits, features, embed, grads, *refs):
    outs, (g, passed, mids, loads, stores) = refs[:9], (refs[9], refs[10:13], refs[13:19], refs[19], refs[20])
    pulls, pushes = [], []

    def pull(source, target):
        pulls.append(pltpu.make_async_copy(source, target, loads.at[len(pulls)]))
        pulls[-1].start()
        return pulls[-1]

    def push(source, target):
        pushes.append(pltpu.make_async_copy(source, target, stores.at[len(pushes)]))
        pushes[-1].start()

    m_first, m_second, m_bottom, m_return, m_final, m_read = mids
    o_first, o_second, o_bottom, o_return, o_final, o_read = outs[3:]
    by_return = [pull(grads.at[n * 768 : (n + 1) * 768], g.at[n * 768 : (n + 1) * 768]) for n in range(3)]
    spots = [AT_BOTTOM + n * 768 for n in range(3)]
    by_bottom = [pull(grads.at[i : i + 768], g.at[i : i + 768]) for i in spots]
    through = [pull(features.at[n * 16 : (n + 1) * 16], passed[1].at[n * 16 : (n + 1) * 16]) for n in range(4)]
    tail = [pull(grads.at[AT_FINAL:AT_BOTTOM], g.at[AT_FINAL:AT_BOTTOM]), pull(grads.at[AT_SECOND:ROWS], g.at[AT_SECOND:ROWS])]
    small = [pull(logits, passed[0]), pull(embed, passed[2])]
    for ta in range(3):
        by_return[ta].wait()
        for tb in range(3):
            for half in range(2):
                start = AT_RETURN + ((ta * 3 + tb) * 2 + half) * 128
                m_return[ta, tb, :, half * 128 : (half + 1) * 128] = g[start : start + 128, :].astype(F32)
        push(m_return.at[ta], o_return.at[ta])
    for ta in range(3):
        by_bottom[ta].wait()
        for tb in range(3):
            start = AT_BOTTOM + (ta * 3 + tb) * 256
            m_bottom[ta, tb] = g[start : start + 256, :].astype(F32)
        push(m_bottom.at[ta], o_bottom.at[ta])
    for n in range(4):
        through[n].wait()
        push(passed[1].at[n * 16 : (n + 1) * 16], outs[1].at[n * 16 : (n + 1) * 16])
    for copy in tail:
        copy.wait()
    for t in range(9):
        ta, tb = t // 3, t % 3
        m_final[ta, tb] = g[AT_FINAL + t * 64 : AT_FINAL + (t + 1) * 64, :].astype(F32)
        m_second[ta, tb] = g[AT_SECOND + t * 64 : AT_SECOND + (t + 1) * 64, :].astype(F32)
        start, low = (AT_FIRST + ta * 64, tb * 64) if tb < 2 else (AT_FIRST + (192 if ta < 2 else 256), ta % 2 * 64)
        m_first[ta, tb] = g[start : start + 64, low : low + 64].astype(F32)
    m_read[...] = g[AT_READ : AT_READ + 16, 0:64].astype(F32)[0:2]
    for copy in small:
        copy.wait()
    for source, target in ((m_final, o_final), (m_second, o_second), (m_first, o_first), (m_read, o_read), (passed[0], outs[0]), (passed[2], outs[2])):
        push(source, target)
    for copy in pushes:
        copy.wait()


def write_out(logits, features, embed, g):
    shapes = [(2, 32, 128), (64, 32, 128), (16, 64), (3, 3, 64, 64), (3, 3, 64, 128), (3, 3, 256, 128), (3, 3, 128, 256), (3, 3, 64, 128), (2, 64)]
    hbm = pl.BlockSpec(memory_space=pl.ANY)
    outs = pl.pallas_call(
        out_kernel,
        out_shape=tuple(jax.ShapeDtypeStruct(s, BF if n == 1 else F32) for n, s in enumerate(shapes)),
        in_specs=[hbm] * 4,
        out_specs=(hbm,) * 9,
        scratch_shapes=[pltpu.VMEM((ROWS, 128), BF)]
        + [pltpu.VMEM(s, BF if n == 1 else F32) for n, s in enumerate(shapes)]
        + [pltpu.SemaphoreType.DMA((14,)), pltpu.SemaphoreType.DMA((16,))],
        compiler_params=pltpu.CompilerParams(vmem_limit_bytes=60 * 2**20),
    )(logits, features, embed, g)
    outs = list(outs)
    outs[2] = outs[2].T
    outs[4] = outs[4].transpose(0, 1, 3, 2)
    return tuple(outs)


def on_device(counts, *args):
    return write_out(*run_net(counts, *args))


def solution(mesh):
    counts = (mesh.shape["row"], mesh.shape["col"])
    cells = P(None, ("batch", "row"), "col")
    in_specs = (P(("batch", "row"), "col"),) + (P(),) * 7 + (cells,)
    out_specs = (cells, cells, P("batch", None)) + (P("batch", None, None, None),) * 5 + (P("batch", None),)
    return jax.shard_map(
        functools.partial(on_device, counts), mesh=mesh, in_specs=in_specs, out_specs=out_specs, check_vma=False
    )
```
